512 devices in a mesh: dom: 32 (over y_hi, z), kb: 16 (over y_lo, x, core).
Axes of the slice: x: 4, y: 4 (y_hi: 2, y_lo: 2; y = y_hi * 2 + y_lo), z: 16, core: 2. Of those that a mesh axis runs over, the one named last changes fastest.
Arguments:
- features: bfloat16 [64, 65536], P(None, ('dom', 'kb')), may hold values from -6 to 6
- vectors: bfloat16 [3, 64, 65536], P(None, None, ('dom', 'kb')), may hold values from -6 to 6
- positions: float32 [3, 65536], P(None, ('dom', 'kb')), may hold values from 0 to 1, as said below
- neighbours: int32 [16, 65536], P(None, ('dom', 'kb')), may hold values from 0 to 384, as said below
- halo_lists: int32 [2, 65536], P(None, ('dom', 'kb')), may hold values from 0 to 127, as said below
- lattice: int32 [3, 8192], replicated, may hold values from -1024 to 1024, as said below
- kspace_filter: float32 [64, 8192], P(None, 'kb'), may hold values from -6 to 6
- node_weight: bfloat16 [64, 64], replicated, may hold values from -0.75 to 0.75
- node_bias: float32 [64], replicated, may hold values from -4 to 4
- message_weight: bfloat16 [64, 192], replicated, may hold values from -0.75 to 0.75
- radial_weight: bfloat16 [20, 192], replicated, may hold values from -3 to 3
- ewald_weight: bfloat16 [64, 64], replicated, may hold values from -0.75 to 0.75
Outputs:
- new_features: bfloat16 [64, 65536], P(None, ('dom', 'kb'))
- new_vectors: bfloat16 [3, 64, 65536], P(None, None, ('dom', 'kb'))
The draws below stay inside these ranges and needn't reach their ends.
Inputs may be any that keep to these rules, and one draw needn't show every extreme that they name: `neighbours`: entry j of column a names atom a's neighbour in the numbering of E = 385 columns: own atoms, then the atoms received from the device below, then those from the device above; 384 marks an empty slot. Empty slots come last in a column, and each atom has 8 or more filled slots. `halo_lists`: for each device, 128 different local atom numbers in each row. `positions`: atom a's third coordinate times 32 * 16 lies between a // 128 and the next integer. `lattice`: rows 0 and 1 lie between -16 and 16.
All inputs are finite; a program needn't handle non-finite values.
Results may differ from the reference program's by a relative error of at most 0.01.
Values may be sent and summed in bfloat16 or wider, within the bound.
No kernel may reach another device: no remote copies, remote signals or barrier semaphores. Data moves between devices by JAX's collectives and lax.ppermute only.
A program may use at most 64 MiB of HBM per device.

```python
import math
import jax
import jax.numpy as jnp
from jax import lax

F = 64
NRBF = 20
NBR = 16
HALO = 128
ATOM_DEV = 128
ATOMS = 65536
KVEC = 8192
N_DOM = 32
N_KB = 16


def draw_positions(key, part):
    slab_count = ATOMS // ATOM_DEV
    across = jax.random.uniform(jax.random.fold_in(key, 11), (2, ATOMS), jnp.float32)
    within = jax.random.uniform(jax.random.fold_in(key, 12), (ATOMS,), jnp.float32)
    slab_number = (jnp.arange(ATOMS) // ATOM_DEV).astype(jnp.float32)
    height = (slab_number + within) / slab_count
    return jnp.concatenate([across, height[None, :]], axis=0)


def draw_neighbours(key, part):
    counts = jax.random.randint(jax.random.fold_in(key, 21), (1, ATOMS), NBR // 2, NBR + 1)
    chosen = jax.random.randint(jax.random.fold_in(key, 22), (NBR, ATOMS), 0, ATOM_DEV + 2 * HALO)
    slot_number = jnp.arange(NBR)[:, None]
    return jnp.where(slot_number < counts, chosen, ATOM_DEV + 2 * HALO).astype(jnp.int32)


def draw_halo_lists(key, part):
    slab_count = ATOMS // ATOM_DEV
    split_keys = jax.random.split(jax.random.fold_in(key, 31), 2 * slab_count)

    def choose(one_key):
        return jax.random.permutation(one_key, ATOM_DEV)[:HALO]
    chosen = jax.vmap(choose)(split_keys)
    return chosen.reshape(2, slab_count * HALO).astype(jnp.int32)


def draw_lattice(key, part):
    across = jax.random.randint(jax.random.fold_in(key, 41), (2, KVEC), -16, 17)
    depth = jax.random.randint(jax.random.fold_in(key, 42), (1, KVEC), -1024, 1025)
    return jnp.concatenate([across, depth], axis=0).astype(jnp.int32)


def levels(own_key, dims, pieces, low, top_value):
    loudness, own = 1.0, jax.random.fold_in(own_key, 6)
    for dim, blocks in pieces:
        steps = jnp.exp(jax.random.uniform(jax.random.fold_in(own, dim), (blocks,), jnp.float32, low / len(pieces), top_value / len(pieces)))
        loudness = loudness * jnp.repeat(steps, dims[dim] // blocks).reshape([-1 if axis == dim else 1 for axis in range(len(dims))])
    return loudness


def noise(own_key, extent, scale, most, shards=(), dtype=jnp.bfloat16):
    level = levels(own_key, extent, shards, -0.22, 0.18) if shards else 1.0
    result = jax.random.normal(own_key, extent, jnp.float32) * scale * level
    return jnp.minimum(jnp.maximum(result, -most), most).astype(dtype)


def setup_inputs(seed: int = 0) -> dict:
    seeds = jax.random.split(jax.random.key(seed), 13)
    features = noise(seeds[0], (F, ATOMS), 1.0, 6.0, ((1, 512),))
    vectors = noise(seeds[1], (3, F, ATOMS), 1.0, 6.0, ((2, 512),))
    positions = draw_positions(jax.random.fold_in(seeds[12], 71), 0)
    neighbours = draw_neighbours(jax.random.fold_in(seeds[12], 71), 0)
    halo_lists = draw_halo_lists(jax.random.fold_in(seeds[12], 71), 0)
    lattice = draw_lattice(jax.random.fold_in(seeds[12], 71), 0)
    kspace_filter = noise(seeds[6], (F, KVEC), 1.0, 6.0, ((1, 16),), jnp.float32)
    node_weight = noise(seeds[7], (F, F), F ** -0.5, 0.75)
    node_bias = noise(seeds[8], (F,), 1.0, 4.0, (), jnp.float32)
    message_weight = noise(seeds[9], (F, 3 * F), F ** -0.5, 0.75)
    radial_weight = noise(seeds[10], (NRBF, 3 * F), 4 ** -0.5, 3.0)
    ewald_weight = noise(seeds[11], (F, F), F ** -0.5, 0.75)
    return {"features": features, "vectors": vectors, "positions": positions, "neighbours": neighbours, "halo_lists": halo_lists, "lattice": lattice, "kspace_filter": kspace_filter, "node_weight": node_weight, "node_bias": node_bias, "message_weight": message_weight, "radial_weight": radial_weight, "ewald_weight": ewald_weight}


full_turn = 2.0 * math.pi
side_length = 6.0
slab_depth = 6.0
radial_reach = 6.0
distance_floor = 1.0

def over_first(first_operand, second_operand):
    return lax.dot_general(first_operand, second_operand, (((0,), (0,)), ((), ())), preferred_element_type=jnp.float32)

def over_last(first_operand, second_operand):
    return lax.dot_general(first_operand, second_operand, (((1,), (1,)), ((), ())), preferred_element_type=jnp.float32)

def phase_tables(coords, lattice_rows):
    phase_angle = (coords[0][:, None] * lattice_rows[0][None, :] + coords[1][:, None] * lattice_rows[1][None, :] + coords[2][:, None] * lattice_rows[2][None, :]) * full_turn
    return (jnp.cos(phase_angle).astype(jnp.bfloat16), jnp.sin(phase_angle).astype(jnp.bfloat16))

def short_range(own_feat, own_vec, own_pos, neighbour_ids, side_feat, side_vec, side_pos, node_weight, node_bias, message_weight, radial_weight, slab_count):
    channels = own_feat.shape[0]
    own_count = own_feat.shape[1]
    slot_count = neighbour_ids.shape[0]
    radial_count = radial_weight.shape[0]
    ext_feat = jnp.concatenate([own_feat, side_feat, jnp.zeros((channels, 1), jnp.bfloat16)], axis=1)
    ext_vec = jnp.concatenate([own_vec, side_vec, jnp.zeros((3, channels, 1), jnp.bfloat16)], axis=2)
    ext_pos = jnp.concatenate([own_pos, side_pos, jnp.zeros((3, 1), jnp.float32)], axis=1)
    empty_slot = ext_feat.shape[1] - 1
    hidden = jax.nn.silu(over_first(node_weight, ext_feat) + node_bias[:, None]).astype(jnp.bfloat16)
    message_in = over_first(message_weight, hidden).astype(jnp.bfloat16)
    flat_ids = neighbour_ids.reshape(-1)
    weights_on = (flat_ids < empty_slot).astype(jnp.float32)
    offsets = jnp.take(ext_pos, flat_ids, axis=1).reshape(3, slot_count, own_count) - own_pos[:, None, :]
    offsets = offsets - jnp.floor(offsets + 0.5)
    box_sides = jnp.array([side_length, side_length, slab_depth * slab_count], jnp.float32)
    cartesian = offsets * box_sides[:, None, None]
    distance = jnp.sqrt(lax.optimization_barrier(jnp.sum(cartesian * cartesian, axis=0)))
    direction = cartesian / jnp.maximum(distance, distance_floor)
    centers = jnp.arange(radial_count).astype(jnp.float32) * (radial_reach / (radial_count - 1))
    spread = 1.5 * radial_reach / radial_count
    radial = jnp.exp(-jnp.square((distance[None] - centers[:, None, None]) / spread)).astype(jnp.bfloat16)
    edge_filter = over_first(radial_weight, radial.reshape(radial_count, -1))
    edge_terms = jnp.take(message_in, flat_ids, axis=1).astype(jnp.float32) * edge_filter * weights_on
    edge_terms = edge_terms.reshape(3 * channels, slot_count, own_count)
    scalar_part = lax.optimization_barrier(jnp.sum(edge_terms[:channels], axis=1))
    neighbour_vec = jnp.take(ext_vec, flat_ids, axis=2).reshape(3, channels, slot_count, own_count).astype(jnp.float32)
    vector_part = lax.optimization_barrier(jnp.sum(neighbour_vec * edge_terms[channels:2 * channels][None] + edge_terms[2 * channels:][None] * direction[:, None], axis=2))
    return (scalar_part, vector_part)

def take_columns(source, chosen):
    return jnp.take(source, chosen, axis=1)

def take_vector_columns(source, chosen):
    return jnp.take(source, chosen, axis=2)

def reference(features, vectors, positions, neighbours, halo_lists, lattice, kspace_filter, node_weight, node_bias, message_weight, radial_weight, ewald_weight):
    slab_count = N_DOM * N_KB
    channels = features.shape[0]
    own_feat = features.reshape(channels, slab_count, ATOM_DEV).transpose(1, 0, 2)
    own_vec = vectors.reshape(3, channels, slab_count, ATOM_DEV).transpose(2, 0, 1, 3)
    own_pos = positions.reshape(3, slab_count, ATOM_DEV).transpose(1, 0, 2)
    own_ids = neighbours.reshape(NBR, slab_count, ATOM_DEV).transpose(1, 0, 2)
    halo_rows = halo_lists.reshape(2, slab_count, HALO)

    def picked(index_rows):
        sent_feat = jax.vmap(take_columns)(own_feat, index_rows)
        sent_vec = jax.vmap(take_vector_columns)(own_vec, index_rows)
        sent_pos = jax.vmap(take_columns)(own_pos, index_rows)
        return (sent_feat, sent_vec, sent_pos)
    up_feat, up_vec, up_pos = picked(halo_rows[0])
    down_feat, down_vec, down_pos = picked(halo_rows[1])
    side_feat = jnp.concatenate([jnp.roll(up_feat, 1, axis=0), jnp.roll(down_feat, -1, axis=0)], axis=2)
    side_vec = jnp.concatenate([jnp.roll(up_vec, 1, axis=0), jnp.roll(down_vec, -1, axis=0)], axis=3)
    side_pos = jnp.concatenate([jnp.roll(up_pos, 1, axis=0), jnp.roll(down_pos, -1, axis=0)], axis=2)

    def per_device(device_group):
        return short_range(device_group[0], device_group[1], device_group[2], device_group[3], device_group[4], device_group[5], device_group[6], node_weight, node_bias, message_weight, radial_weight, slab_count)
    scalar_part, vector_part = lax.map(per_device, (own_feat, own_vec, own_pos, own_ids, side_feat, side_vec, side_pos))
    scalar_all = scalar_part.transpose(1, 0, 2).reshape(channels, -1)
    vector_all = vector_part.transpose(1, 2, 0, 3).reshape(3, channels, -1)
    ewald_in = over_first(ewald_weight, features).astype(jnp.bfloat16)
    lattice_rows = lattice.astype(jnp.float32)
    block_size = 4 * ATOM_DEV
    block_count = ATOMS // block_size
    in_blocks = ewald_in.reshape(channels, block_count, block_size).transpose(1, 0, 2)
    pos_blocks = positions.reshape(3, block_count, block_size).transpose(1, 0, 2)

    def accumulate(totals, device_group):
        cosine_table, sine_table = phase_tables(device_group[1], lattice_rows)
        return ((totals[0] + jnp.dot(device_group[0], cosine_table, preferred_element_type=jnp.float32), totals[1] + jnp.dot(device_group[0], sine_table, preferred_element_type=jnp.float32)), None)
    zero_sums = jnp.zeros((channels, KVEC), jnp.float32)
    totals, ignored = lax.scan(accumulate, (zero_sums, zero_sums), (in_blocks, pos_blocks))
    norm_scale = 1.0 / math.sqrt(KVEC * ATOMS)
    filt_re = (kspace_filter * totals[0] * norm_scale).astype(jnp.bfloat16)
    filt_im = (kspace_filter * totals[1] * norm_scale).astype(jnp.bfloat16)

    def project(coords):
        cosine_table, sine_table = phase_tables(coords, lattice_rows)
        return over_last(filt_re, cosine_table) + over_last(filt_im, sine_table)
    message = lax.map(project, pos_blocks).transpose(1, 0, 2).reshape(channels, -1)
    new_features = (features.astype(jnp.float32) + scalar_all + message).astype(jnp.bfloat16)
    new_vectors = (vectors.astype(jnp.float32) + vector_all).astype(jnp.bfloat16)
    return (new_features, new_vectors)
```

```python
import math

import jax
import jax.numpy as jnp
from jax import lax
from jax.experimental import pallas as pl
from jax.experimental.pallas import tpu as pltpu
from jax.sharding import Mesh
from jax.sharding import PartitionSpec as P

F = 64
NRBF = 20
NBR = 16
ATOM = 128
KDEV = 256
PLANE = 32
DEPTH = 16
SLABS = 512
KVEC = 8192
ATOMS = 65536
PACK = 80
HALO_ROWS = 288
EXT_ROWS = 416

plane_axes = ("yh", "yl", "x", "c")
kb_axes = ("yl", "x", "c")
all_axes = ("yh", "z", "yl", "x", "c")

side_length = 6.0
slab_depth = 6.0
radial_reach = 6.0
distance_floor = 1.0
norm_scale = 1.0 / math.sqrt(KVEC * ATOMS)

sine_terms = (4.44287959, -7.30781805, 3.59778873, -0.79123821)
cosine_terms = (1.41420408, -6.97764206, 5.71523839, -1.72834865)
whole_turns = 1.5 * 2.0**23

VMEM_LIMIT = 40 * 2**20


def dot(a, b, dims):
    return lax.dot_general(a, b, (dims, ((), ())), preferred_element_type=jnp.float32)


def in_three(value):
    first = value.astype(jnp.bfloat16)
    rest = value - first.astype(jnp.float32)
    second = rest.astype(jnp.bfloat16)
    third = (rest - second.astype(jnp.float32)).astype(jnp.bfloat16)
    return first, second, third


def polynomial(terms, u):
    value = terms[-1] * u + terms[-2]
    for term in terms[-3::-1]:
        value = value * u + term
    return value


def cosine_and_sine(turns):
    r = turns - ((turns + whole_turns) - whole_turns)
    u = r * r
    s = r * polynomial(sine_terms, u)
    c = polynomial(cosine_terms, u)
    return 1.0 - s * s, s * c


def call(kernel, outs, scratch=(), flops=0, bytes_accessed=0, smem=0, count=0):
    vmem = pl.BlockSpec(memory_space=pltpu.VMEM)
    scalars = [pl.BlockSpec(memory_space=pltpu.SMEM)] * smem
    return pl.pallas_call(
        kernel,
        out_shape=outs,
        in_specs=scalars + [vmem] * count,
        out_specs=jax.tree.map(lambda _: vmem, outs),
        scratch_shapes=list(scratch),
        compiler_params=pltpu.CompilerParams(vmem_limit_bytes=VMEM_LIMIT),
        cost_estimate=pl.CostEstimate(flops=flops, bytes_accessed=bytes_accessed, transcendentals=0),
    )


def pack_kernel(feat, pos, weight, out):
    projected = dot(weight[...], feat[...], ((0,), (0,))).astype(jnp.bfloat16)
    pieces = in_three(pos[...])
    pad = jnp.zeros((PACK - F - 9, ATOM), jnp.bfloat16)
    row = jnp.concatenate([projected, *pieces, pad], axis=0)
    for p in range(PLANE):
        out[p] = row


def halo_kernel(feat, vec, pos, halo, up, down):
    pieces = in_three(pos[...])
    pad = jnp.zeros((5, ATOM), jnp.bfloat16)
    tail = jnp.zeros((HALO_ROWS - 280, ATOM), jnp.bfloat16)
    rows = jnp.concatenate(
        [feat[...], vec[0], vec[1], vec[2], pieces[0], pad, pieces[1], pad, pieces[2], pad, tail], axis=0
    )
    atom = lax.broadcasted_iota(jnp.int32, (ATOM, ATOM), 0)
    for side, out in ((0, up), (1, down)):
        chosen = jnp.where(atom == halo[side : side + 1, :], 1.0, 0.0).astype(jnp.bfloat16)
        out[...] = dot(rows, chosen, ((1,), (0,))).astype(jnp.bfloat16)


def table_kernel(k_at, got, lattice, table, partial, columns, total):
    rows = lattice[:, pl.ds(pl.multiple_of(k_at[0], KDEV), KDEV)].astype(jnp.float32)
    turned = jnp.concatenate([rows, jnp.zeros((5, KDEV), jnp.float32)], axis=0).T
    for i in range(3):
        columns[i] = jnp.broadcast_to(turned[:, i : i + 1], (KDEV, ATOM))
    total[...] = jnp.zeros_like(total)

    @pl.loop(0, PLANE // 2)
    def _(step):
        left, right = got[2 * step], got[2 * step + 1]
        both = jnp.concatenate([left, right], axis=1)
        pieces = both[F : F + 16].astype(jnp.float32)
        pos = pieces[0:3] + pieces[3:6] + pieces[6:9]
        at = pl.ds(pl.multiple_of(step * 2 * ATOM, 2 * ATOM), 2 * ATOM)
        for k in range(0, KDEV, 32):
            halves = []
            for half in range(2):
                lanes = slice(half * ATOM, (half + 1) * ATOM)
                turns = (
                    columns[0, k : k + 32] * pos[0:1, lanes] + columns[1, k : k + 32] * pos[1:2, lanes]
                ) + columns[2, k : k + 32] * pos[2:3, lanes]
                halves.append(cosine_and_sine(turns))
            for i in range(2):
                table[i * KDEV + k : i * KDEV + k + 32, at] = jnp.concatenate(
                    [halves[0][i], halves[1][i]], axis=1
                ).astype(jnp.bfloat16)
        total[...] += dot(table[:, at], both[:F], ((1,), (1,)))

    partial[...] = jnp.concatenate([total[:KDEV], total[KDEV:]], axis=1).astype(jnp.bfloat16)


def sum_kernel(arrived, out):
    total = arrived[0].astype(jnp.float32)
    for i in range(1, DEPTH):
        total = total + arrived[i].astype(jnp.float32)
    total = total.astype(jnp.bfloat16)
    for i in range(DEPTH):
        out[i] = total


def project_kernel(half_at, got, kfilter, table, out):
    total = got[...].astype(jnp.float32).T
    own = kfilter[:, pl.ds(pl.multiple_of(half_at[0], KDEV), KDEV)]
    filtered = jnp.concatenate([own * total[:F] * norm_scale, own * total[F:] * norm_scale], axis=1)
    filtered = filtered.astype(jnp.bfloat16)

    @pl.loop(0, PLANE // 2)
    def _(step):
        at = pl.ds(pl.multiple_of(step * 2 * ATOM, 2 * ATOM), 2 * ATOM)
        message = dot(filtered, table[:, at], ((1,), (0,))).astype(jnp.bfloat16)
        out[2 * step] = message[:, :ATOM]
        out[2 * step + 1] = message[:, ATOM:]


def finish_kernel(arrived, scalar, out):
    total = arrived[0].astype(jnp.float32)
    for i in range(1, PLANE):
        total = total + arrived[i].astype(jnp.float32)
    out[...] = (scalar[...] + total).astype(jnp.bfloat16)


def short_kernel(
    feat, vec, pos, ids, below, above, node_weight, bias, message_weight, radial_weight,
    scalar_out, vector_out, ext, chosen, filters, directions,
):
    pieces = in_three(pos[...])
    pad = jnp.zeros((5, ATOM), jnp.bfloat16)
    tail = jnp.zeros((8, ATOM), jnp.bfloat16)
    own_tail = jnp.concatenate([pieces[0], pad, pieces[1], pad, pieces[2], pad, tail], axis=0)
    own_vec = jnp.concatenate([vec[0], vec[1], vec[2]], axis=0)
    ext[192:, :ATOM] = jnp.concatenate([own_vec, own_tail], axis=0)
    ext[192:, ATOM : 2 * ATOM] = below[F:]
    ext[192:, 2 * ATOM :] = above[F:]
    ext_feat = jnp.concatenate([feat[...], below[:F], above[:F]], axis=1)
    hidden = dot(node_weight[...], ext_feat, ((0,), (0,))) + bias[...]
    hidden = (hidden / (1.0 + jnp.exp(-hidden))).astype(jnp.bfloat16)
    ext[:192] = dot(message_weight[...], hidden, ((0,), (0,))).astype(jnp.bfloat16)

    number = lax.broadcasted_iota(jnp.int32, (3 * ATOM, ATOM), 0)
    for j in range(NBR):
        chosen[:, j * ATOM : (j + 1) * ATOM] = jnp.where(number == ids[j : j + 1, :], 1.0, 0.0).astype(jnp.bfloat16)
    found = dot(ext[384:], chosen[...], ((1,), (0,)))
    there = found[0:3] + found[8:11] + found[16:19]
    here = jnp.concatenate([pos[...]] * NBR, axis=1)
    offset = there - here
    offset = offset - jnp.floor(offset + 0.5)
    side = lax.broadcasted_iota(jnp.int32, (3, 1), 0)
    box = jnp.where(side == 2, slab_depth * SLABS, side_length).astype(jnp.float32)
    cartesian = offset * box
    square = cartesian * cartesian
    distance = jnp.sqrt(square[0:1] + square[1:2] + square[2:3])
    directions[0:3] = cartesian / jnp.maximum(distance, distance_floor)
    center = lax.broadcasted_iota(jnp.int32, (NRBF, 1), 0).astype(jnp.float32) * (radial_reach / (NRBF - 1))
    away = (distance - center) / (1.5 * radial_reach / NRBF)
    radial = jnp.exp(-(away * away)).astype(jnp.bfloat16)
    filters[...] = dot(radial_weight[...], radial, ((0,), (0,)))

    def slots(step, sums):
        at = pl.ds(pl.multiple_of(step * 2 * ATOM, 2 * ATOM), 2 * ATOM)
        picked = dot(ext[:384], chosen[:, at], ((1,), (0,)))
        terms = picked[:192] * filters[:, at]
        toward = directions[:, at]
        parts = [terms[:F]]
        for x in range(3):
            parts.append(
                picked[192 + x * F : 192 + (x + 1) * F] * terms[F : 2 * F] + terms[2 * F :] * toward[x : x + 1]
            )
        return tuple(s + p[:, :ATOM] + p[:, ATOM:] for s, p in zip(sums, parts))

    zero = jnp.zeros((F, ATOM), jnp.float32)
    sums = lax.fori_loop(0, NBR // 2, slots, (zero,) * 4)
    scalar_out[...] = feat[...].astype(jnp.float32) + sums[0]
    for x in range(3):
        vector_out[x] = (vec[x].astype(jnp.float32) + sums[1 + x]).astype(jnp.bfloat16)


def exchanged(x, axes):
    return lax.all_to_all(x, axes, split_axis=0, concat_axis=0, tiled=True)


def shifted(x, steps):
    return lax.ppermute(x, all_axes, [(i, (i + steps) % SLABS) for i in range(SLABS)])


def shards(
    features, vectors, positions, neighbours, halo_lists, lattice, kspace_filter,
    node_weight, node_bias, message_weight, radial_weight, ewald_weight,
):
    bf16, f32 = jnp.bfloat16, jnp.float32
    shape = jax.ShapeDtypeStruct
    half_at = (lax.axis_index("yh") * KDEV).astype(jnp.int32).reshape(1)
    k_at = (lax.axis_index(kb_axes) * 2 * KDEV + half_at).astype(jnp.int32).reshape(1)
    packed = call(pack_kernel, shape((PLANE, PACK, ATOM), bf16), count=3)(features, positions, ewald_weight)
    got = exchanged(packed, plane_axes)
    up, down = call(halo_kernel, (shape((HALO_ROWS, ATOM), bf16),) * 2, count=4)(
        features, vectors, positions, halo_lists
    )
    below, above = shifted(up, 1), shifted(down, -1)
    table, partial = call(
        table_kernel,
        (shape((2 * KDEV, PLANE * ATOM), bf16), shape((KDEV, 2 * F), bf16)),
        scratch=[pltpu.VMEM((3, KDEV, ATOM), f32), pltpu.VMEM((2 * KDEV, F), f32)],
        smem=1,
        count=2,
    )(k_at, got, lattice)
    arrived = exchanged(partial.reshape(DEPTH, KDEV // DEPTH, 2 * F), "z")
    scalar, new_vectors = call(
        short_kernel,
        (shape((F, ATOM), f32), shape((3, F, ATOM), bf16)),
        scratch=[
            pltpu.VMEM((EXT_ROWS, 3 * ATOM), bf16),
            pltpu.VMEM((3 * ATOM, NBR * ATOM), bf16),
            pltpu.VMEM((192, NBR * ATOM), f32),
            pltpu.VMEM((8, NBR * ATOM), f32),
        ],
        count=10,
    )(
        features, vectors, positions, neighbours, below, above,
        node_weight, node_bias[:, None], message_weight, radial_weight,
    )
    owned = call(sum_kernel, shape((DEPTH, KDEV // DEPTH, 2 * F), bf16), count=1)(arrived)
    totals = exchanged(owned, "z").reshape(KDEV, 2 * F)
    messages = call(project_kernel, shape((PLANE, F, ATOM), bf16), smem=1, count=3)(
        half_at, totals, kspace_filter, table
    )
    returned = exchanged(messages, plane_axes)
    new_features = call(finish_kernel, shape((F, ATOM), bf16), count=2)(returned, scalar)
    return new_features, new_vectors


def solution(mesh):
    fine = Mesh(mesh.devices.reshape(2, 16, 2, 4, 2), all_axes)
    atoms = P(None, all_axes)
    placed = (
        atoms, P(None, None, all_axes), atoms, atoms, atoms, P(), P(None, kb_axes),
        P(), P(), P(), P(), P(),
    )
    return jax.shard_map(
        shards,
        mesh=fine,
        in_specs=placed,
        out_specs=(atoms, P(None, None, all_axes)),
        check_vma=False,
    )
```

```python
import math

import jax
import jax.numpy as jnp
from jax import lax
from jax.experimental import pallas as pl
from jax.experimental.pallas import tpu as pltpu
from jax.sharding import Mesh
from jax.sharding import PartitionSpec as P

F = 64
NRBF = 20
NBR = 16
ATOM = 128
KDEV = 256
PLANE = 32
DEPTH = 16
SLABS = 512
KVEC = 8192
ATOMS = 65536
PACK = 80
HALO_ROWS = 288
EXT_ROWS = 416
GROUP = 8

plane_axes = ("yh", "yl", "x", "c")
kb_axes = ("yl", "x", "c")
all_axes = ("yh", "z", "yl", "x", "c")

side_length = 6.0
slab_depth = 6.0
radial_reach = 6.0
distance_floor = 1.0
norm_scale = 1.0 / math.sqrt(KVEC * ATOMS)

sine_terms = (4.44287959, -7.30781805, 3.59778873, -0.79123821)
cosine_terms = (1.41420408, -6.97764206, 5.71523839, -1.72834865)
whole_turns = 1.5 * 2.0**23

VMEM_LIMIT = 16 * 2**20
TABLE_LIMIT = 51 * 2**20


def dot(a, b, dims):
    return lax.dot_general(a, b, (dims, ((), ())), preferred_element_type=jnp.float32)


def in_three(value):
    first = value.astype(jnp.bfloat16)
    rest = value - first.astype(jnp.float32)
    second = rest.astype(jnp.bfloat16)
    third = (rest - second.astype(jnp.float32)).astype(jnp.bfloat16)
    return first, second, third


def polynomial(terms, u):
    value = terms[-1] * u + terms[-2]
    for term in terms[-3::-1]:
        value = value * u + term
    return value


def cosine_and_sine(turns):
    r = turns - ((turns + whole_turns) - whole_turns)
    u = r * r
    s = r * polynomial(sine_terms, u)
    c = polynomial(cosine_terms, u)
    return 1.0 - s * s, s * c


VM, SM, ANY, FAR = pltpu.VMEM, pltpu.SMEM, pl.ANY, pltpu.HBM


def call(kernel, places, outs, *operands, scratch=(), out_places=None, limit=VMEM_LIMIT):
    return pl.pallas_call(
        kernel,
        out_shape=outs,
        in_specs=[pl.BlockSpec(memory_space=place) for place in places],
        out_specs=jax.tree.map(lambda _: pl.BlockSpec(memory_space=VM), outs)
        if out_places is None
        else tuple(pl.BlockSpec(memory_space=place) for place in out_places),
        scratch_shapes=list(scratch),
        compiler_params=pltpu.CompilerParams(vmem_limit_bytes=limit),
        cost_estimate=pl.CostEstimate(flops=0, bytes_accessed=0, transcendentals=0),
    )(*operands)


def packed_for_all(feat, pos, count):
    first = lax.reduce_precision(pos, 8, 7)
    second = lax.reduce_precision(pos - first, 8, 7)
    third = (pos - first) - second
    pieces = [piece.astype(jnp.bfloat16) for piece in (first, second, third)]
    pad = jnp.zeros((PACK - F - 9, ATOM), jnp.bfloat16)
    return jnp.broadcast_to(jnp.concatenate([feat, *pieces, pad], axis=0), (count, PACK, ATOM))


def prepare_kernel(places, feat, vec, pos, halo, lattice, kfilter, up, down, columns, own_filter):
    pieces = in_three(pos[...])
    pad = jnp.zeros((5, ATOM), jnp.bfloat16)
    tail = jnp.zeros((HALO_ROWS - 280, ATOM), jnp.bfloat16)
    rows = jnp.concatenate(
        [feat[...], vec[0], vec[1], vec[2], pieces[0], pad, pieces[1], pad, pieces[2], pad, tail], axis=0
    )
    atom = lax.broadcasted_iota(jnp.int32, (ATOM, ATOM), 0)
    for side, out in ((0, up), (1, down)):
        chosen = jnp.where(atom == halo[side : side + 1, :], 1.0, 0.0).astype(jnp.bfloat16)
        out[...] = dot(rows, chosen, ((1,), (0,))).astype(jnp.bfloat16)
    own = lattice[:, pl.ds(pl.multiple_of(places[0], KDEV), KDEV)].astype(jnp.float32)
    turned = jnp.concatenate([own, jnp.zeros((5, KDEV), jnp.float32)], axis=0).T
    for i in range(3):
        columns[i] = jnp.broadcast_to(turned[:, i : i + 1], (KDEV, ATOM))
    own_filter[...] = kfilter[:, pl.ds(pl.multiple_of(places[1], KDEV), KDEV)] * norm_scale


def table_kernel(got, columns, weight, below, above, own_filter, table_at, partial, table, total, done):
    total[...] = jnp.zeros_like(total)

    def stored(step):
        columns_of = pl.ds(pl.multiple_of(step * GROUP * ATOM, GROUP * ATOM), GROUP * ATOM)
        return pltpu.make_async_copy(table.at[:, columns_of], table_at.at[:, columns_of], done.at[step])

    @pl.loop(0, PLANE // GROUP)
    def _(step):
        for pair in range(0, GROUP, 2):
            first = step * GROUP + pair
            both = jnp.concatenate([got[first], got[first + 1]], axis=1)
            pieces = both[F : F + 16].astype(jnp.float32)
            pos = pieces[0:3] + pieces[3:6] + pieces[6:9]
            projected = dot(weight[...], both[:F], ((0,), (0,))).astype(jnp.bfloat16)
            at = pl.ds(pl.multiple_of(first * ATOM, 2 * ATOM), 2 * ATOM)
            for k in range(0, KDEV, 64):
                tiles = []
                for part in range(k, k + 64, 16):
                    halves = []
                    for half in range(2):
                        lanes = slice(half * ATOM, (half + 1) * ATOM)
                        turns = (
                            columns[0, part : part + 16] * pos[0:1, lanes]
                            + columns[1, part : part + 16] * pos[1:2, lanes]
                        ) + columns[2, part : part + 16] * pos[2:3, lanes]
                        halves.append(cosine_and_sine(turns))
                    tiles.append(
                        [jnp.concatenate([halves[0][i], halves[1][i]], axis=1).astype(jnp.bfloat16) for i in range(2)]
                    )
                cosines = jnp.concatenate([t[0] for t in tiles], axis=0)
                sines = jnp.concatenate([t[1] for t in tiles], axis=0)
                table[k : k + 64, at] = cosines
                table[KDEV + k : KDEV + k + 64, at] = sines
                sums = dot(jnp.concatenate([cosines, sines], axis=0), projected, ((1,), (1,)))
                total[k : k + 64] += sums[:64]
                total[KDEV + k : KDEV + k + 64] += sums[64:]
        stored(step).start()

    partial[...] = jnp.concatenate([total[:KDEV], total[KDEV:]], axis=1).astype(jnp.bfloat16)
    for step in range(PLANE // GROUP):
        stored(step).wait()


def sum_kernel(arrived, scalar, out):
    total = arrived[0].astype(jnp.float32)
    for i in range(1, DEPTH):
        total = total + arrived[i].astype(jnp.float32)
    total = total.astype(jnp.bfloat16)
    for i in range(DEPTH):
        out[i] = total


def project_kernel(got, own_filter, table_at, out, table, done):
    width = 8 * ATOM
    loads = [
        pltpu.make_async_copy(
            table_at.at[:, i * width : (i + 1) * width], table.at[:, i * width : (i + 1) * width], done.at[i]
        )
        for i in range(PLANE // 8)
    ]
    for load in loads:
        load.start()
    total = got[...].astype(jnp.float32).T
    own = own_filter[...]
    filtered = jnp.concatenate([own * total[:F], own * total[F:]], axis=1).astype(jnp.bfloat16)
    for i, load in enumerate(loads):
        load.wait()
        message = dot(filtered, table[:, i * width : (i + 1) * width], ((1,), (0,))).astype(jnp.bfloat16)
        for p in range(8):
            out[8 * i + p] = message[:, p * ATOM : (p + 1) * ATOM]


def finish_kernel(arrived, scalar, out):
    total = arrived[0].astype(jnp.float32)
    for i in range(1, PLANE):
        total = total + arrived[i].astype(jnp.float32)
    out[...] = (scalar[...] + total).astype(jnp.bfloat16)


def short_kernel(
    feat, vec, pos, ids, below, above, node_weight, bias, message_weight, radial_weight,
    scalar_out, vector_out, ext, chosen, filters, directions,
):
    pieces = in_three(pos[...])
    pad = jnp.zeros((5, ATOM), jnp.bfloat16)
    tail = jnp.zeros((8, ATOM), jnp.bfloat16)
    own_tail = jnp.concatenate([pieces[0], pad, pieces[1], pad, pieces[2], pad, tail], axis=0)
    own_vec = jnp.concatenate([vec[0], vec[1], vec[2]], axis=0)
    ext[192:, :ATOM] = jnp.concatenate([own_vec, own_tail], axis=0)
    ext[192:, ATOM : 2 * ATOM] = below[F:]
    ext[192:, 2 * ATOM :] = above[F:]
    ext_feat = jnp.concatenate([feat[...], below[:F], above[:F]], axis=1)
    hidden = dot(node_weight[...], ext_feat, ((0,), (0,))) + bias[...]
    hidden = (hidden / (1.0 + jnp.exp(-hidden))).astype(jnp.bfloat16)
    ext[:192] = dot(message_weight[...], hidden, ((0,), (0,))).astype(jnp.bfloat16)

    number = lax.broadcasted_iota(jnp.int32, (3 * ATOM, ATOM), 0)
    for j in range(NBR):
        chosen[:, j * ATOM : (j + 1) * ATOM] = jnp.where(number == ids[j : j + 1, :], 1.0, 0.0).astype(jnp.bfloat16)
    found = dot(ext[384:], chosen[...], ((1,), (0,)))
    there = found[0:3] + found[8:11] + found[16:19]
    here = jnp.concatenate([pos[...]] * NBR, axis=1)
    offset = there - here
    offset = offset - jnp.floor(offset + 0.5)
    side = lax.broadcasted_iota(jnp.int32, (3, 1), 0)
    box = jnp.where(side == 2, slab_depth * SLABS, side_length).astype(jnp.float32)
    cartesian = offset * box
    square = cartesian * cartesian
    distance = jnp.sqrt(square[0:1] + square[1:2] + square[2:3])
    directions[0:3] = cartesian / jnp.maximum(distance, distance_floor)
    center = lax.broadcasted_iota(jnp.int32, (NRBF, 1), 0).astype(jnp.float32) * (radial_reach / (NRBF - 1))
    away = (distance - center) / (1.5 * radial_reach / NRBF)
    radial = jnp.exp(-(away * away)).astype(jnp.bfloat16)
    filters[...] = dot(radial_weight[...], radial, ((0,), (0,)))

    def slots(step, sums):
        at = pl.ds(pl.multiple_of(step * 2 * ATOM, 2 * ATOM), 2 * ATOM)
        picked = dot(ext[:384], chosen[:, at], ((1,), (0,)))
        terms = picked[:192] * filters[:, at]
        toward = directions[:, at]
        parts = [terms[:F]]
        for x in range(3):
            parts.append(
                picked[192 + x * F : 192 + (x + 1) * F] * terms[F : 2 * F] + terms[2 * F :] * toward[x : x + 1]
            )
        return tuple(s + p[:, :ATOM] + p[:, ATOM:] for s, p in zip(sums, parts))

    zero = jnp.zeros((F, ATOM), jnp.float32)
    sums = lax.fori_loop(0, NBR // 2, slots, (zero,) * 4)
    scalar_out[...] = feat[...].astype(jnp.float32) + sums[0]
    for x in range(3):
        vector_out[x] = (vec[x].astype(jnp.float32) + sums[1 + x]).astype(jnp.bfloat16)


def exchanged(x, axes):
    return lax.all_to_all(x, axes, split_axis=0, concat_axis=0, tiled=True)


def shifted(x, steps):
    return lax.ppermute(x, all_axes, [(i, (i + steps) % SLABS) for i in range(SLABS)])


def shards(
    features, vectors, positions, neighbours, halo_lists, lattice, kspace_filter,
    node_weight, node_bias, message_weight, radial_weight, ewald_weight,
):
    bf16, f32 = jnp.bfloat16, jnp.float32
    shape = jax.ShapeDtypeStruct
    half_at = lax.axis_index("yh") * KDEV
    places = jnp.stack([lax.axis_index(kb_axes) * 2 * KDEV + half_at, half_at]).astype(jnp.int32)
    got = exchanged(packed_for_all(features, positions, PLANE), plane_axes)
    halo = shape((HALO_ROWS, ATOM), bf16)
    up, down, columns, own_filter = call(
        prepare_kernel,
        [SM] + [VM] * 6,
        (halo, halo, shape((3, KDEV, ATOM), f32), shape((F, KDEV), f32)),
        places, features, vectors, positions, halo_lists, lattice, kspace_filter,
    )
    below, above = shifted(up, 1), shifted(down, -1)
    table, partial = call(
        table_kernel,
        [VM, VM, VM, ANY, ANY, ANY],
        (shape((2 * KDEV, PLANE * ATOM), bf16), shape((KDEV, 2 * F), bf16)),
        got, columns, ewald_weight, below, above, own_filter,
        scratch=[
            VM((2 * KDEV, PLANE * ATOM), bf16),
            VM((2 * KDEV, F), f32),
            pltpu.SemaphoreType.DMA((PLANE // GROUP,)),
        ],
        out_places=[FAR, VM],
        limit=TABLE_LIMIT,
    )
    arrived = exchanged(partial.reshape(DEPTH, KDEV // DEPTH, 2 * F), "z")
    scalar, new_vectors = call(
        short_kernel,
        [VM] * 10,
        (shape((F, ATOM), f32), shape((3, F, ATOM), bf16)),
        features, vectors, positions, neighbours, below, above,
        node_weight, node_bias[:, None], message_weight, radial_weight,
        scratch=[
            VM((EXT_ROWS, 3 * ATOM), bf16),
            VM((3 * ATOM, NBR * ATOM), bf16),
            VM((192, NBR * ATOM), f32),
            VM((8, NBR * ATOM), f32),
        ],
    )
    owned = call(sum_kernel, [VM, ANY], shape((DEPTH, KDEV // DEPTH, 2 * F), bf16), arrived, scalar)
    totals = exchanged(owned, "z").reshape(KDEV, 2 * F)
    messages = call(
        project_kernel, [VM, VM, FAR], shape((PLANE, F, ATOM), bf16), totals, own_filter, table,
        scratch=[VM((2 * KDEV, PLANE * ATOM), bf16), pltpu.SemaphoreType.DMA((PLANE // 8,))],
        limit=TABLE_LIMIT,
    )
    returned = exchanged(messages, plane_axes)
    new_features = call(finish_kernel, [VM] * 2, shape((F, ATOM), bf16), returned, scalar)
    return new_features, new_vectors


def solution(mesh):
    fine = Mesh(mesh.devices.reshape(2, 16, 2, 4, 2), all_axes)
    atoms = P(None, all_axes)
    placed = (
        atoms, P(None, None, all_axes), atoms, atoms, atoms, P(), P(None, kb_axes),
        P(), P(), P(), P(), P(),
    )
    return jax.shard_map(
        shards,
        mesh=fine,
        in_specs=placed,
        out_specs=(atoms, P(None, None, all_axes)),
        check_vma=False,
    )
```

```python
import math

import jax
import jax.numpy as jnp
from jax import lax
from jax.experimental import pallas as pl
from jax.experimental.pallas import tpu as pltpu
from jax.sharding import Mesh
from jax.sharding import PartitionSpec as P

F = 64
NRBF = 20
NBR = 16
ATOM = 128
KDEV = 256
PLANE = 32
DEPTH = 16
SLABS = 512
KVEC = 8192
ATOMS = 65536
PACK = 80
HALO_ROWS = 272
GROUP = 8

plane_axes = ("yh", "yl", "x", "c")
kb_axes = ("yl", "x", "c")
all_axes = ("yh", "z", "yl", "x", "c")

side_length = 6.0
slab_depth = 6.0
radial_reach = 6.0
distance_floor = 1.0
norm_scale = 1.0 / math.sqrt(KVEC * ATOMS)

sine_terms = (4.44287959, -7.30781805, 3.59778873, -0.79123821)
cosine_terms = (1.41420408, -6.97764206, 5.71523839, -1.72834865)
whole_turns = 1.5 * 2.0**23

VMEM_LIMIT = 16 * 2**20


def dot(a, b, dims):
    return lax.dot_general(a, b, (dims, ((), ())), preferred_element_type=jnp.float32)


def polynomial(terms, u):
    value = terms[-1] * u + terms[-2]
    for term in terms[-3::-1]:
        value = value * u + term
    return value


def cosine_and_sine(turns):
    r = turns - ((turns + whole_turns) - whole_turns)
    u = r * r
    s = r * polynomial(sine_terms, u)
    c = polynomial(cosine_terms, u)
    return 1.0 - s * s, s * c


VM, SM, ANY = pltpu.VMEM, pltpu.SMEM, pl.ANY


def call(kernel, places, outs, *operands, scratch=()):
    return pl.pallas_call(
        kernel,
        out_shape=outs,
        in_specs=[pl.BlockSpec(memory_space=place) for place in places],
        out_specs=jax.tree.map(lambda _: pl.BlockSpec(memory_space=VM), outs),
        scratch_shapes=list(scratch),
        compiler_params=pltpu.CompilerParams(vmem_limit_bytes=VMEM_LIMIT),
        cost_estimate=pl.CostEstimate(flops=0, bytes_accessed=0, transcendentals=0),
    )(*operands)


def packed_rows(feat, pos):
    first = lax.reduce_precision(pos, 8, 7)
    second = lax.reduce_precision(pos - first, 8, 7)
    third = (pos - first) - second
    rows = jnp.pad(feat, ((0, PACK - F), (0, 0)))
    for i, piece in enumerate((first, second, third)):
        at = F + 3 * i
        rows = rows + jnp.pad(piece.astype(jnp.bfloat16), ((at, PACK - at - 3), (0, 0)))
    return rows


def summed(pieces):
    return pieces[0:3] + pieces[3:6] + pieces[6:9]


def halo_kernel(packed, vec, halo, up, down):
    rows = jnp.concatenate([packed[...], vec[0], vec[1], vec[2]], axis=0)
    atom = lax.broadcasted_iota(jnp.int32, (ATOM, ATOM), 0)
    for side, out in ((0, up), (1, down)):
        chosen = jnp.where(atom == halo[side : side + 1, :], 1.0, 0.0).astype(jnp.bfloat16)
        out[...] = dot(rows, chosen, ((1,), (0,))).astype(jnp.bfloat16)


def prepare_kernel(places, lattice, kfilter, weight, columns, own_filter, own_weight):
    own_weight[...] = weight[...]
    own = lattice[:, pl.ds(pl.multiple_of(places[0], KDEV), KDEV)].astype(jnp.float32)
    turned = jnp.concatenate([own, jnp.zeros((5, KDEV), jnp.float32)], axis=0).T
    for i in range(3):
        columns[i] = jnp.broadcast_to(turned[:, i : i + 1], (KDEV, ATOM))
    own_filter[...] = kfilter[:, pl.ds(pl.multiple_of(places[1], KDEV), KDEV)] * norm_scale


def table_kernel(got, columns, below, above, own_filter, table, partial, total):
    total[...] = jnp.zeros_like(total)

    @pl.loop(0, PLANE // GROUP)
    def _(step):
        for pair in range(0, GROUP, 2):
            first = step * GROUP + pair
            both = jnp.concatenate([got[first], got[first + 1]], axis=1)
            pos = summed(both[F:].astype(jnp.float32))
            at = pl.ds(pl.multiple_of(first * ATOM, 2 * ATOM), 2 * ATOM)
            for k in range(0, KDEV, 64):
                rows = slice(k, k + 64)
                halves = []
                for lanes in (slice(0, ATOM), slice(ATOM, 2 * ATOM)):
                    halves.append(
                        (columns[0, rows] * pos[0:1, lanes] + columns[1, rows] * pos[1:2, lanes])
                        + columns[2, rows] * pos[2:3, lanes]
                    )
                cosines, sines = cosine_and_sine(jnp.concatenate(halves, axis=1))
                cosines, sines = cosines.astype(jnp.bfloat16), sines.astype(jnp.bfloat16)
                table[k : k + 64, at] = cosines
                table[KDEV + k : KDEV + k + 64, at] = sines
                sums = dot(jnp.concatenate([cosines, sines], axis=0), both[:F], ((1,), (1,)))
                total[k : k + 64] += sums[:64]
                total[KDEV + k : KDEV + k + 64] += sums[64:]

    partial[...] = jnp.concatenate([total[:KDEV], total[KDEV:]], axis=1).astype(jnp.bfloat16)


def sum_kernel(arrived, out):
    total = arrived[0].astype(jnp.float32)
    for i in range(1, DEPTH):
        total = total + arrived[i].astype(jnp.float32)
    total = total.astype(jnp.bfloat16)
    for i in range(DEPTH):
        out[i] = total


def project_kernel(got, own_filter, weight, table, out):
    own = own_filter[...]
    total = [dot(weight[...], got[:, part * F : (part + 1) * F], ((0,), (1,))) for part in range(2)]
    filtered = jnp.concatenate([own * total[0], own * total[1]], axis=1).astype(jnp.bfloat16)
    for first in range(0, PLANE, 8):
        message = dot(filtered, table[:, first * ATOM : (first + 8) * ATOM], ((1,), (0,))).astype(jnp.bfloat16)
        for p in range(8):
            out[first + p] = message[:, p * ATOM : (p + 1) * ATOM]


def finish_kernel(arrived, scalar, out):
    total = arrived[0].astype(jnp.float32)
    for i in range(1, PLANE):
        total = total + arrived[i].astype(jnp.float32)
    out[...] = (scalar[...] + total).astype(jnp.bfloat16)


def short_kernel(
    packed, vec, ids, below, above, node_weight, bias, message_weight, radial_weight, messages,
    scalar_out, vector_out, ext, chosen, filters, directions,
):
    pos = summed(packed[F:].astype(jnp.float32))
    ext[192:384, :ATOM] = jnp.concatenate([vec[0], vec[1], vec[2]], axis=0)
    ext[384:, :ATOM] = packed[F:]
    for side, at in ((below, ATOM), (above, 2 * ATOM)):
        ext[192:384, at : at + ATOM] = side[PACK:]
        ext[384:, at : at + ATOM] = side[F:PACK]
    ext_feat = jnp.concatenate([packed[:F], below[:F], above[:F]], axis=1)
    bias_column = jnp.broadcast_to(bias[...], (8, F)).T[:, 0:1]
    hidden = dot(node_weight[...], ext_feat, ((0,), (0,))) + bias_column
    hidden = (hidden / (1.0 + jnp.exp(-hidden))).astype(jnp.bfloat16)
    ext[:192] = dot(message_weight[...], hidden, ((0,), (0,))).astype(jnp.bfloat16)

    number = lax.broadcasted_iota(jnp.int32, (3 * ATOM, ATOM), 0)
    for j in range(NBR):
        chosen[:, j * ATOM : (j + 1) * ATOM] = jnp.where(number == ids[j : j + 1, :], 1.0, 0.0).astype(jnp.bfloat16)
    found = dot(ext[384:], chosen[...], ((1,), (0,)))
    offset = summed(found) - jnp.concatenate([pos] * NBR, axis=1)
    offset = offset - jnp.floor(offset + 0.5)
    side = lax.broadcasted_iota(jnp.int32, (3, 1), 0)
    box = jnp.where(side == 2, slab_depth * SLABS, side_length).astype(jnp.float32)
    cartesian = offset * box
    square = cartesian * cartesian
    distance = jnp.sqrt(square[0:1] + square[1:2] + square[2:3])
    directions[0:3] = cartesian / jnp.maximum(distance, distance_floor)
    center = lax.broadcasted_iota(jnp.int32, (NRBF, 1), 0).astype(jnp.float32) * (radial_reach / (NRBF - 1))
    away = (distance - center) / (1.5 * radial_reach / NRBF)
    radial = jnp.exp(-(away * away)).astype(jnp.bfloat16)
    filters[...] = dot(radial_weight[...], radial, ((0,), (0,)))

    def slots(step, sums):
        at = pl.ds(pl.multiple_of(step * 2 * ATOM, 2 * ATOM), 2 * ATOM)
        picked = dot(ext[:384], chosen[:, at], ((1,), (0,)))
        terms = picked[:192] * filters[:, at]
        toward = directions[:, at]
        parts = [terms[:F]]
        for x in range(3):
            parts.append(
                picked[192 + x * F : 192 + (x + 1) * F] * terms[F : 2 * F] + terms[2 * F :] * toward[x : x + 1]
            )
        return tuple(s + p[:, :ATOM] + p[:, ATOM:] for s, p in zip(sums, parts))

    zero = jnp.zeros((F, ATOM), jnp.float32)
    sums = lax.fori_loop(0, NBR // 2, slots, (zero,) * 4)
    scalar_out[...] = packed[:F].astype(jnp.float32) + sums[0]
    for x in range(3):
        vector_out[x] = (vec[x].astype(jnp.float32) + sums[1 + x]).astype(jnp.bfloat16)


def exchanged(x, axes):
    return lax.all_to_all(x, axes, split_axis=0, concat_axis=0, tiled=True)


def shifted(x, steps):
    return lax.ppermute(x, all_axes, [(i, (i + steps) % SLABS) for i in range(SLABS)])


def shards(
    features, vectors, positions, neighbours, halo_lists, lattice, kspace_filter,
    node_weight, node_bias, message_weight, radial_weight, ewald_weight,
):
    bf16, f32 = jnp.bfloat16, jnp.float32
    shape = jax.ShapeDtypeStruct
    half_at = lax.axis_index("yh") * KDEV
    places = jnp.stack([lax.axis_index(kb_axes) * 2 * KDEV + half_at, half_at]).astype(jnp.int32)
    packed = packed_rows(features, positions)
    got = exchanged(jnp.broadcast_to(packed, (PLANE, PACK, ATOM)), plane_axes)
    halo = shape((HALO_ROWS, ATOM), bf16)
    up, down = call(halo_kernel, [VM] * 3, (halo, halo), packed, vectors, halo_lists)
    below, above = shifted(up, 1), shifted(down, -1)
    columns, own_filter, own_weight = call(
        prepare_kernel,
        [SM, VM, VM, VM],
        (shape((3, KDEV, ATOM), f32), shape((F, KDEV), f32), shape((F, F), bf16)),
        places, lattice, kspace_filter, ewald_weight,
    )
    table, partial = call(
        table_kernel,
        [VM, VM, ANY, ANY, ANY],
        (shape((2 * KDEV, PLANE * ATOM), bf16), shape((KDEV, 2 * F), bf16)),
        got, columns, below, above, own_filter,
        scratch=[VM((2 * KDEV, F), f32)],
    )
    arrived = exchanged(partial.reshape(DEPTH, KDEV // DEPTH, 2 * F), "z")
    owned = call(sum_kernel, [VM], shape((DEPTH, KDEV // DEPTH, 2 * F), bf16), arrived)
    totals = exchanged(owned, "z").reshape(KDEV, 2 * F)
    messages = call(
        project_kernel, [VM] * 4, shape((PLANE, F, ATOM), bf16), totals, own_filter, own_weight, table
    )
    returned = exchanged(messages, plane_axes)
    scalar, new_vectors = call(
        short_kernel,
        [VM] * 9 + [ANY],
        (shape((F, ATOM), f32), shape((3, F, ATOM), bf16)),
        packed, vectors, neighbours, below, above,
        node_weight, node_bias.reshape(1, F), message_weight, radial_weight, messages,
        scratch=[
            VM((400, 3 * ATOM), bf16),
            VM((3 * ATOM, NBR * ATOM), bf16),
            VM((192, NBR * ATOM), f32),
            VM((8, NBR * ATOM), f32),
        ],
    )
    new_features = call(finish_kernel, [VM] * 2, shape((F, ATOM), bf16), returned, scalar)
    return new_features, new_vectors


def solution(mesh):
    fine = Mesh(mesh.devices.reshape(2, 16, 2, 4, 2), all_axes)
    atoms = P(None, all_axes)
    placed = (
        atoms, P(None, None, all_axes), atoms, atoms, atoms, P(), P(None, kb_axes),
        P(), P(), P(), P(), P(),
    )
    return jax.shard_map(
        shards,
        mesh=fine,
        in_specs=placed,
        out_specs=(atoms, P(None, None, all_axes)),
        check_vma=False,
    )
```

```python
import math

import jax
import jax.numpy as jnp
from jax import lax
from jax.experimental import pallas as pl
from jax.experimental.pallas import tpu as pltpu
from jax.sharding import Mesh
from jax.sharding import PartitionSpec as P

F = 64
NRBF = 20
NBR = 16
ATOM = 128
KDEV = 256
PLANE = 32
DEPTH = 16
SLABS = 512
KVEC = 8192
ATOMS = 65536
PACK = 80
HALO_ROWS = 272
GROUP = 8

plane_axes = ("yh", "yl", "x", "c")
kb_axes = ("yl", "x", "c")
all_axes = ("yh", "z", "yl", "x", "c")

side_length = 6.0
slab_depth = 6.0
radial_reach = 6.0
distance_floor = 1.0
norm_scale = 1.0 / math.sqrt(KVEC * ATOMS)

sine_terms = (4.44287959, -7.30781805, 3.59778873, -0.79123821)
cosine_terms = (1.41420408, -6.97764206, 5.71523839, -1.72834865)
whole_turns = 1.5 * 2.0**23

VMEM_LIMIT = 16 * 2**20


def dot(a, b, dims):
    return lax.dot_general(a, b, (dims, ((), ())), preferred_element_type=jnp.float32)


def polynomial(terms, u):
    value = terms[-1] * u + terms[-2]
    for term in terms[-3::-1]:
        value = value * u + term
    return value


def cosine_and_sine(turns):
    r = turns - ((turns + whole_turns) - whole_turns)
    u = r * r
    s = r * polynomial(sine_terms, u)
    c = polynomial(cosine_terms, u)
    return 1.0 - s * s, s * c


VM, SM, ANY = pltpu.VMEM, pltpu.SMEM, pl.ANY


def call(kernel, places, outs, *operands, scratch=()):
    return pl.pallas_call(
        kernel,
        out_shape=outs,
        in_specs=[pl.BlockSpec(memory_space=place) for place in places],
        out_specs=jax.tree.map(lambda _: pl.BlockSpec(memory_space=VM), outs),
        scratch_shapes=list(scratch),
        compiler_params=pltpu.CompilerParams(vmem_limit_bytes=VMEM_LIMIT),
        cost_estimate=pl.CostEstimate(flops=0, bytes_accessed=0, transcendentals=0),
    )(*operands)


def packed_rows(feat, pos):
    placed = [jnp.pad(pos, ((at, PACK - at - 3), (0, 0))) for at in (F, F + 3, F + 6)]
    firsts = [lax.reduce_precision(value, 8, 7) for value in placed]
    seconds = [lax.reduce_precision(value - first, 8, 7) for value, first in zip(placed[1:], firsts[1:])]
    pieces = firsts[0] + seconds[0] + ((placed[2] - firsts[2]) - seconds[1])
    return jnp.pad(feat, ((0, PACK - F), (0, 0))) + pieces.astype(jnp.bfloat16)


def summed(pieces):
    return pieces[0:3] + pieces[3:6] + pieces[6:9]


def halo_kernel(packed, vec, halo, up, down):
    rows = jnp.concatenate([packed[...], vec[0], vec[1], vec[2]], axis=0)
    atom = lax.broadcasted_iota(jnp.int32, (ATOM, ATOM), 0)
    for side, out in ((0, up), (1, down)):
        chosen = jnp.where(atom == halo[side : side + 1, :], 1.0, 0.0).astype(jnp.bfloat16)
        out[...] = dot(rows, chosen, ((1,), (0,))).astype(jnp.bfloat16)


def table_kernel(got, lattice, below, above, own_filter, table, partial, columns, total):
    turned = lattice[...].T
    for i in range(3):
        columns[i] = jnp.broadcast_to(turned[:, i : i + 1], (KDEV, ATOM))
    total[...] = jnp.zeros_like(total)

    @pl.loop(0, PLANE // GROUP)
    def _(step):
        for pair in range(0, GROUP, 2):
            first = step * GROUP + pair
            both = jnp.concatenate([got[first], got[first + 1]], axis=1)
            pos = summed(both[F:].astype(jnp.float32))
            at = pl.ds(pl.multiple_of(first * ATOM, 2 * ATOM), 2 * ATOM)
            for k in range(0, KDEV, 64):
                rows = slice(k, k + 64)
                halves = []
                for lanes in (slice(0, ATOM), slice(ATOM, 2 * ATOM)):
                    halves.append(
                        (columns[0, rows] * pos[0:1, lanes] + columns[1, rows] * pos[1:2, lanes])
                        + columns[2, rows] * pos[2:3, lanes]
                    )
                cosines, sines = cosine_and_sine(jnp.concatenate(halves, axis=1))
                cosines, sines = cosines.astype(jnp.bfloat16), sines.astype(jnp.bfloat16)
                table[k : k + 64, at] = cosines
                table[KDEV + k : KDEV + k + 64, at] = sines
                sums = dot(jnp.concatenate([cosines, sines], axis=0), both[:F], ((1,), (1,)))
                total[k : k + 64] += sums[:64]
                total[KDEV + k : KDEV + k + 64] += sums[64:]

    partial[...] = jnp.concatenate([total[:KDEV], total[KDEV:]], axis=1).astype(jnp.bfloat16)


def sum_kernel(arrived, out):
    total = arrived[0].astype(jnp.float32)
    for i in range(1, DEPTH):
        total = total + arrived[i].astype(jnp.float32)
    total = total.astype(jnp.bfloat16)
    for i in range(DEPTH):
        out[i] = total


def project_kernel(got, own_filter, table, out):
    own, weight = own_filter[:, :KDEV], own_filter[:, KDEV:].astype(jnp.bfloat16)
    total = [dot(weight, got[:, part * F : (part + 1) * F], ((0,), (1,))) for part in range(2)]
    filtered = jnp.concatenate([own * total[0], own * total[1]], axis=1).astype(jnp.bfloat16)
    for first in range(0, PLANE, 8):
        message = dot(filtered, table[:, first * ATOM : (first + 8) * ATOM], ((1,), (0,))).astype(jnp.bfloat16)
        for p in range(8):
            out[first + p] = message[:, p * ATOM : (p + 1) * ATOM]


def finish_kernel(arrived, scalar, out):
    total = arrived[0].astype(jnp.float32)
    for i in range(1, PLANE):
        total = total + arrived[i].astype(jnp.float32)
    out[...] = (scalar[...] + total).astype(jnp.bfloat16)


def short_kernel(
    packed, vec, ids, below, above, node_weight, bias, message_weight, radial_weight, messages,
    scalar_out, vector_out, ext, chosen, filters, directions,
):
    pos = summed(packed[F:].astype(jnp.float32))
    ext[192:384, :ATOM] = jnp.concatenate([vec[0], vec[1], vec[2]], axis=0)
    ext[384:, :ATOM] = packed[F:]
    for side, at in ((below, ATOM), (above, 2 * ATOM)):
        ext[192:384, at : at + ATOM] = side[PACK:]
        ext[384:, at : at + ATOM] = side[F:PACK]
    ext_feat = jnp.concatenate([packed[:F], below[:F], above[:F]], axis=1)
    bias_column = jnp.broadcast_to(bias[...], (8, F)).T[:, 0:1]
    hidden = dot(node_weight[...], ext_feat, ((0,), (0,))) + bias_column
    hidden = (hidden / (1.0 + jnp.exp(-hidden))).astype(jnp.bfloat16)
    ext[:192] = dot(message_weight[...], hidden, ((0,), (0,))).astype(jnp.bfloat16)

    number = lax.broadcasted_iota(jnp.int32, (3 * ATOM, ATOM), 0)
    for j in range(NBR):
        chosen[:, j * ATOM : (j + 1) * ATOM] = jnp.where(number == ids[j : j + 1, :], 1.0, 0.0).astype(jnp.bfloat16)
    found = dot(ext[384:], chosen[...], ((1,), (0,)))
    offset = summed(found) - jnp.concatenate([pos] * NBR, axis=1)
    offset = offset - jnp.floor(offset + 0.5)
    side = lax.broadcasted_iota(jnp.int32, (3, 1), 0)
    box = jnp.where(side == 2, slab_depth * SLABS, side_length).astype(jnp.float32)
    cartesian = offset * box
    square = cartesian * cartesian
    distance = jnp.sqrt(square[0:1] + square[1:2] + square[2:3])
    directions[0:3] = cartesian / jnp.maximum(distance, distance_floor)
    center = lax.broadcasted_iota(jnp.int32, (NRBF, 1), 0).astype(jnp.float32) * (radial_reach / (NRBF - 1))
    away = (distance - center) / (1.5 * radial_reach / NRBF)
    radial = jnp.exp(-(away * away)).astype(jnp.bfloat16)
    filters[...] = dot(radial_weight[...], radial, ((0,), (0,)))

    def slots(step, sums):
        at = pl.ds(pl.multiple_of(step * 2 * ATOM, 2 * ATOM), 2 * ATOM)
        picked = dot(ext[:384], chosen[:, at], ((1,), (0,)))
        terms = picked[:192] * filters[:, at]
        toward = directions[:, at]
        parts = [terms[:F]]
        for x in range(3):
            parts.append(
                picked[192 + x * F : 192 + (x + 1) * F] * terms[F : 2 * F] + terms[2 * F :] * toward[x : x + 1]
            )
        return tuple(s + p[:, :ATOM] + p[:, ATOM:] for s, p in zip(sums, parts))

    zero = jnp.zeros((F, ATOM), jnp.float32)
    sums = lax.fori_loop(0, NBR // 2, slots, (zero,) * 4)
    scalar_out[...] = packed[:F].astype(jnp.float32) + sums[0]
    for x in range(3):
        vector_out[x] = (vec[x].astype(jnp.float32) + sums[1 + x]).astype(jnp.bfloat16)


def exchanged(x, axes):
    return lax.all_to_all(x, axes, split_axis=0, concat_axis=0, tiled=True)


def shifted(x, steps):
    return lax.ppermute(x, all_axes, [(i, (i + steps) % SLABS) for i in range(SLABS)])


def shards(
    features, vectors, positions, neighbours, halo_lists, lattice, kspace_filter,
    node_weight, node_bias, message_weight, radial_weight, ewald_weight,
):
    bf16, f32 = jnp.bfloat16, jnp.float32
    shape = jax.ShapeDtypeStruct
    half_at = lax.axis_index("yh") * KDEV
    k_at = lax.axis_index(kb_axes) * 2 * KDEV + half_at
    packed = packed_rows(features, positions)
    got = exchanged(jnp.broadcast_to(packed, (PLANE, PACK, ATOM)), plane_axes)
    own_lattice = jnp.pad(lax.dynamic_slice_in_dim(lattice, k_at, KDEV, 1).astype(f32), ((0, 5), (0, 0)))
    own_filter = jnp.pad(lax.dynamic_slice_in_dim(kspace_filter, half_at, KDEV, 1) * norm_scale, ((0, 0), (0, F)))
    own_filter = own_filter + jnp.pad(ewald_weight.astype(f32), ((0, 0), (KDEV, 0)))
    halo = shape((HALO_ROWS, ATOM), bf16)
    up, down = call(halo_kernel, [VM] * 3, (halo, halo), packed, vectors, halo_lists)
    below, above = shifted(up, 1), shifted(down, -1)
    table, partial = call(
        table_kernel,
        [VM, VM, ANY, ANY, ANY],
        (shape((2 * KDEV, PLANE * ATOM), bf16), shape((KDEV, 2 * F), bf16)),
        got, own_lattice, below, above, own_filter,
        scratch=[VM((3, KDEV, ATOM), f32), VM((2 * KDEV, F), f32)],
    )
    arrived = exchanged(partial.reshape(DEPTH, KDEV // DEPTH, 2 * F), "z")
    owned = call(sum_kernel, [VM], shape((DEPTH, KDEV // DEPTH, 2 * F), bf16), arrived)
    totals = exchanged(owned, "z").reshape(KDEV, 2 * F)
    messages = call(
        project_kernel, [VM] * 3, shape((PLANE, F, ATOM), bf16), totals, own_filter, table
    )
    returned = exchanged(messages, plane_axes)
    scalar, new_vectors = call(
        short_kernel,
        [VM] * 9 + [ANY],
        (shape((F, ATOM), f32), shape((3, F, ATOM), bf16)),
        packed, vectors, neighbours, below, above,
        node_weight, node_bias.reshape(1, F), message_weight, radial_weight, messages,
        scratch=[
            VM((400, 3 * ATOM), bf16),
            VM((3 * ATOM, NBR * ATOM), bf16),
            VM((192, NBR * ATOM), f32),
            VM((8, NBR * ATOM), f32),
        ],
    )
    new_features = call(finish_kernel, [VM] * 2, shape((F, ATOM), bf16), returned, scalar)
    return new_features, new_vectors


def solution(mesh):
    fine = Mesh(mesh.devices.reshape(2, 16, 2, 4, 2), all_axes)
    atoms = P(None, all_axes)
    placed = (
        atoms, P(None, None, all_axes), atoms, atoms, atoms, P(), P(None, kb_axes),
        P(), P(), P(), P(), P(),
    )
    return jax.shard_map(
        shards,
        mesh=fine,
        in_specs=placed,
        out_specs=(atoms, P(None, None, all_axes)),
        check_vma=False,
    )
```

```python
import math

import jax
import jax.numpy as jnp
from jax import lax
from jax.experimental import pallas as pl
from jax.experimental.pallas import tpu as pltpu
from jax.sharding import Mesh
from jax.sharding import PartitionSpec as P

F = 64
NRBF = 20
NBR = 16
ATOM = 128
KDEV = 256
PLANE = 32
DEPTH = 16
SLABS = 512
KVEC = 8192
ATOMS = 65536
PACK = 80
HALO_ROWS = 272
GROUP = 8

plane_axes = ("yh", "yl", "x", "c")
kb_axes = ("yl", "x", "c")
all_axes = ("yh", "z", "yl", "x", "c")

side_length = 6.0
slab_depth = 6.0
radial_reach = 6.0
distance_floor = 1.0
norm_scale = 1.0 / math.sqrt(KVEC * ATOMS)

sine_terms = (4.44287959, -7.30781805, 3.59778873, -0.79123821)
cosine_terms = (1.41420408, -6.97764206, 5.71523839, -1.72834865)
whole_turns = 1.5 * 2.0**23

VMEM_LIMIT = 16 * 2**20


def dot(a, b, dims):
    return lax.dot_general(a, b, (dims, ((), ())), preferred_element_type=jnp.float32)


def polynomial(terms, u):
    value = terms[-1] * u + terms[-2]
    for term in terms[-3::-1]:
        value = value * u + term
    return value


def cosine_and_sine(turns):
    r = turns - ((turns + whole_turns) - whole_turns)
    u = r * r
    s = r * polynomial(sine_terms, u)
    c = polynomial(cosine_terms, u)
    return 1.0 - s * s, s * c


VM, SM, ANY = pltpu.VMEM, pltpu.SMEM, pl.ANY


def call(kernel, places, outs, *operands, scratch=()):
    return pl.pallas_call(
        kernel,
        out_shape=outs,
        in_specs=[pl.BlockSpec(memory_space=place) for place in places],
        out_specs=jax.tree.map(lambda _: pl.BlockSpec(memory_space=VM), outs),
        scratch_shapes=list(scratch),
        compiler_params=pltpu.CompilerParams(vmem_limit_bytes=VMEM_LIMIT),
        cost_estimate=pl.CostEstimate(flops=0, bytes_accessed=0, transcendentals=0),
    )(*operands)


def packed_rows(feat, pos):
    placed = [jnp.pad(pos, ((at, PACK - at - 3), (0, 0))) for at in (F, F + 3, F + 6)]
    firsts = [lax.reduce_precision(value, 8, 7) for value in placed]
    seconds = [lax.reduce_precision(value - first, 8, 7) for value, first in zip(placed[1:], firsts[1:])]
    pieces = firsts[0] + seconds[0] + ((placed[2] - firsts[2]) - seconds[1])
    return jnp.pad(feat, ((0, PACK - F), (0, 0))) + pieces.astype(jnp.bfloat16)


def summed(pieces):
    return pieces[0:3] + pieces[3:6] + pieces[6:9]


def halo_kernel(row, packed, vec, halo, after, out):
    rows = jnp.concatenate([packed[...], vec[0], vec[1], vec[2]], axis=0)
    atom = lax.broadcasted_iota(jnp.int32, (ATOM, ATOM), 0)
    chosen = jnp.where(atom == halo[pl.ds(row[0], 1), :], 1.0, 0.0).astype(jnp.bfloat16)
    out[...] = dot(rows, chosen, ((1,), (0,))).astype(jnp.bfloat16)


def table_kernel(got, lattice, far, own_filter, table, partial, columns, total):
    turned = lattice[...].T
    for i in range(3):
        columns[i] = jnp.broadcast_to(turned[:, i : i + 1], (KDEV, ATOM))
    total[...] = jnp.zeros_like(total)

    @pl.loop(0, PLANE // GROUP)
    def _(step):
        for pair in range(0, GROUP, 2):
            first = step * GROUP + pair
            both = jnp.concatenate([got[first], got[first + 1]], axis=1)
            pos = summed(both[F:].astype(jnp.float32))
            at = pl.ds(pl.multiple_of(first * ATOM, 2 * ATOM), 2 * ATOM)
            for k in range(0, KDEV, 64):
                rows = slice(k, k + 64)
                halves = []
                for lanes in (slice(0, ATOM), slice(ATOM, 2 * ATOM)):
                    halves.append(
                        (columns[0, rows] * pos[0:1, lanes] + columns[1, rows] * pos[1:2, lanes])
                        + columns[2, rows] * pos[2:3, lanes]
                    )
                cosines, sines = cosine_and_sine(jnp.concatenate(halves, axis=1))
                cosines, sines = cosines.astype(jnp.bfloat16), sines.astype(jnp.bfloat16)
                table[k : k + 64, at] = cosines
                table[KDEV + k : KDEV + k + 64, at] = sines
                sums = dot(jnp.concatenate([cosines, sines], axis=0), both[:F], ((1,), (1,)))
                total[k : k + 64] += sums[:64]
                total[KDEV + k : KDEV + k + 64] += sums[64:]

    partial[...] = jnp.concatenate([total[:KDEV], total[KDEV:]], axis=1).astype(jnp.bfloat16)


def sum_kernel(arrived, out):
    total = arrived[0].astype(jnp.float32)
    for i in range(1, DEPTH):
        total = total + arrived[i].astype(jnp.float32)
    total = total.astype(jnp.bfloat16)
    for i in range(DEPTH):
        out[i] = total


def project_kernel(got, own_filter, table, out):
    own, weight = own_filter[:, :KDEV], own_filter[:, KDEV:].astype(jnp.bfloat16)
    total = [dot(weight, got[:, part * F : (part + 1) * F], ((0,), (1,))) for part in range(2)]
    filtered = jnp.concatenate([own * total[0], own * total[1]], axis=1).astype(jnp.bfloat16)
    for first in range(0, PLANE, 8):
        message = dot(filtered, table[:, first * ATOM : (first + 8) * ATOM], ((1,), (0,))).astype(jnp.bfloat16)
        for p in range(8):
            out[first + p] = message[:, p * ATOM : (p + 1) * ATOM]


def finish_kernel(arrived, scalar, out):
    total = arrived[0].astype(jnp.float32)
    for i in range(1, PLANE):
        total = total + arrived[i].astype(jnp.float32)
    out[...] = (scalar[...] + total).astype(jnp.bfloat16)


def short_kernel(
    core, packed, vec, ids, near, far, node_weight, bias, message_weight, radial_weight,
    scalar_out, vector_out, feats, ext, chosen, filters, directions,
):
    pos = summed(packed[F:].astype(jnp.float32))
    feats[:, :ATOM] = packed[:F]
    ext[192:384, :ATOM] = jnp.concatenate([vec[0], vec[1], vec[2]], axis=0)
    ext[384:, :ATOM] = packed[F:]
    near_at = pl.ds(pl.multiple_of((2 - core[0]) * ATOM, ATOM), ATOM)
    far_at = pl.ds(pl.multiple_of((1 + core[0]) * ATOM, ATOM), ATOM)
    for side, at in ((near, near_at), (far, far_at)):
        feats[:, at] = side[:F]
        ext[192:384, at] = side[PACK:]
        ext[384:, at] = side[F:PACK]
    bias_column = jnp.broadcast_to(bias[...], (8, F)).T[:, 0:1]
    hidden = dot(node_weight[...], feats[...], ((0,), (0,))) + bias_column
    hidden = (hidden / (1.0 + jnp.exp(-hidden))).astype(jnp.bfloat16)
    ext[:192] = dot(message_weight[...], hidden, ((0,), (0,))).astype(jnp.bfloat16)

    number = lax.broadcasted_iota(jnp.int32, (3 * ATOM, ATOM), 0)
    for j in range(NBR):
        chosen[:, j * ATOM : (j + 1) * ATOM] = jnp.where(number == ids[j : j + 1, :], 1.0, 0.0).astype(jnp.bfloat16)
    found = dot(ext[384:], chosen[...], ((1,), (0,)))
    offset = summed(found) - jnp.concatenate([pos] * NBR, axis=1)
    offset = offset - jnp.floor(offset + 0.5)
    side = lax.broadcasted_iota(jnp.int32, (3, 1), 0)
    box = jnp.where(side == 2, slab_depth * SLABS, side_length).astype(jnp.float32)
    cartesian = offset * box
    square = cartesian * cartesian
    distance = jnp.sqrt(square[0:1] + square[1:2] + square[2:3])
    directions[0:3] = cartesian / jnp.maximum(distance, distance_floor)
    center = lax.broadcasted_iota(jnp.int32, (NRBF, 1), 0).astype(jnp.float32) * (radial_reach / (NRBF - 1))
    away = (distance - center) / (1.5 * radial_reach / NRBF)
    radial = jnp.exp(-(away * away)).astype(jnp.bfloat16)
    filters[...] = dot(radial_weight[...], radial, ((0,), (0,)))

    def slots(step, sums):
        at = pl.ds(pl.multiple_of(step * 2 * ATOM, 2 * ATOM), 2 * ATOM)
        picked = dot(ext[:384], chosen[:, at], ((1,), (0,)))
        terms = picked[:192] * filters[:, at]
        toward = directions[:, at]
        parts = [terms[:F]]
        for x in range(3):
            parts.append(
                picked[192 + x * F : 192 + (x + 1) * F] * terms[F : 2 * F] + terms[2 * F :] * toward[x : x + 1]
            )
        return tuple(s + p[:, :ATOM] + p[:, ATOM:] for s, p in zip(sums, parts))

    zero = jnp.zeros((F, ATOM), jnp.float32)
    sums = lax.fori_loop(0, NBR // 2, slots, (zero,) * 4)
    scalar_out[...] = packed[:F].astype(jnp.float32) + sums[0]
    for x in range(3):
        vector_out[x] = (vec[x].astype(jnp.float32) + sums[1 + x]).astype(jnp.bfloat16)


def exchanged(x, axes):
    return lax.all_to_all(x, axes, split_axis=0, concat_axis=0, tiled=True)


def swapped(x, first):
    pairs = [((first + i) % SLABS, (first + (i ^ 1)) % SLABS) for i in range(SLABS)]
    return lax.ppermute(x, all_axes, pairs)


def shards(
    features, vectors, positions, neighbours, halo_lists, lattice, kspace_filter,
    node_weight, node_bias, message_weight, radial_weight, ewald_weight,
):
    bf16, f32 = jnp.bfloat16, jnp.float32
    shape = jax.ShapeDtypeStruct
    half_at = lax.axis_index("yh") * KDEV
    k_at = lax.axis_index(kb_axes) * 2 * KDEV + half_at
    packed = packed_rows(features, positions)
    got = exchanged(jnp.broadcast_to(packed, (PLANE, PACK, ATOM)), plane_axes)
    own_lattice = jnp.pad(lax.dynamic_slice_in_dim(lattice, k_at, KDEV, 1).astype(f32), ((0, 5), (0, 0)))
    own_filter = jnp.pad(lax.dynamic_slice_in_dim(kspace_filter, half_at, KDEV, 1) * norm_scale, ((0, 0), (0, F)))
    own_filter = own_filter + jnp.pad(ewald_weight.astype(f32), ((0, 0), (KDEV, 0)))
    core = lax.axis_index("c").astype(jnp.int32).reshape(1)
    halo = shape((HALO_ROWS, ATOM), bf16)
    far = call(
        halo_kernel, [SM, VM, VM, VM, ANY], halo, 1 - core, packed, vectors, halo_lists, own_lattice
    )
    far = swapped(far, 1)
    table, partial = call(
        table_kernel,
        [VM, VM, ANY, ANY],
        (shape((2 * KDEV, PLANE * ATOM), bf16), shape((KDEV, 2 * F), bf16)),
        got, own_lattice, far, own_filter,
        scratch=[VM((3, KDEV, ATOM), f32), VM((2 * KDEV, F), f32)],
    )
    arrived = exchanged(partial.reshape(DEPTH, KDEV // DEPTH, 2 * F), "z")
    owned = call(sum_kernel, [VM], shape((DEPTH, KDEV // DEPTH, 2 * F), bf16), arrived)
    totals = exchanged(owned, "z").reshape(KDEV, 2 * F)
    messages = call(
        project_kernel, [VM] * 3, shape((PLANE, F, ATOM), bf16), totals, own_filter, table
    )
    returned = exchanged(messages, plane_axes)
    near = call(halo_kernel, [SM, VM, VM, VM, ANY], halo, core, packed, vectors, halo_lists, messages)
    near = swapped(near, 0)
    scalar, new_vectors = call(
        short_kernel,
        [SM] + [VM] * 9,
        (shape((F, ATOM), f32), shape((3, F, ATOM), bf16)),
        core, packed, vectors, neighbours, near, far,
        node_weight, node_bias.reshape(1, F), message_weight, radial_weight,
        scratch=[
            VM((F, 3 * ATOM), bf16),
            VM((400, 3 * ATOM), bf16),
            VM((3 * ATOM, NBR * ATOM), bf16),
            VM((192, NBR * ATOM), f32),
            VM((8, NBR * ATOM), f32),
        ],
    )
    new_features = call(finish_kernel, [VM] * 2, shape((F, ATOM), bf16), returned, scalar)
    return new_features, new_vectors


def solution(mesh):
    fine = Mesh(mesh.devices.reshape(2, 16, 2, 4, 2), all_axes)
    atoms = P(None, all_axes)
    placed = (
        atoms, P(None, None, all_axes), atoms, atoms, atoms, P(), P(None, kb_axes),
        P(), P(), P(), P(), P(),
    )
    return jax.shard_map(
        shards,
        mesh=fine,
        in_specs=placed,
        out_specs=(atoms, P(None, None, all_axes)),
        check_vma=False,
    )
```

```python
import math

import jax
import jax.numpy as jnp
from jax import lax
from jax.experimental import pallas as pl
from jax.experimental.pallas import tpu as pltpu
from jax.sharding import Mesh
from jax.sharding import PartitionSpec as P

F = 64
NRBF = 20
NBR = 16
ATOM = 128
KDEV = 256
PLANE = 32
DEPTH = 16
SLABS = 512
KVEC = 8192
ATOMS = 65536
PACK = 80
HALO_ROWS = 272
GROUP = 4
SPARE = 11

plane_axes = ("yh", "yl", "x", "c")
kb_axes = ("yl", "x", "c")
all_axes = ("yh", "z", "yl", "x", "c")

side_length = 6.0
slab_depth = 6.0
radial_reach = 6.0
distance_floor = 1.0
norm_scale = 1.0 / math.sqrt(KVEC * ATOMS)

sine_terms = (4.44287959, -7.30781805, 3.59778873, -0.79123821)
cosine_terms = (1.41420408, -6.97764206, 5.71523839, -1.72834865)
whole_turns = 1.5 * 2.0**23

VMEM_LIMIT = 16 * 2**20


def dot(a, b, dims):
    return lax.dot_general(a, b, (dims, ((), ())), preferred_element_type=jnp.float32)


def polynomial(terms, u):
    value = terms[-1] * u + terms[-2]
    for term in terms[-3::-1]:
        value = value * u + term
    return value


def cosine_and_sine(turns):
    r = turns - ((turns + whole_turns) - whole_turns)
    u = r * r
    s = r * polynomial(sine_terms, u)
    c = polynomial(cosine_terms, u)
    return 1.0 - s * s, s * c


VM, SM, ANY = pltpu.VMEM, pltpu.SMEM, pl.ANY


def call(kernel, places, outs, *operands, scratch=(), kept=None, far_outs=()):
    return pl.pallas_call(
        kernel,
        out_shape=outs,
        in_specs=[pl.BlockSpec(memory_space=place) for place in places],
        out_specs=jax.tree.map(lambda _: pl.BlockSpec(memory_space=VM), outs)
        if kept is None
        else [pl.BlockSpec(memory_space=ANY if i in far_outs else VM) for i in range(len(outs))],
        input_output_aliases=kept or {},
        scratch_shapes=list(scratch),
        compiler_params=pltpu.CompilerParams(vmem_limit_bytes=VMEM_LIMIT),
        cost_estimate=pl.CostEstimate(flops=0, bytes_accessed=0, transcendentals=0),
    )(*operands)


def packed_rows(feat, pos):
    placed = [jnp.pad(pos, ((at, PACK - at - 3), (0, 0))) for at in (F, F + 3, F + 6)]
    firsts = [lax.reduce_precision(value, 8, 7) for value in placed]
    seconds = [lax.reduce_precision(value - first, 8, 7) for value, first in zip(placed[1:], firsts[1:])]
    pieces = firsts[0] + seconds[0] + ((placed[2] - firsts[2]) - seconds[1])
    return jnp.pad(feat, ((0, PACK - F), (0, 0))) + pieces.astype(jnp.bfloat16)


def summed(pieces):
    return pieces[0:3] + pieces[3:6] + pieces[6:9]


def halo_kernel(core, packed, vec, halo, far, near):
    rows = jnp.concatenate([packed[...], vec[0], vec[1], vec[2]], axis=0)
    atom = lax.broadcasted_iota(jnp.int32, (ATOM, ATOM), 0)
    for row, out in ((1 - core[0], far), (core[0], near)):
        chosen = jnp.where(atom == halo[pl.ds(row, 1), :], 1.0, 0.0).astype(jnp.bfloat16)
        out[...] = dot(rows, chosen, ((1,), (0,))).astype(jnp.bfloat16)


def table_kernel(got, lattice, far, own_filter, table_at, partial, far_kept, table, columns, total, done):
    turned = lattice[...].T
    for i in range(3):
        columns[i] = jnp.broadcast_to(turned[:, i : i + 1], (KDEV, ATOM))
    total[...] = jnp.zeros_like(total)

    def stored(step):
        atoms = pl.ds(pl.multiple_of(step * GROUP * ATOM, GROUP * ATOM), GROUP * ATOM)
        return pltpu.make_async_copy(table.at[:, atoms], table_at.at[0, :, atoms], done.at[step])

    @pl.loop(0, PLANE // GROUP)
    def _(step):
        for pair in range(0, GROUP, 2):
            first = step * GROUP + pair
            both = jnp.concatenate([got[first], got[first + 1]], axis=1)
            pos = summed(both[F:].astype(jnp.float32))
            at = pl.ds(pl.multiple_of(first * ATOM, 2 * ATOM), 2 * ATOM)
            for k in range(0, KDEV, 64):
                rows = slice(k, k + 64)
                halves = []
                for lanes in (slice(0, ATOM), slice(ATOM, 2 * ATOM)):
                    halves.append(
                        (columns[0, rows] * pos[0:1, lanes] + columns[1, rows] * pos[1:2, lanes])
                        + columns[2, rows] * pos[2:3, lanes]
                    )
                cosines, sines = cosine_and_sine(jnp.concatenate(halves, axis=1))
                cosines, sines = cosines.astype(jnp.bfloat16), sines.astype(jnp.bfloat16)
                table[k : k + 64, at] = cosines
                table[KDEV + k : KDEV + k + 64, at] = sines
                sums = dot(jnp.concatenate([cosines, sines], axis=0), both[:F], ((1,), (1,)))
                total[k : k + 64] += sums[:64]
                total[KDEV + k : KDEV + k + 64] += sums[64:]
        stored(step).start()

    partial[...] = jnp.concatenate([total[:KDEV], total[KDEV:]], axis=1).astype(jnp.bfloat16)
    for step in range(PLANE // GROUP):
        stored(step).wait()


def sum_kernel(arrived, near, out, near_kept):
    total = arrived[0].astype(jnp.float32)
    for i in range(1, DEPTH):
        total = total + arrived[i].astype(jnp.float32)
    total = total.astype(jnp.bfloat16)
    for i in range(DEPTH):
        out[i] = total


def project_kernel(got, own_filter, table_at, near, out, table, done):
    parts = ((0, 4), (4, 12), (12, 20), (20, 28), (28, 32))
    loads = []
    for i, (first, last) in enumerate(parts):
        atoms = slice(first * ATOM, last * ATOM)
        loads.append(pltpu.make_async_copy(table_at.at[0, :, atoms], table.at[:, atoms], done.at[i]))
    for load in loads:
        load.start()
    own, weight = own_filter[:, :KDEV], own_filter[:, KDEV:].astype(jnp.bfloat16)
    total = [dot(weight, got[:, part * F : (part + 1) * F], ((0,), (1,))) for part in range(2)]
    filtered = jnp.concatenate([own * total[0], own * total[1]], axis=1).astype(jnp.bfloat16)
    for (first, last), load in zip(parts, loads):
        load.wait()
        message = dot(filtered, table[:, first * ATOM : last * ATOM], ((1,), (0,))).astype(jnp.bfloat16)
        for p in range(last - first):
            out[first + p] = message[:, p * ATOM : (p + 1) * ATOM]


def finish_kernel(arrived, scalar, out):
    total = arrived[0].astype(jnp.float32)
    for i in range(1, PLANE):
        total = total + arrived[i].astype(jnp.float32)
    out[...] = (scalar[...] + total).astype(jnp.bfloat16)


def short_kernel(
    core, packed, vec, ids, near, far, node_weight, bias, message_weight, radial_weight, messages,
    scalar_out, vector_out, feats, ext, chosen, filters, directions,
):
    pos = summed(packed[F:].astype(jnp.float32))
    feats[:, :ATOM] = packed[:F]
    ext[192:384, :ATOM] = jnp.concatenate([vec[0], vec[1], vec[2]], axis=0)
    ext[384:, :ATOM] = packed[F:]
    near_at = pl.ds(pl.multiple_of((2 - core[0]) * ATOM, ATOM), ATOM)
    far_at = pl.ds(pl.multiple_of((1 + core[0]) * ATOM, ATOM), ATOM)
    for side, at in ((near, near_at), (far, far_at)):
        feats[:, at] = side[:F]
        ext[192:384, at] = side[PACK:]
        ext[384:, at] = side[F:PACK]
    bias_column = jnp.broadcast_to(bias[...], (8, F)).T[:, 0:1]
    hidden = dot(node_weight[...], feats[...], ((0,), (0,))) + bias_column
    hidden = (hidden / (1.0 + jnp.exp(-hidden))).astype(jnp.bfloat16)
    ext[:192] = dot(message_weight[...], hidden, ((0,), (0,))).astype(jnp.bfloat16)

    number = lax.broadcasted_iota(jnp.int32, (3 * ATOM, ATOM), 0)
    for j in range(NBR):
        chosen[:, j * ATOM : (j + 1) * ATOM] = jnp.where(number == ids[j : j + 1, :], 1.0, 0.0).astype(jnp.bfloat16)
    found = dot(ext[384:], chosen[...], ((1,), (0,)))
    offset = summed(found) - jnp.concatenate([pos] * NBR, axis=1)
    offset = offset - jnp.floor(offset + 0.5)
    side = lax.broadcasted_iota(jnp.int32, (3, 1), 0)
    box = jnp.where(side == 2, slab_depth * SLABS, side_length).astype(jnp.float32)
    cartesian = offset * box
    square = cartesian * cartesian
    distance = jnp.sqrt(square[0:1] + square[1:2] + square[2:3])
    directions[0:3] = cartesian / jnp.maximum(distance, distance_floor)
    center = lax.broadcasted_iota(jnp.int32, (NRBF, 1), 0).astype(jnp.float32) * (radial_reach / (NRBF - 1))
    away = (distance - center) / (1.5 * radial_reach / NRBF)
    radial = jnp.exp(-(away * away)).astype(jnp.bfloat16)
    filters[...] = dot(radial_weight[...], radial, ((0,), (0,)))

    def slots(step, sums):
        at = pl.ds(pl.multiple_of(step * 2 * ATOM, 2 * ATOM), 2 * ATOM)
        picked = dot(ext[:384], chosen[:, at], ((1,), (0,)))
        terms = picked[:192] * filters[:, at]
        toward = directions[:, at]
        parts = [terms[:F]]
        for x in range(3):
            parts.append(
                picked[192 + x * F : 192 + (x + 1) * F] * terms[F : 2 * F] + terms[2 * F :] * toward[x : x + 1]
            )
        return tuple(s + p[:, :ATOM] + p[:, ATOM:] for s, p in zip(sums, parts))

    zero = jnp.zeros((F, ATOM), jnp.float32)
    sums = lax.fori_loop(0, NBR // 2, slots, (zero,) * 4)
    scalar_out[...] = packed[:F].astype(jnp.float32) + sums[0]
    for x in range(3):
        vector_out[x] = (vec[x].astype(jnp.float32) + sums[1 + x]).astype(jnp.bfloat16)


def exchanged(x, axes):
    return lax.all_to_all(x, axes, split_axis=0, concat_axis=0, tiled=True)


def swapped(x, first):
    pairs = [((first + i) % SLABS, (first + (i ^ 1)) % SLABS) for i in range(SLABS)]
    return lax.ppermute(x, all_axes, pairs)


def shards(
    features, vectors, positions, neighbours, halo_lists, lattice, kspace_filter,
    node_weight, node_bias, message_weight, radial_weight, ewald_weight,
):
    bf16, f32 = jnp.bfloat16, jnp.float32
    shape = jax.ShapeDtypeStruct
    half_at = lax.axis_index("yh") * KDEV
    k_at = lax.axis_index(kb_axes) * 2 * KDEV + half_at
    packed = packed_rows(features, positions)
    got = exchanged(jnp.broadcast_to(packed, (PLANE, PACK, ATOM)), plane_axes)
    own_lattice = jnp.pad(lax.dynamic_slice_in_dim(lattice, k_at, KDEV, 1).astype(f32), ((0, 5), (0, 0)))
    own_filter = jnp.pad(lax.dynamic_slice_in_dim(kspace_filter, half_at, KDEV, 1) * norm_scale, ((0, 0), (0, F)))
    own_filter = own_filter + jnp.pad(ewald_weight.astype(f32), ((0, 0), (KDEV, 0)))
    core = lax.axis_index("c").astype(jnp.int32).reshape(1)
    halo = shape((HALO_ROWS, ATOM), bf16)
    far, near = call(halo_kernel, [SM, VM, VM, VM], (halo, halo), core, packed, vectors, halo_lists)
    table, partial, far = call(
        table_kernel,
        [VM, VM, ANY, ANY],
        (shape((SPARE, 2 * KDEV, PLANE * ATOM), bf16), shape((KDEV, 2 * F), bf16), halo),
        got, own_lattice, far, own_filter,
        scratch=[
            VM((2 * KDEV, PLANE * ATOM), bf16),
            VM((3, KDEV, ATOM), f32),
            VM((2 * KDEV, F), f32),
            pltpu.SemaphoreType.DMA((PLANE // GROUP,)),
        ],
        kept={2: 2},
        far_outs=(0, 2),
    )
    arrived = exchanged(partial.reshape(DEPTH, KDEV // DEPTH, 2 * F), "z")
    far = swapped(far, 1)
    owned, near = call(
        sum_kernel,
        [VM, ANY],
        (shape((DEPTH, KDEV // DEPTH, 2 * F), bf16), halo),
        arrived, near,
        kept={1: 1},
        far_outs=(1,),
    )
    near = swapped(near, 0)
    totals = exchanged(owned, "z").reshape(KDEV, 2 * F)
    messages = call(
        project_kernel,
        [VM, VM, ANY, ANY],
        shape((PLANE, F, ATOM), bf16),
        totals, own_filter, table, near,
        scratch=[VM((2 * KDEV, PLANE * ATOM), bf16), pltpu.SemaphoreType.DMA((5,))],
    )
    returned = exchanged(messages, plane_axes)
    scalar, new_vectors = call(
        short_kernel,
        [SM] + [VM] * 9 + [ANY],
        (shape((F, ATOM), f32), shape((3, F, ATOM), bf16)),
        core, packed, vectors, neighbours, near, far,
        node_weight, node_bias.reshape(1, F), message_weight, radial_weight, messages,
        scratch=[
            VM((F, 3 * ATOM), bf16),
            VM((400, 3 * ATOM), bf16),
            VM((3 * ATOM, NBR * ATOM), bf16),
            VM((192, NBR * ATOM), f32),
            VM((8, NBR * ATOM), f32),
        ],
    )
    new_features = call(finish_kernel, [VM] * 2, shape((F, ATOM), bf16), returned, scalar)
    return new_features, new_vectors


def solution(mesh):
    fine = Mesh(mesh.devices.reshape(2, 16, 2, 4, 2), all_axes)
    atoms = P(None, all_axes)
    placed = (
        atoms, P(None, None, all_axes), atoms, atoms, atoms, P(), P(None, kb_axes),
        P(), P(), P(), P(), P(),
    )
    return jax.shard_map(
        shards,
        mesh=fine,
        in_specs=placed,
        out_specs=(atoms, P(None, None, all_axes)),
        check_vma=False,
    )
```

```python
import math

import jax
import jax.numpy as jnp
from jax import lax
from jax.experimental import pallas as pl
from jax.experimental.pallas import tpu as pltpu
from jax.sharding import Mesh
from jax.sharding import PartitionSpec as P

F = 64
NRBF = 20
NBR = 16
ATOM = 128
KDEV = 256
PLANE = 32
SAME = 16
DEPTH = 16
SLABS = 512
KVEC = 8192
ATOMS = 65536
PACK = 80
HALO_ROWS = 272
GROUP = 8

same_axes = ("yh", "yl", "x")
kb_axes = ("yl", "x", "c")
all_axes = ("yh", "z", "yl", "x", "c")

side_length = 6.0
slab_depth = 6.0
radial_reach = 6.0
distance_floor = 1.0
norm_scale = 1.0 / math.sqrt(KVEC * ATOMS)

sine_terms = (4.44287959, -7.30781805, 3.59778873, -0.79123821)
cosine_terms = (1.41420408, -6.97764206, 5.71523839, -1.72834865)
whole_turns = 1.5 * 2.0**23

VMEM_LIMIT = 16 * 2**20


def dot(a, b, dims):
    return lax.dot_general(a, b, (dims, ((), ())), preferred_element_type=jnp.float32)


def polynomial(terms, u):
    value = terms[-1] * u + terms[-2]
    for term in terms[-3::-1]:
        value = value * u + term
    return value


def cosine_and_sine(turns):
    r = turns - ((turns + whole_turns) - whole_turns)
    u = r * r
    s = r * polynomial(sine_terms, u)
    c = polynomial(cosine_terms, u)
    return 1.0 - s * s, s * c


VM, SM, ANY = pltpu.VMEM, pltpu.SMEM, pl.ANY


def call(kernel, places, outs, *operands, scratch=()):
    return pl.pallas_call(
        kernel,
        out_shape=outs,
        in_specs=[pl.BlockSpec(memory_space=place) for place in places],
        out_specs=jax.tree.map(lambda _: pl.BlockSpec(memory_space=VM), outs),
        scratch_shapes=list(scratch),
        compiler_params=pltpu.CompilerParams(vmem_limit_bytes=VMEM_LIMIT),
        cost_estimate=pl.CostEstimate(flops=0, bytes_accessed=0, transcendentals=0),
    )(*operands)


def packed_rows(feat, pos):
    placed = [jnp.pad(pos, ((at, PACK - at - 3), (0, 0))) for at in (F, F + 3, F + 6)]
    firsts = [lax.reduce_precision(value, 8, 7) for value in placed]
    seconds = [lax.reduce_precision(value - first, 8, 7) for value, first in zip(placed[1:], firsts[1:])]
    pieces = firsts[0] + seconds[0] + ((placed[2] - firsts[2]) - seconds[1])
    return jnp.pad(feat, ((0, PACK - F), (0, 0))) + pieces.astype(jnp.bfloat16)


def summed(pieces):
    return pieces[0:3] + pieces[3:6] + pieces[6:9]


def halo_kernel(core, packed, vec, halo, far, near):
    rows = jnp.concatenate([packed[...], vec[0], vec[1], vec[2]], axis=0)
    atom = lax.broadcasted_iota(jnp.int32, (ATOM, ATOM), 0)
    for row, out in ((1 - core[0], far), (core[0], near)):
        chosen = jnp.where(atom == halo[pl.ds(row, 1), :], 1.0, 0.0).astype(jnp.bfloat16)
        out[...] = dot(rows, chosen, ((1,), (0,))).astype(jnp.bfloat16)


def table_kernel(own, other, lattice, far, own_filter, table, partial, columns, total):
    turned = lattice[...].T
    for i in range(3):
        columns[i] = jnp.broadcast_to(turned[:, i : i + 1], (KDEV, ATOM))
    total[...] = jnp.zeros_like(total)

    for part, got in enumerate((own, other)):

        @pl.loop(0, SAME // GROUP)
        def _(step):
            for pair in range(0, GROUP, 2):
                first = step * GROUP + pair
                both = jnp.concatenate([got[first], got[first + 1]], axis=1)
                pos = summed(both[F:].astype(jnp.float32))
                at = pl.ds(pl.multiple_of((part * SAME + first) * ATOM, 2 * ATOM), 2 * ATOM)
                for k in range(0, KDEV, 64):
                    rows = slice(k, k + 64)
                    halves = []
                    for lanes in (slice(0, ATOM), slice(ATOM, 2 * ATOM)):
                        halves.append(
                            (columns[0, rows] * pos[0:1, lanes] + columns[1, rows] * pos[1:2, lanes])
                            + columns[2, rows] * pos[2:3, lanes]
                        )
                    cosines, sines = cosine_and_sine(jnp.concatenate(halves, axis=1))
                    cosines, sines = cosines.astype(jnp.bfloat16), sines.astype(jnp.bfloat16)
                    table[k : k + 64, at] = cosines
                    table[KDEV + k : KDEV + k + 64, at] = sines
                    sums = dot(jnp.concatenate([cosines, sines], axis=0), both[:F], ((1,), (1,)))
                    total[k : k + 64] += sums[:64]
                    total[KDEV + k : KDEV + k + 64] += sums[64:]

    partial[...] = jnp.concatenate([total[:KDEV], total[KDEV:]], axis=1).astype(jnp.bfloat16)


def sum_kernel(arrived, out):
    total = arrived[0].astype(jnp.float32)
    for i in range(1, DEPTH):
        total = total + arrived[i].astype(jnp.float32)
    total = total.astype(jnp.bfloat16)
    for i in range(DEPTH):
        out[i] = total


def filtered_sums(got, own_filter):
    own, weight = own_filter[:, :KDEV], own_filter[:, KDEV:].astype(jnp.bfloat16)
    total = [dot(weight, got[:, part * F : (part + 1) * F], ((0,), (1,))) for part in range(2)]
    return jnp.concatenate([own * total[0], own * total[1]], axis=1).astype(jnp.bfloat16)


def project_other_kernel(got, own_filter, table, near, out):
    filtered = filtered_sums(got, own_filter)
    for first in range(0, SAME, 8):
        atoms = slice((SAME + first) * ATOM, (SAME + first + 8) * ATOM)
        message = dot(filtered, table[:, atoms], ((1,), (0,))).astype(jnp.bfloat16)
        for p in range(8):
            out[(first + p) * F : (first + p + 1) * F] = message[:, p * ATOM : (p + 1) * ATOM]
    out[SAME * F :] = near[...]


def project_own_kernel(got, own_filter, table, received, out):
    filtered = filtered_sums(got, own_filter)
    for first in range(0, SAME, 8):
        message = dot(filtered, table[:, first * ATOM : (first + 8) * ATOM], ((1,), (0,)))
        for p in range(first, first + 8):
            there = received[p * F : (p + 1) * F].astype(jnp.float32)
            out[p] = (message[:, (p - first) * ATOM : (p - first + 1) * ATOM] + there).astype(jnp.bfloat16)


def finish_kernel(arrived, scalar, out):
    total = arrived[0].astype(jnp.float32)
    for i in range(1, SAME):
        total = total + arrived[i].astype(jnp.float32)
    out[...] = (scalar[...] + total).astype(jnp.bfloat16)


def short_kernel(
    core, packed, vec, ids, near, far, node_weight, bias, message_weight, radial_weight, messages,
    scalar_out, vector_out, feats, ext, chosen, filters, directions,
):
    pos = summed(packed[F:].astype(jnp.float32))
    feats[:, :ATOM] = packed[:F]
    ext[192:384, :ATOM] = jnp.concatenate([vec[0], vec[1], vec[2]], axis=0)
    ext[384:, :ATOM] = packed[F:]
    near_at = pl.ds(pl.multiple_of((2 - core[0]) * ATOM, ATOM), ATOM)
    far_at = pl.ds(pl.multiple_of((1 + core[0]) * ATOM, ATOM), ATOM)
    for side, start, at in ((near, SAME * F, near_at), (far, 0, far_at)):
        feats[:, at] = side[start : start + F]
        ext[192:384, at] = side[start + PACK : start + HALO_ROWS]
        ext[384:, at] = side[start + F : start + PACK]
    bias_column = jnp.broadcast_to(bias[...], (8, F)).T[:, 0:1]
    hidden = dot(node_weight[...], feats[...], ((0,), (0,))) + bias_column
    hidden = (hidden / (1.0 + jnp.exp(-hidden))).astype(jnp.bfloat16)
    ext[:192] = dot(message_weight[...], hidden, ((0,), (0,))).astype(jnp.bfloat16)

    number = lax.broadcasted_iota(jnp.int32, (3 * ATOM, ATOM), 0)
    for j in range(NBR):
        chosen[:, j * ATOM : (j + 1) * ATOM] = jnp.where(number == ids[j : j + 1, :], 1.0, 0.0).astype(jnp.bfloat16)
    found = dot(ext[384:], chosen[...], ((1,), (0,)))
    offset = summed(found) - jnp.concatenate([pos] * NBR, axis=1)
    offset = offset - jnp.floor(offset + 0.5)
    side = lax.broadcasted_iota(jnp.int32, (3, 1), 0)
    box = jnp.where(side == 2, slab_depth * SLABS, side_length).astype(jnp.float32)
    cartesian = offset * box
    square = cartesian * cartesian
    distance = jnp.sqrt(square[0:1] + square[1:2] + square[2:3])
    directions[0:3] = cartesian / jnp.maximum(distance, distance_floor)
    center = lax.broadcasted_iota(jnp.int32, (NRBF, 1), 0).astype(jnp.float32) * (radial_reach / (NRBF - 1))
    away = (distance - center) / (1.5 * radial_reach / NRBF)
    radial = jnp.exp(-(away * away)).astype(jnp.bfloat16)
    filters[...] = dot(radial_weight[...], radial, ((0,), (0,)))

    def slots(step, sums):
        at = pl.ds(pl.multiple_of(step * 2 * ATOM, 2 * ATOM), 2 * ATOM)
        picked = dot(ext[:384], chosen[:, at], ((1,), (0,)))
        terms = picked[:192] * filters[:, at]
        toward = directions[:, at]
        parts = [terms[:F]]
        for x in range(3):
            parts.append(
                picked[192 + x * F : 192 + (x + 1) * F] * terms[F : 2 * F] + terms[2 * F :] * toward[x : x + 1]
            )
        return tuple(s + p[:, :ATOM] + p[:, ATOM:] for s, p in zip(sums, parts))

    zero = jnp.zeros((F, ATOM), jnp.float32)
    sums = lax.fori_loop(0, NBR // 2, slots, (zero,) * 4)
    scalar_out[...] = packed[:F].astype(jnp.float32) + sums[0]
    for x in range(3):
        vector_out[x] = (vec[x].astype(jnp.float32) + sums[1 + x]).astype(jnp.bfloat16)


def exchanged(x, axes):
    return lax.all_to_all(x, axes, split_axis=0, concat_axis=0, tiled=True)


def swapped(x, first):
    pairs = [((first + i) % SLABS, (first + (i ^ 1)) % SLABS) for i in range(SLABS)]
    return lax.ppermute(x, all_axes, pairs)


def shards(
    features, vectors, positions, neighbours, halo_lists, lattice, kspace_filter,
    node_weight, node_bias, message_weight, radial_weight, ewald_weight,
):
    bf16, f32 = jnp.bfloat16, jnp.float32
    shape = jax.ShapeDtypeStruct
    half_at = lax.axis_index("yh") * KDEV
    k_at = lax.axis_index(kb_axes) * 2 * KDEV + half_at
    packed = packed_rows(features, positions)
    own = exchanged(jnp.broadcast_to(packed, (SAME, PACK, ATOM)), same_axes)
    other = swapped(own, 0)
    own_lattice = jnp.pad(lax.dynamic_slice_in_dim(lattice, k_at, KDEV, 1).astype(f32), ((0, 5), (0, 0)))
    own_filter = jnp.pad(lax.dynamic_slice_in_dim(kspace_filter, half_at, KDEV, 1) * norm_scale, ((0, 0), (0, F)))
    own_filter = own_filter + jnp.pad(ewald_weight.astype(f32), ((0, 0), (KDEV, 0)))
    core = lax.axis_index("c").astype(jnp.int32).reshape(1)
    halo = shape((HALO_ROWS, ATOM), bf16)
    far, near = call(halo_kernel, [SM, VM, VM, VM], (halo, halo), core, packed, vectors, halo_lists)
    far = swapped(far, 1)
    table, partial = call(
        table_kernel,
        [VM, VM, VM, ANY, ANY],
        (shape((2 * KDEV, PLANE * ATOM), bf16), shape((KDEV, 2 * F), bf16)),
        own, other, own_lattice, far, own_filter,
        scratch=[VM((3, KDEV, ATOM), f32), VM((2 * KDEV, F), f32)],
    )
    arrived = exchanged(partial.reshape(DEPTH, KDEV // DEPTH, 2 * F), "z")
    owned = call(sum_kernel, [VM], shape((DEPTH, KDEV // DEPTH, 2 * F), bf16), arrived)
    totals = exchanged(owned, "z").reshape(KDEV, 2 * F)
    for_other = call(
        project_other_kernel,
        [VM] * 4,
        shape((SAME * F + HALO_ROWS, ATOM), bf16),
        totals, own_filter, table, near,
    )
    received = swapped(for_other, 0)
    messages = call(
        project_own_kernel, [VM] * 4, shape((SAME, F, ATOM), bf16), totals, own_filter, table, received
    )
    returned = exchanged(messages, same_axes)
    scalar, new_vectors = call(
        short_kernel,
        [SM] + [VM] * 9 + [ANY],
        (shape((F, ATOM), f32), shape((3, F, ATOM), bf16)),
        core, packed, vectors, neighbours, received, far,
        node_weight, node_bias.reshape(1, F), message_weight, radial_weight, messages,
        scratch=[
            VM((F, 3 * ATOM), bf16),
            VM((400, 3 * ATOM), bf16),
            VM((3 * ATOM, NBR * ATOM), bf16),
            VM((192, NBR * ATOM), f32),
            VM((8, NBR * ATOM), f32),
        ],
    )
    new_features = call(finish_kernel, [VM] * 2, shape((F, ATOM), bf16), returned, scalar)
    return new_features, new_vectors


def solution(mesh):
    fine = Mesh(mesh.devices.reshape(2, 16, 2, 4, 2), all_axes)
    atoms = P(None, all_axes)
    placed = (
        atoms, P(None, None, all_axes), atoms, atoms, atoms, P(), P(None, kb_axes),
        P(), P(), P(), P(), P(),
    )
    return jax.shard_map(
        shards,
        mesh=fine,
        in_specs=placed,
        out_specs=(atoms, P(None, None, all_axes)),
        check_vma=False,
    )
```

```python
import math

import jax
import jax.numpy as jnp
from jax import lax
from jax.experimental import pallas as pl
from jax.experimental.pallas import tpu as pltpu
from jax.sharding import Mesh
from jax.sharding import PartitionSpec as P

F = 64
NRBF = 20
NBR = 16
ATOM = 128
KDEV = 256
PLANE = 32
SAME = 16
DEPTH = 16
SLABS = 512
KVEC = 8192
ATOMS = 65536
PACK = 80
HALO_ROWS = 272
GROUP = 4
SPARE = 22

same_axes = ("yh", "yl", "x")
kb_axes = ("yl", "x", "c")
all_axes = ("yh", "z", "yl", "x", "c")

side_length = 6.0
slab_depth = 6.0
radial_reach = 6.0
distance_floor = 1.0
norm_scale = 1.0 / math.sqrt(KVEC * ATOMS)

sine_terms = (4.44287959, -7.30781805, 3.59778873, -0.79123821)
cosine_terms = (1.41420408, -6.97764206, 5.71523839, -1.72834865)
whole_turns = 1.5 * 2.0**23

VMEM_LIMIT = 16 * 2**20


def dot(a, b, dims):
    return lax.dot_general(a, b, (dims, ((), ())), preferred_element_type=jnp.float32)


def polynomial(terms, u):
    value = terms[-1] * u + terms[-2]
    for term in terms[-3::-1]:
        value = value * u + term
    return value


def cosine_and_sine(turns):
    r = turns - ((turns + whole_turns) - whole_turns)
    u = r * r
    s = r * polynomial(sine_terms, u)
    c = polynomial(cosine_terms, u)
    return 1.0 - s * s, s * c


VM, SM, ANY = pltpu.VMEM, pltpu.SMEM, pl.ANY


def call(kernel, places, outs, *operands, scratch=(), far_outs=(), flops=0):
    return pl.pallas_call(
        kernel,
        out_shape=outs,
        in_specs=[pl.BlockSpec(memory_space=place) for place in places],
        out_specs=tuple(pl.BlockSpec(memory_space=ANY if i in far_outs else VM) for i in range(len(outs)))
        if isinstance(outs, tuple)
        else pl.BlockSpec(memory_space=VM),
        scratch_shapes=list(scratch),
        compiler_params=pltpu.CompilerParams(vmem_limit_bytes=VMEM_LIMIT),
        cost_estimate=pl.CostEstimate(flops=flops, bytes_accessed=0, transcendentals=0),
    )(*operands)


def packed_rows(feat, pos):
    placed = [jnp.pad(pos, ((at, PACK - at - 3), (0, 0))) for at in (F, F + 3, F + 6)]
    firsts = [lax.reduce_precision(value, 8, 7) for value in placed]
    seconds = [lax.reduce_precision(value - first, 8, 7) for value, first in zip(placed[1:], firsts[1:])]
    pieces = firsts[0] + seconds[0] + ((placed[2] - firsts[2]) - seconds[1])
    return jnp.pad(feat, ((0, PACK - F), (0, 0))) + pieces.astype(jnp.bfloat16)


def summed(pieces):
    return pieces[0:3] + pieces[3:6] + pieces[6:9]


def halo_kernel(core, packed, vec, halo, after, far, near):
    rows = jnp.concatenate([packed[...], vec[0], vec[1], vec[2]], axis=0)
    atom = lax.broadcasted_iota(jnp.int32, (ATOM, ATOM), 0)
    for row, out in ((1 - core[0], far), (core[0], near)):
        chosen = jnp.where(atom == halo[pl.ds(row, 1), :], 1.0, 0.0).astype(jnp.bfloat16)
        out[...] = dot(rows, chosen, ((1,), (0,))).astype(jnp.bfloat16)


def make_columns(lattice, columns):
    turned = lattice[...].T
    for i in range(3):
        columns[i] = jnp.broadcast_to(turned[:, i : i + 1], (KDEV, ATOM))


def add_atoms(got, first, columns, table, total):
    for pair in range(0, GROUP, 2):
        both = jnp.concatenate([got[first + pair], got[first + pair + 1]], axis=1)
        pos = summed(both[F:].astype(jnp.float32))
        at = pl.ds(pl.multiple_of((first + pair) * ATOM, 2 * ATOM), 2 * ATOM)
        for k in range(0, KDEV, 64):
            rows = slice(k, k + 64)
            halves = []
            for lanes in (slice(0, ATOM), slice(ATOM, 2 * ATOM)):
                halves.append(
                    (columns[0, rows] * pos[0:1, lanes] + columns[1, rows] * pos[1:2, lanes])
                    + columns[2, rows] * pos[2:3, lanes]
                )
            cosines, sines = cosine_and_sine(jnp.concatenate(halves, axis=1))
            cosines, sines = cosines.astype(jnp.bfloat16), sines.astype(jnp.bfloat16)
            table[k : k + 64, at] = cosines
            table[KDEV + k : KDEV + k + 64, at] = sines
            sums = dot(jnp.concatenate([cosines, sines], axis=0), both[:F], ((1,), (1,)))
            total[k : k + 64] += sums[:64]
            total[KDEV + k : KDEV + k + 64] += sums[64:]


def own_table_kernel(got, lattice, own_filter, table_at, total, table, columns, done):
    make_columns(lattice, columns)
    total[...] = jnp.zeros_like(total)

    def stored(step):
        atoms = pl.ds(pl.multiple_of(step * GROUP * ATOM, GROUP * ATOM), GROUP * ATOM)
        return pltpu.make_async_copy(table.at[:, atoms], table_at.at[0, :, atoms], done.at[step])

    @pl.loop(0, SAME // GROUP)
    def _(step):
        add_atoms(got, step * GROUP, columns, table, total)
        stored(step).start()

    for step in range(SAME // GROUP):
        stored(step).wait()


def other_table_kernel(got, lattice, own_total, table, partial, columns, total):
    make_columns(lattice, columns)
    total[...] = own_total[...]

    @pl.loop(0, SAME // GROUP)
    def _(step):
        add_atoms(got, step * GROUP, columns, table, total)

    partial[...] = jnp.concatenate([total[:KDEV], total[KDEV:]], axis=1).astype(jnp.bfloat16)


def sum_kernel(arrived, far, out):
    total = arrived[0].astype(jnp.float32)
    for i in range(1, DEPTH):
        total = total + arrived[i].astype(jnp.float32)
    total = total.astype(jnp.bfloat16)
    for i in range(DEPTH):
        out[i] = total


def filtered_sums(got, own_filter):
    own, weight = own_filter[:, :KDEV], own_filter[:, KDEV:].astype(jnp.bfloat16)
    total = [dot(weight, got[:, part * F : (part + 1) * F], ((0,), (1,))) for part in range(2)]
    return jnp.concatenate([own * total[0], own * total[1]], axis=1).astype(jnp.bfloat16)


def project_other_kernel(got, own_filter, table, near, out):
    filtered = filtered_sums(got, own_filter)
    for first in range(0, SAME, 8):
        message = dot(filtered, table[:, first * ATOM : (first + 8) * ATOM], ((1,), (0,))).astype(jnp.bfloat16)
        for p in range(8):
            out[(first + p) * F : (first + p + 1) * F] = message[:, p * ATOM : (p + 1) * ATOM]
    out[SAME * F :] = near[...]


def project_own_kernel(got, own_filter, table_at, received, out, table, done):
    loads = []
    for i, first in enumerate(range(0, SAME, 4)):
        atoms = slice(first * ATOM, (first + 4) * ATOM)
        loads.append(pltpu.make_async_copy(table_at.at[0, :, atoms], table.at[:, atoms], done.at[i]))
    for load in loads:
        load.start()
    filtered = filtered_sums(got, own_filter)
    for first, load in zip(range(0, SAME, 4), loads):
        load.wait()
        message = dot(filtered, table[:, first * ATOM : (first + 4) * ATOM], ((1,), (0,)))
        for p in range(first, first + 4):
            there = received[p * F : (p + 1) * F].astype(jnp.float32)
            out[p] = (message[:, (p - first) * ATOM : (p - first + 1) * ATOM] + there).astype(jnp.bfloat16)


def finish_kernel(arrived, scalar, out):
    total = arrived[0].astype(jnp.float32)
    for i in range(1, SAME):
        total = total + arrived[i].astype(jnp.float32)
    out[...] = (scalar[...] + total).astype(jnp.bfloat16)


def short_kernel(
    core, packed, vec, ids, near, far, node_weight, bias, message_weight, radial_weight, messages,
    scalar_out, vector_out, feats, ext, chosen, filters, directions,
):
    pos = summed(packed[F:].astype(jnp.float32))
    feats[:, :ATOM] = packed[:F]
    ext[192:384, :ATOM] = jnp.concatenate([vec[0], vec[1], vec[2]], axis=0)
    ext[384:, :ATOM] = packed[F:]
    near_at = pl.ds(pl.multiple_of((2 - core[0]) * ATOM, ATOM), ATOM)
    far_at = pl.ds(pl.multiple_of((1 + core[0]) * ATOM, ATOM), ATOM)
    for side, start, at in ((near, SAME * F, near_at), (far, 0, far_at)):
        feats[:, at] = side[start : start + F]
        ext[192:384, at] = side[start + PACK : start + HALO_ROWS]
        ext[384:, at] = side[start + F : start + PACK]
    bias_column = jnp.broadcast_to(bias[...], (8, F)).T[:, 0:1]
    hidden = dot(node_weight[...], feats[...], ((0,), (0,))) + bias_column
    hidden = (hidden / (1.0 + jnp.exp(-hidden))).astype(jnp.bfloat16)
    ext[:192] = dot(message_weight[...], hidden, ((0,), (0,))).astype(jnp.bfloat16)

    number = lax.broadcasted_iota(jnp.int32, (3 * ATOM, ATOM), 0)
    for j in range(NBR):
        chosen[:, j * ATOM : (j + 1) * ATOM] = jnp.where(number == ids[j : j + 1, :], 1.0, 0.0).astype(jnp.bfloat16)
    found = dot(ext[384:], chosen[...], ((1,), (0,)))
    offset = summed(found) - jnp.concatenate([pos] * NBR, axis=1)
    offset = offset - jnp.floor(offset + 0.5)
    side = lax.broadcasted_iota(jnp.int32, (3, 1), 0)
    box = jnp.where(side == 2, slab_depth * SLABS, side_length).astype(jnp.float32)
    cartesian = offset * box
    square = cartesian * cartesian
    distance = jnp.sqrt(square[0:1] + square[1:2] + square[2:3])
    directions[0:3] = cartesian / jnp.maximum(distance, distance_floor)
    center = lax.broadcasted_iota(jnp.int32, (NRBF, 1), 0).astype(jnp.float32) * (radial_reach / (NRBF - 1))
    away = (distance - center) / (1.5 * radial_reach / NRBF)
    radial = jnp.exp(-(away * away)).astype(jnp.bfloat16)
    filters[...] = dot(radial_weight[...], radial, ((0,), (0,)))

    def slots(step, sums):
        at = pl.ds(pl.multiple_of(step * 2 * ATOM, 2 * ATOM), 2 * ATOM)
        picked = dot(ext[:384], chosen[:, at], ((1,), (0,)))
        terms = picked[:192] * filters[:, at]
        toward = directions[:, at]
        parts = [terms[:F]]
        for x in range(3):
            parts.append(
                picked[192 + x * F : 192 + (x + 1) * F] * terms[F : 2 * F] + terms[2 * F :] * toward[x : x + 1]
            )
        return tuple(s + p[:, :ATOM] + p[:, ATOM:] for s, p in zip(sums, parts))

    zero = jnp.zeros((F, ATOM), jnp.float32)
    sums = lax.fori_loop(0, NBR // 2, slots, (zero,) * 4)
    scalar_out[...] = packed[:F].astype(jnp.float32) + sums[0]
    for x in range(3):
        vector_out[x] = (vec[x].astype(jnp.float32) + sums[1 + x]).astype(jnp.bfloat16)


def exchanged(x, axes):
    return lax.all_to_all(x, axes, split_axis=0, concat_axis=0, tiled=True)


def swapped(x, first):
    pairs = [((first + i) % SLABS, (first + (i ^ 1)) % SLABS) for i in range(SLABS)]
    return lax.ppermute(x, all_axes, pairs)


def shards(
    features, vectors, positions, neighbours, halo_lists, lattice, kspace_filter,
    node_weight, node_bias, message_weight, radial_weight, ewald_weight,
):
    bf16, f32 = jnp.bfloat16, jnp.float32
    shape = jax.ShapeDtypeStruct
    half_at = lax.axis_index("yh") * KDEV
    k_at = lax.axis_index(kb_axes) * 2 * KDEV + half_at
    packed = packed_rows(features, positions)
    own = exchanged(jnp.broadcast_to(packed, (SAME, PACK, ATOM)), same_axes)
    other = swapped(own, 0)
    own_lattice = jnp.pad(lax.dynamic_slice_in_dim(lattice, k_at, KDEV, 1).astype(f32), ((0, 5), (0, 0)))
    own_filter = jnp.pad(lax.dynamic_slice_in_dim(kspace_filter, half_at, KDEV, 1) * norm_scale, ((0, 0), (0, F)))
    own_filter = own_filter + jnp.pad(ewald_weight.astype(f32), ((0, 0), (KDEV, 0)))
    core = lax.axis_index("c").astype(jnp.int32).reshape(1)
    halo = shape((HALO_ROWS, ATOM), bf16)
    own_table, own_total = call(
        own_table_kernel,
        [VM, VM, ANY],
        (shape((SPARE, 2 * KDEV, SAME * ATOM), bf16), shape((2 * KDEV, F), f32)),
        own, own_lattice, own_filter,
        scratch=[
            VM((2 * KDEV, SAME * ATOM), bf16),
            VM((3, KDEV, ATOM), f32),
            pltpu.SemaphoreType.DMA((SAME // GROUP,)),
        ],
        far_outs=(0,),
        flops=10**11,
    )
    other_table, partial = call(
        other_table_kernel,
        [VM] * 3,
        (shape((2 * KDEV, SAME * ATOM), bf16), shape((KDEV, 2 * F), bf16)),
        other, own_lattice, own_total,
        scratch=[VM((3, KDEV, ATOM), f32), VM((2 * KDEV, F), f32)],
    )
    arrived = exchanged(partial.reshape(DEPTH, KDEV // DEPTH, 2 * F), "z")
    far, near = call(
        halo_kernel, [SM, VM, VM, VM, ANY], (halo, halo), core, packed, vectors, halo_lists, partial
    )
    far = swapped(far, 1)
    owned = call(sum_kernel, [VM, ANY], shape((DEPTH, KDEV // DEPTH, 2 * F), bf16), arrived, far)
    totals = exchanged(owned, "z").reshape(KDEV, 2 * F)
    for_other = call(
        project_other_kernel,
        [VM] * 4,
        shape((SAME * F + HALO_ROWS, ATOM), bf16),
        totals, own_filter, other_table, near,
    )
    received = swapped(for_other, 0)
    messages = call(
        project_own_kernel,
        [VM, VM, ANY, VM],
        shape((SAME, F, ATOM), bf16),
        totals, own_filter, own_table, received,
        scratch=[VM((2 * KDEV, SAME * ATOM), bf16), pltpu.SemaphoreType.DMA((SAME // 4,))],
    )
    returned = exchanged(messages, same_axes)
    scalar, new_vectors = call(
        short_kernel,
        [SM] + [VM] * 9 + [ANY],
        (shape((F, ATOM), f32), shape((3, F, ATOM), bf16)),
        core, packed, vectors, neighbours, received, far,
        node_weight, node_bias.reshape(1, F), message_weight, radial_weight, messages,
        scratch=[
            VM((F, 3 * ATOM), bf16),
            VM((400, 3 * ATOM), bf16),
            VM((3 * ATOM, NBR * ATOM), bf16),
            VM((192, NBR * ATOM), f32),
            VM((8, NBR * ATOM), f32),
        ],
    )
    new_features = call(finish_kernel, [VM] * 2, shape((F, ATOM), bf16), returned, scalar)
    return new_features, new_vectors


def solution(mesh):
    fine = Mesh(mesh.devices.reshape(2, 16, 2, 4, 2), all_axes)
    atoms = P(None, all_axes)
    placed = (
        atoms, P(None, None, all_axes), atoms, atoms, atoms, P(), P(None, kb_axes),
        P(), P(), P(), P(), P(),
    )
    return jax.shard_map(
        shards,
        mesh=fine,
        in_specs=placed,
        out_specs=(atoms, P(None, None, all_axes)),
        check_vma=False,
    )
```

```python
import math

import jax
import jax.numpy as jnp
from jax import lax
from jax.experimental import pallas as pl
from jax.experimental.pallas import tpu as pltpu
from jax.sharding import Mesh
from jax.sharding import PartitionSpec as P

F = 64
NRBF = 20
NBR = 16
ATOM = 128
KDEV = 256
PLANE = 32
SAME = 16
DEPTH = 16
SLABS = 512
KVEC = 8192
ATOMS = 65536
PACK = 80
HALO_ROWS = 272

same_axes = ("yh", "yl", "x")
kb_axes = ("yl", "x", "c")
all_axes = ("yh", "z", "yl", "x", "c")

side_length = 6.0
slab_depth = 6.0
radial_reach = 6.0
distance_floor = 1.0
norm_scale = 1.0 / math.sqrt(KVEC * ATOMS)

sine_terms = (4.44287959, -7.30781805, 3.59778873, -0.79123821)
cosine_terms = (1.41420408, -6.97764206, 5.71523839, -1.72834865)
whole_turns = 1.5 * 2.0**23

VMEM_LIMIT = 16 * 2**20


def dot(a, b, dims):
    return lax.dot_general(a, b, (dims, ((), ())), preferred_element_type=jnp.float32)


def polynomial(terms, u):
    value = terms[-1] * u + terms[-2]
    for term in terms[-3::-1]:
        value = value * u + term
    return value


def cosine_and_sine(turns):
    r = turns - ((turns + whole_turns) - whole_turns)
    u = r * r
    s = r * polynomial(sine_terms, u)
    c = polynomial(cosine_terms, u)
    return 1.0 - s * s, s * c


VM, SM, ANY = pltpu.VMEM, pltpu.SMEM, pl.ANY


def call(kernel, places, outs, *operands, scratch=(), flops=0):
    return pl.pallas_call(
        kernel,
        out_shape=outs,
        in_specs=[pl.BlockSpec(memory_space=place) for place in places],
        out_specs=jax.tree.map(lambda _: pl.BlockSpec(memory_space=VM), outs),
        scratch_shapes=list(scratch),
        compiler_params=pltpu.CompilerParams(vmem_limit_bytes=VMEM_LIMIT),
        cost_estimate=pl.CostEstimate(flops=flops, bytes_accessed=0, transcendentals=0),
    )(*operands)


def packed_rows(feat, pos):
    placed = [jnp.pad(pos, ((at, PACK - at - 3), (0, 0))) for at in (F, F + 3, F + 6)]
    firsts = [lax.reduce_precision(value, 8, 7) for value in placed]
    seconds = [lax.reduce_precision(value - first, 8, 7) for value, first in zip(placed[1:], firsts[1:])]
    pieces = firsts[0] + seconds[0] + ((placed[2] - firsts[2]) - seconds[1])
    return jnp.pad(feat, ((0, PACK - F), (0, 0))) + pieces.astype(jnp.bfloat16)


def summed(pieces):
    return pieces[0:3] + pieces[3:6] + pieces[6:9]


def halo_kernel(core, packed, vec, halo, far, near):
    rows = jnp.concatenate([packed[...], vec[0], vec[1], vec[2]], axis=0)
    atom = lax.broadcasted_iota(jnp.int32, (ATOM, ATOM), 0)
    for row, out in ((1 - core[0], far), (core[0], near)):
        chosen = jnp.where(atom == halo[pl.ds(row, 1), :], 1.0, 0.0).astype(jnp.bfloat16)
        out[...] = dot(rows, chosen, ((1,), (0,))).astype(jnp.bfloat16)


def add_atoms(got, constants, table, columns, total):
    turned = constants[F:, :KDEV].T
    for i in range(3):
        columns[i] = jnp.broadcast_to(turned[:, i : i + 1], (KDEV, ATOM))
    for first in range(0, SAME, 2):
        both = jnp.concatenate([got[first], got[first + 1]], axis=1)
        pos = summed(both[F:].astype(jnp.float32))
        at = slice(first * ATOM, (first + 2) * ATOM)
        for k in range(0, KDEV, 64):
            rows = slice(k, k + 64)
            halves = []
            for lanes in (slice(0, ATOM), slice(ATOM, 2 * ATOM)):
                halves.append(
                    (columns[0, rows] * pos[0:1, lanes] + columns[1, rows] * pos[1:2, lanes])
                    + columns[2, rows] * pos[2:3, lanes]
                )
            cosines, sines = cosine_and_sine(jnp.concatenate(halves, axis=1))
            cosines, sines = cosines.astype(jnp.bfloat16), sines.astype(jnp.bfloat16)
            table[k : k + 64, at] = cosines
            table[KDEV + k : KDEV + k + 64, at] = sines
            sums = dot(jnp.concatenate([cosines, sines], axis=0), both[:F], ((1,), (1,)))
            total[k : k + 64] += sums[:64]
            total[KDEV + k : KDEV + k + 64] += sums[64:]


def own_table_kernel(got, constants, table, total, columns):
    total[...] = jnp.zeros_like(total)
    add_atoms(got, constants, table, columns, total)


def other_table_kernel(got, constants, own_total, far, table, partial, columns, total):
    total[...] = own_total[...]
    add_atoms(got, constants, table, columns, total)
    partial[...] = jnp.concatenate([total[:KDEV], total[KDEV:]], axis=1).astype(jnp.bfloat16)


def sum_kernel(arrived, out):
    total = arrived[0].astype(jnp.float32)
    for i in range(1, DEPTH):
        total = total + arrived[i].astype(jnp.float32)
    total = total.astype(jnp.bfloat16)
    for i in range(DEPTH):
        out[i] = total


def filtered_sums(got, constants):
    own, weight = constants[:F, :KDEV], constants[:F, KDEV:].astype(jnp.bfloat16)
    total = [dot(weight, got[:, part * F : (part + 1) * F], ((0,), (1,))) for part in range(2)]
    return jnp.concatenate([own * total[0], own * total[1]], axis=1).astype(jnp.bfloat16)


def project_other_kernel(got, constants, table, near, out):
    filtered = filtered_sums(got, constants)
    for first in range(0, SAME, 8):
        message = dot(filtered, table[:, first * ATOM : (first + 8) * ATOM], ((1,), (0,))).astype(jnp.bfloat16)
        for p in range(8):
            out[(first + p) * F : (first + p + 1) * F] = message[:, p * ATOM : (p + 1) * ATOM]
    out[SAME * F :] = near[...]


def project_own_kernel(got, constants, table, received, out):
    filtered = filtered_sums(got, constants)
    for first in range(0, SAME, 8):
        message = dot(filtered, table[:, first * ATOM : (first + 8) * ATOM], ((1,), (0,)))
        for p in range(first, first + 8):
            there = received[p * F : (p + 1) * F].astype(jnp.float32)
            out[p] = (message[:, (p - first) * ATOM : (p - first + 1) * ATOM] + there).astype(jnp.bfloat16)


def finish_kernel(arrived, scalar, out):
    total = arrived[0].astype(jnp.float32)
    for i in range(1, SAME):
        total = total + arrived[i].astype(jnp.float32)
    out[...] = (scalar[...] + total).astype(jnp.bfloat16)


def short_kernel(
    core, packed, vec, ids, near, far, node_weight, bias, message_weight, radial_weight, messages,
    scalar_out, vector_out, feats, ext, chosen, filters, directions,
):
    pos = summed(packed[F:].astype(jnp.float32))
    feats[:, :ATOM] = packed[:F]
    ext[192:384, :ATOM] = jnp.concatenate([vec[0], vec[1], vec[2]], axis=0)
    ext[384:, :ATOM] = packed[F:]
    near_at = pl.ds(pl.multiple_of((2 - core[0]) * ATOM, ATOM), ATOM)
    far_at = pl.ds(pl.multiple_of((1 + core[0]) * ATOM, ATOM), ATOM)
    for side, start, at in ((near, SAME * F, near_at), (far, 0, far_at)):
        feats[:, at] = side[start : start + F]
        ext[192:384, at] = side[start + PACK : start + HALO_ROWS]
        ext[384:, at] = side[start + F : start + PACK]
    bias_column = jnp.broadcast_to(bias[...], (8, F)).T[:, 0:1]
    hidden = dot(node_weight[...], feats[...], ((0,), (0,))) + bias_column
    hidden = (hidden / (1.0 + jnp.exp(-hidden))).astype(jnp.bfloat16)
    ext[:192] = dot(message_weight[...], hidden, ((0,), (0,))).astype(jnp.bfloat16)

    number = lax.broadcasted_iota(jnp.int32, (3 * ATOM, ATOM), 0)
    for j in range(NBR):
        chosen[:, j * ATOM : (j + 1) * ATOM] = jnp.where(number == ids[j : j + 1, :], 1.0, 0.0).astype(jnp.bfloat16)
    found = dot(ext[384:], chosen[...], ((1,), (0,)))
    offset = summed(found) - jnp.concatenate([pos] * NBR, axis=1)
    offset = offset - jnp.floor(offset + 0.5)
    side = lax.broadcasted_iota(jnp.int32, (3, 1), 0)
    box = jnp.where(side == 2, slab_depth * SLABS, side_length).astype(jnp.float32)
    cartesian = offset * box
    square = cartesian * cartesian
    distance = jnp.sqrt(square[0:1] + square[1:2] + square[2:3])
    directions[0:3] = cartesian / jnp.maximum(distance, distance_floor)
    center = lax.broadcasted_iota(jnp.int32, (NRBF, 1), 0).astype(jnp.float32) * (radial_reach / (NRBF - 1))
    away = (distance - center) / (1.5 * radial_reach / NRBF)
    radial = jnp.exp(-(away * away)).astype(jnp.bfloat16)
    filters[...] = dot(radial_weight[...], radial, ((0,), (0,)))

    def slots(step, sums):
        at = pl.ds(pl.multiple_of(step * 2 * ATOM, 2 * ATOM), 2 * ATOM)
        picked = dot(ext[:384], chosen[:, at], ((1,), (0,)))
        terms = picked[:192] * filters[:, at]
        toward = directions[:, at]
        parts = [terms[:F]]
        for x in range(3):
            parts.append(
                picked[192 + x * F : 192 + (x + 1) * F] * terms[F : 2 * F] + terms[2 * F :] * toward[x : x + 1]
            )
        return tuple(s + p[:, :ATOM] + p[:, ATOM:] for s, p in zip(sums, parts))

    zero = jnp.zeros((F, ATOM), jnp.float32)
    sums = lax.fori_loop(0, NBR // 2, slots, (zero,) * 4)
    scalar_out[...] = packed[:F].astype(jnp.float32) + sums[0]
    for x in range(3):
        vector_out[x] = (vec[x].astype(jnp.float32) + sums[1 + x]).astype(jnp.bfloat16)


def exchanged(x, axes):
    return lax.all_to_all(x, axes, split_axis=0, concat_axis=0, tiled=True)


def swapped(x, first):
    pairs = [((first + i) % SLABS, (first + (i ^ 1)) % SLABS) for i in range(SLABS)]
    return lax.ppermute(x, all_axes, pairs)


def shards(
    features, vectors, positions, neighbours, halo_lists, lattice, kspace_filter,
    node_weight, node_bias, message_weight, radial_weight, ewald_weight,
):
    bf16, f32 = jnp.bfloat16, jnp.float32
    shape = jax.ShapeDtypeStruct
    half_at = lax.axis_index("yh") * KDEV
    k_at = lax.axis_index(kb_axes) * 2 * KDEV + half_at
    packed = packed_rows(features, positions)
    own = exchanged(jnp.broadcast_to(packed, (SAME, PACK, ATOM)), same_axes)
    other = swapped(own, 0)
    own_lattice = lax.dynamic_slice_in_dim(lattice, k_at, KDEV, 1).astype(f32)
    own_filter = lax.dynamic_slice_in_dim(kspace_filter, half_at, KDEV, 1) * norm_scale
    constants = jnp.pad(own_filter, ((0, 8), (0, F))) + jnp.pad(own_lattice, ((F, 5), (0, F)))
    constants = constants + jnp.pad(ewald_weight.astype(f32), ((0, 8), (KDEV, 0)))
    core = lax.axis_index("c").astype(jnp.int32).reshape(1)
    halo = shape((HALO_ROWS, ATOM), bf16)
    far, near = call(halo_kernel, [SM, VM, VM, VM], (halo, halo), core, packed, vectors, halo_lists)
    far = swapped(far, 1)
    half_table = shape((2 * KDEV, SAME * ATOM), bf16)
    own_table, own_total = call(
        own_table_kernel,
        [VM, VM],
        (half_table, shape((2 * KDEV, F), f32)),
        own, constants,
        scratch=[VM((3, KDEV, ATOM), f32)],
        flops=3 * 10**9,
    )
    other_table, partial = call(
        other_table_kernel,
        [VM, VM, VM, ANY],
        (half_table, shape((KDEV, 2 * F), bf16)),
        other, constants, own_total, far,
        scratch=[VM((3, KDEV, ATOM), f32), VM((2 * KDEV, F), f32)],
    )
    arrived = exchanged(partial.reshape(DEPTH, KDEV // DEPTH, 2 * F), "z")
    owned = call(sum_kernel, [VM], shape((DEPTH, KDEV // DEPTH, 2 * F), bf16), arrived)
    totals = exchanged(owned, "z").reshape(KDEV, 2 * F)
    for_other = call(
        project_other_kernel,
        [VM] * 4,
        shape((SAME * F + HALO_ROWS, ATOM), bf16),
        totals, constants, other_table, near,
    )
    received = swapped(for_other, 0)
    messages = call(
        project_own_kernel, [VM] * 4, shape((SAME, F, ATOM), bf16), totals, constants, own_table, received
    )
    returned = exchanged(messages, same_axes)
    scalar, new_vectors = call(
        short_kernel,
        [SM] + [VM] * 9 + [ANY],
        (shape((F, ATOM), f32), shape((3, F, ATOM), bf16)),
        core, packed, vectors, neighbours, received, far,
        node_weight, node_bias.reshape(1, F), message_weight, radial_weight, messages,
        scratch=[
            VM((F, 3 * ATOM), bf16),
            VM((400, 3 * ATOM), bf16),
            VM((3 * ATOM, NBR * ATOM), bf16),
            VM((192, NBR * ATOM), f32),
            VM((8, NBR * ATOM), f32),
        ],
    )
    new_features = call(finish_kernel, [VM] * 2, shape((F, ATOM), bf16), returned, scalar)
    return new_features, new_vectors


def solution(mesh):
    fine = Mesh(mesh.devices.reshape(2, 16, 2, 4, 2), all_axes)
    atoms = P(None, all_axes)
    placed = (
        atoms, P(None, None, all_axes), atoms, atoms, atoms, P(), P(None, kb_axes),
        P(), P(), P(), P(), P(),
    )
    return jax.shard_map(
        shards,
        mesh=fine,
        in_specs=placed,
        out_specs=(atoms, P(None, None, all_axes)),
        check_vma=False,
    )
```

```python
import math

import jax
import jax.numpy as jnp
from jax import lax
from jax.experimental import pallas as pl
from jax.experimental.pallas import tpu as pltpu
from jax.sharding import Mesh
from jax.sharding import PartitionSpec as P

F = 64
NRBF = 20
NBR = 16
ATOM = 128
KDEV = 256
PLANE = 32
SAME = 16
DEPTH = 16
SLABS = 512
KVEC = 8192
ATOMS = 65536
PACK = 80
HALO_ROWS = 272

same_axes = ("yh", "yl", "x")
kb_axes = ("yl", "x", "c")
all_axes = ("yh", "z", "yl", "x", "c")

side_length = 6.0
slab_depth = 6.0
radial_reach = 6.0
distance_floor = 1.0
norm_scale = 1.0 / math.sqrt(KVEC * ATOMS)

sine_terms = (4.44287959, -7.30781805, 3.59778873, -0.79123821)
cosine_terms = (1.41420408, -6.97764206, 5.71523839, -1.72834865)
whole_turns = 1.5 * 2.0**23

VMEM_LIMIT = 16 * 2**20


def dot(a, b, dims):
    return lax.dot_general(a, b, (dims, ((), ())), preferred_element_type=jnp.float32)


def polynomial(terms, u):
    value = terms[-1] * u + terms[-2]
    for term in terms[-3::-1]:
        value = value * u + term
    return value


def cosine_and_sine(turns):
    r = turns - ((turns + whole_turns) - whole_turns)
    u = r * r
    s = r * polynomial(sine_terms, u)
    c = polynomial(cosine_terms, u)
    return 1.0 - s * s, s * c


VM, SM, ANY = pltpu.VMEM, pltpu.SMEM, pl.ANY


def call(kernel, places, outs, *operands, scratch=(), flops=0):
    return pl.pallas_call(
        kernel,
        out_shape=outs,
        in_specs=[pl.BlockSpec(memory_space=place) for place in places],
        out_specs=jax.tree.map(lambda _: pl.BlockSpec(memory_space=VM), outs),
        scratch_shapes=list(scratch),
        compiler_params=pltpu.CompilerParams(vmem_limit_bytes=VMEM_LIMIT),
        cost_estimate=pl.CostEstimate(flops=flops, bytes_accessed=0, transcendentals=0),
    )(*operands)


def packed_rows(feat, pos):
    placed = [jnp.pad(pos, ((at, PACK - at - 3), (0, 0))) for at in (F, F + 3, F + 6)]
    firsts = [lax.reduce_precision(value, 8, 7) for value in placed]
    seconds = [lax.reduce_precision(value - first, 8, 7) for value, first in zip(placed[1:], firsts[1:])]
    pieces = firsts[0] + seconds[0] + ((placed[2] - firsts[2]) - seconds[1])
    return jnp.pad(feat, ((0, PACK - F), (0, 0))) + pieces.astype(jnp.bfloat16)


def summed(pieces):
    return pieces[0:3] + pieces[3:6] + pieces[6:9]


def halo_kernel(core, packed, vec, halo, far, near):
    rows = jnp.concatenate([packed[...], vec[0], vec[1], vec[2]], axis=0)
    atom = lax.broadcasted_iota(jnp.int32, (ATOM, ATOM), 0)
    for row, out in ((1 - core[0], far), (core[0], near)):
        chosen = jnp.where(atom == halo[pl.ds(row, 1), :], 1.0, 0.0).astype(jnp.bfloat16)
        out[...] = dot(rows, chosen, ((1,), (0,))).astype(jnp.bfloat16)


def add_atoms(got, constants, table, columns, total):
    turned = constants[F:, :KDEV].T
    for i in range(3):
        columns[i] = jnp.broadcast_to(turned[:, i : i + 1], (KDEV, ATOM))
    for first in range(0, SAME, 2):
        both = jnp.concatenate([got[first], got[first + 1]], axis=1)
        pos = summed(both[F:].astype(jnp.float32))
        at = slice(first * ATOM, (first + 2) * ATOM)
        for k in range(0, KDEV, 64):
            rows = slice(k, k + 64)
            halves = []
            for lanes in (slice(0, ATOM), slice(ATOM, 2 * ATOM)):
                halves.append(
                    (columns[0, rows] * pos[0:1, lanes] + columns[1, rows] * pos[1:2, lanes])
                    + columns[2, rows] * pos[2:3, lanes]
                )
            cosines, sines = cosine_and_sine(jnp.concatenate(halves, axis=1))
            cosines, sines = cosines.astype(jnp.bfloat16), sines.astype(jnp.bfloat16)
            table[k : k + 64, at] = cosines
            table[KDEV + k : KDEV + k + 64, at] = sines
            sums = dot(jnp.concatenate([cosines, sines], axis=0), both[:F], ((1,), (1,)))
            total[k : k + 64] += sums[:64]
            total[KDEV + k : KDEV + k + 64] += sums[64:]


def own_table_kernel(got, constants, table, total, columns):
    total[...] = jnp.zeros_like(total)
    add_atoms(got, constants, table, columns, total)


def other_table_kernel(got, constants, own_total, far, table, partial, columns, total):
    total[...] = own_total[...]
    add_atoms(got, constants, table, columns, total)
    partial[...] = jnp.concatenate([total[:KDEV], total[KDEV:]], axis=1).astype(jnp.bfloat16)


def sum_kernel(arrived, out):
    total = arrived[0].astype(jnp.float32)
    for i in range(1, DEPTH):
        total = total + arrived[i].astype(jnp.float32)
    total = total.astype(jnp.bfloat16)
    for i in range(DEPTH):
        out[i] = total


def filtered_sums(got, constants):
    own, weight = constants[:F, :KDEV], constants[:F, KDEV:].astype(jnp.bfloat16)
    total = [dot(weight, got[:, part * F : (part + 1) * F], ((0,), (1,))) for part in range(2)]
    return jnp.concatenate([own * total[0], own * total[1]], axis=1).astype(jnp.bfloat16)


def project_other_kernel(got, constants, table, near, out):
    filtered = filtered_sums(got, constants)
    for first in range(0, SAME, 8):
        message = dot(filtered, table[:, first * ATOM : (first + 8) * ATOM], ((1,), (0,))).astype(jnp.bfloat16)
        for p in range(8):
            out[(first + p) * F : (first + p + 1) * F] = message[:, p * ATOM : (p + 1) * ATOM]
    out[SAME * F :] = near[...]


def project_own_kernel(got, constants, table, out):
    filtered = filtered_sums(got, constants)
    for first in range(0, SAME, 8):
        message = dot(filtered, table[:, first * ATOM : (first + 8) * ATOM], ((1,), (0,)))
        for p in range(8):
            out[first + p] = message[:, p * ATOM : (p + 1) * ATOM]


def join_kernel(own, received, out):
    for p in range(SAME):
        out[p] = (own[p] + received[p * F : (p + 1) * F].astype(jnp.float32)).astype(jnp.bfloat16)


def finish_kernel(arrived, scalar, out):
    total = arrived[0].astype(jnp.float32)
    for i in range(1, SAME):
        total = total + arrived[i].astype(jnp.float32)
    out[...] = (scalar[...] + total).astype(jnp.bfloat16)


def short_kernel(
    core, packed, vec, ids, near, far, node_weight, bias, message_weight, radial_weight, messages,
    scalar_out, vector_out, feats, ext, chosen, filters, directions,
):
    pos = summed(packed[F:].astype(jnp.float32))
    feats[:, :ATOM] = packed[:F]
    ext[192:384, :ATOM] = jnp.concatenate([vec[0], vec[1], vec[2]], axis=0)
    ext[384:, :ATOM] = packed[F:]
    near_at = pl.ds(pl.multiple_of((2 - core[0]) * ATOM, ATOM), ATOM)
    far_at = pl.ds(pl.multiple_of((1 + core[0]) * ATOM, ATOM), ATOM)
    for side, start, at in ((near, SAME * F, near_at), (far, 0, far_at)):
        feats[:, at] = side[start : start + F]
        ext[192:384, at] = side[start + PACK : start + HALO_ROWS]
        ext[384:, at] = side[start + F : start + PACK]
    bias_column = jnp.broadcast_to(bias[...], (8, F)).T[:, 0:1]
    hidden = dot(node_weight[...], feats[...], ((0,), (0,))) + bias_column
    hidden = (hidden / (1.0 + jnp.exp(-hidden))).astype(jnp.bfloat16)
    ext[:192] = dot(message_weight[...], hidden, ((0,), (0,))).astype(jnp.bfloat16)

    number = lax.broadcasted_iota(jnp.int32, (3 * ATOM, ATOM), 0)
    for j in range(NBR):
        chosen[:, j * ATOM : (j + 1) * ATOM] = jnp.where(number == ids[j : j + 1, :], 1.0, 0.0).astype(jnp.bfloat16)
    found = dot(ext[384:], chosen[...], ((1,), (0,)))
    offset = summed(found) - jnp.concatenate([pos] * NBR, axis=1)
    offset = offset - jnp.floor(offset + 0.5)
    side = lax.broadcasted_iota(jnp.int32, (3, 1), 0)
    box = jnp.where(side == 2, slab_depth * SLABS, side_length).astype(jnp.float32)
    cartesian = offset * box
    square = cartesian * cartesian
    distance = jnp.sqrt(square[0:1] + square[1:2] + square[2:3])
    directions[0:3] = cartesian / jnp.maximum(distance, distance_floor)
    center = lax.broadcasted_iota(jnp.int32, (NRBF, 1), 0).astype(jnp.float32) * (radial_reach / (NRBF - 1))
    away = (distance - center) / (1.5 * radial_reach / NRBF)
    radial = jnp.exp(-(away * away)).astype(jnp.bfloat16)
    filters[...] = dot(radial_weight[...], radial, ((0,), (0,)))

    def slots(step, sums):
        at = pl.ds(pl.multiple_of(step * 2 * ATOM, 2 * ATOM), 2 * ATOM)
        picked = dot(ext[:384], chosen[:, at], ((1,), (0,)))
        terms = picked[:192] * filters[:, at]
        toward = directions[:, at]
        parts = [terms[:F]]
        for x in range(3):
            parts.append(
                picked[192 + x * F : 192 + (x + 1) * F] * terms[F : 2 * F] + terms[2 * F :] * toward[x : x + 1]
            )
        return tuple(s + p[:, :ATOM] + p[:, ATOM:] for s, p in zip(sums, parts))

    zero = jnp.zeros((F, ATOM), jnp.float32)
    sums = lax.fori_loop(0, NBR // 2, slots, (zero,) * 4)
    scalar_out[...] = packed[:F].astype(jnp.float32) + sums[0]
    for x in range(3):
        vector_out[x] = (vec[x].astype(jnp.float32) + sums[1 + x]).astype(jnp.bfloat16)


def exchanged(x, axes):
    return lax.all_to_all(x, axes, split_axis=0, concat_axis=0, tiled=True)


def swapped(x, first):
    pairs = [((first + i) % SLABS, (first + (i ^ 1)) % SLABS) for i in range(SLABS)]
    return lax.ppermute(x, all_axes, pairs)


def shards(
    features, vectors, positions, neighbours, halo_lists, lattice, kspace_filter,
    node_weight, node_bias, message_weight, radial_weight, ewald_weight,
):
    bf16, f32 = jnp.bfloat16, jnp.float32
    shape = jax.ShapeDtypeStruct
    half_at = lax.axis_index("yh") * KDEV
    k_at = lax.axis_index(kb_axes) * 2 * KDEV + half_at
    packed = packed_rows(features, positions)
    own = exchanged(jnp.broadcast_to(packed, (SAME, PACK, ATOM)), same_axes)
    other = swapped(own, 0)
    own_lattice = lax.dynamic_slice_in_dim(lattice, k_at, KDEV, 1).astype(f32)
    own_filter = lax.dynamic_slice_in_dim(kspace_filter, half_at, KDEV, 1) * norm_scale
    constants = jnp.pad(own_filter, ((0, 8), (0, F))) + jnp.pad(own_lattice, ((F, 5), (0, F)))
    constants = constants + jnp.pad(ewald_weight.astype(f32), ((0, 8), (KDEV, 0)))
    core = lax.axis_index("c").astype(jnp.int32).reshape(1)
    halo = shape((HALO_ROWS, ATOM), bf16)
    far, near = call(halo_kernel, [SM, VM, VM, VM], (halo, halo), core, packed, vectors, halo_lists)
    far = swapped(far, 1)
    half_table = shape((2 * KDEV, SAME * ATOM), bf16)
    own_table, own_total = call(
        own_table_kernel,
        [VM, VM],
        (half_table, shape((2 * KDEV, F), f32)),
        own, constants,
        scratch=[VM((3, KDEV, ATOM), f32)],
        flops=3 * 10**9,
    )
    other_table, partial = call(
        other_table_kernel,
        [VM, VM, VM, ANY],
        (half_table, shape((KDEV, 2 * F), bf16)),
        other, constants, own_total, far,
        scratch=[VM((3, KDEV, ATOM), f32), VM((2 * KDEV, F), f32)],
    )
    arrived = exchanged(partial.reshape(DEPTH, KDEV // DEPTH, 2 * F), "z")
    owned = call(sum_kernel, [VM], shape((DEPTH, KDEV // DEPTH, 2 * F), bf16), arrived)
    totals = exchanged(owned, "z").reshape(KDEV, 2 * F)
    for_other = call(
        project_other_kernel,
        [VM] * 4,
        shape((SAME * F + HALO_ROWS, ATOM), bf16),
        totals, constants, other_table, near,
    )
    received = swapped(for_other, 0)
    own_messages = call(
        project_own_kernel, [VM] * 3, shape((SAME, F, ATOM), f32), totals, constants, own_table,
        flops=10**9,
    )
    messages = call(join_kernel, [VM] * 2, shape((SAME, F, ATOM), bf16), own_messages, received)
    returned = exchanged(messages, same_axes)
    scalar, new_vectors = call(
        short_kernel,
        [SM] + [VM] * 9 + [ANY],
        (shape((F, ATOM), f32), shape((3, F, ATOM), bf16)),
        core, packed, vectors, neighbours, received, far,
        node_weight, node_bias.reshape(1, F), message_weight, radial_weight, messages,
        scratch=[
            VM((F, 3 * ATOM), bf16),
            VM((400, 3 * ATOM), bf16),
            VM((3 * ATOM, NBR * ATOM), bf16),
            VM((192, NBR * ATOM), f32),
            VM((8, NBR * ATOM), f32),
        ],
    )
    new_features = call(finish_kernel, [VM] * 2, shape((F, ATOM), bf16), returned, scalar)
    return new_features, new_vectors


def solution(mesh):
    fine = Mesh(mesh.devices.reshape(2, 16, 2, 4, 2), all_axes)
    atoms = P(None, all_axes)
    placed = (
        atoms, P(None, None, all_axes), atoms, atoms, atoms, P(), P(None, kb_axes),
        P(), P(), P(), P(), P(),
    )
    return jax.shard_map(
        shards,
        mesh=fine,
        in_specs=placed,
        out_specs=(atoms, P(None, None, all_axes)),
        check_vma=False,
    )
```

```python
import math

import jax
import jax.numpy as jnp
from jax import lax
from jax.experimental import pallas as pl
from jax.experimental.pallas import tpu as pltpu
from jax.sharding import Mesh
from jax.sharding import PartitionSpec as P

F = 64
NRBF = 20
NBR = 16
ATOM = 128
KDEV = 256
PLANE = 32
SAME = 16
DEPTH = 16
SLABS = 512
KVEC = 8192
ATOMS = 65536
PACK = 80
HALO_ROWS = 272

same_axes = ("yh", "yl", "x")
kb_axes = ("yl", "x", "c")
all_axes = ("yh", "z", "yl", "x", "c")

side_length = 6.0
slab_depth = 6.0
radial_reach = 6.0
distance_floor = 1.0
norm_scale = 1.0 / math.sqrt(KVEC * ATOMS)

sine_terms = (4.44287959, -7.30781805, 3.59778873, -0.79123821)
cosine_terms = (1.41420408, -6.97764206, 5.71523839, -1.72834865)
whole_turns = 1.5 * 2.0**23

VMEM_LIMIT = 16 * 2**20


def dot(a, b, dims):
    return lax.dot_general(a, b, (dims, ((), ())), preferred_element_type=jnp.float32)


def polynomial(terms, u):
    value = terms[-1] * u + terms[-2]
    for term in terms[-3::-1]:
        value = value * u + term
    return value


def cosine_and_sine(turns):
    r = turns - ((turns + whole_turns) - whole_turns)
    u = r * r
    s = r * polynomial(sine_terms, u)
    c = polynomial(cosine_terms, u)
    return 1.0 - s * s, s * c


VM, SM, ANY = pltpu.VMEM, pltpu.SMEM, pl.ANY


def call(kernel, places, outs, *operands, scratch=(), flops=0):
    return pl.pallas_call(
        kernel,
        out_shape=outs,
        in_specs=[pl.BlockSpec(memory_space=place) for place in places],
        out_specs=jax.tree.map(lambda _: pl.BlockSpec(memory_space=VM), outs),
        scratch_shapes=list(scratch),
        compiler_params=pltpu.CompilerParams(vmem_limit_bytes=VMEM_LIMIT),
        cost_estimate=pl.CostEstimate(flops=flops, bytes_accessed=0, transcendentals=0),
    )(*operands)


def packed_rows(feat, pos):
    placed = [jnp.pad(pos, ((at, PACK - at - 3), (0, 0))) for at in (F, F + 3, F + 6)]
    firsts = [lax.reduce_precision(value, 8, 7) for value in placed]
    seconds = [lax.reduce_precision(value - first, 8, 7) for value, first in zip(placed[1:], firsts[1:])]
    pieces = firsts[0] + seconds[0] + ((placed[2] - firsts[2]) - seconds[1])
    return jnp.pad(feat, ((0, PACK - F), (0, 0))) + pieces.astype(jnp.bfloat16)


def summed(pieces):
    return pieces[0:3] + pieces[3:6] + pieces[6:9]


def halo_kernel(core, packed, vec, halo, far, near):
    rows = jnp.concatenate([packed[...], vec[0], vec[1], vec[2]], axis=0)
    atom = lax.broadcasted_iota(jnp.int32, (ATOM, ATOM), 0)
    for row, out in ((1 - core[0], far), (core[0], near)):
        chosen = jnp.where(atom == halo[pl.ds(row, 1), :], 1.0, 0.0).astype(jnp.bfloat16)
        out[...] = dot(rows, chosen, ((1,), (0,))).astype(jnp.bfloat16)


def add_atoms(got, table, columns, total):
    for first in range(0, SAME, 2):
        both = jnp.concatenate([got[first], got[first + 1]], axis=1)
        pos = summed(both[F:].astype(jnp.float32))
        at = slice(first * ATOM, (first + 2) * ATOM)
        for k in range(0, KDEV, 64):
            rows = slice(k, k + 64)
            halves = []
            for lanes in (slice(0, ATOM), slice(ATOM, 2 * ATOM)):
                halves.append(
                    (columns[0, rows] * pos[0:1, lanes] + columns[1, rows] * pos[1:2, lanes])
                    + columns[2, rows] * pos[2:3, lanes]
                )
            cosines, sines = cosine_and_sine(jnp.concatenate(halves, axis=1))
            cosines, sines = cosines.astype(jnp.bfloat16), sines.astype(jnp.bfloat16)
            table[k : k + 64, at] = cosines
            table[KDEV + k : KDEV + k + 64, at] = sines
            sums = dot(jnp.concatenate([cosines, sines], axis=0), both[:F], ((1,), (1,)))
            total[k : k + 64] += sums[:64]
            total[KDEV + k : KDEV + k + 64] += sums[64:]


def own_table_kernel(got, lattice, constants, table, total, columns):
    turned = jnp.concatenate([lattice[...], jnp.zeros((5, KDEV), jnp.float32)], axis=0).T
    for i in range(3):
        columns[i] = jnp.broadcast_to(turned[:, i : i + 1], (KDEV, ATOM))
    total[...] = jnp.zeros_like(total)
    add_atoms(got, table, columns, total)


def other_table_kernel(got, columns, own_total, far, table, partial, total):
    total[...] = own_total[...]
    add_atoms(got, table, columns, total)
    partial[...] = jnp.concatenate([total[:KDEV], total[KDEV:]], axis=1).astype(jnp.bfloat16)


def sum_kernel(arrived, out):
    total = arrived[0].astype(jnp.float32)
    for i in range(1, DEPTH):
        total = total + arrived[i].astype(jnp.float32)
    total = total.astype(jnp.bfloat16)
    for i in range(DEPTH):
        out[i] = total


def filtered_sums(half, got, constants):
    own = constants[:, pl.ds(pl.multiple_of(half[0], KDEV), KDEV)] * norm_scale
    weight = constants[:, 2 * KDEV :].astype(jnp.bfloat16)
    total = [dot(weight, got[:, part * F : (part + 1) * F], ((0,), (1,))) for part in range(2)]
    return jnp.concatenate([own * total[0], own * total[1]], axis=1).astype(jnp.bfloat16)


def project_other_kernel(half, got, constants, table, near, out):
    filtered = filtered_sums(half, got, constants)
    for first in range(0, SAME, 8):
        message = dot(filtered, table[:, first * ATOM : (first + 8) * ATOM], ((1,), (0,))).astype(jnp.bfloat16)
        for p in range(8):
            out[(first + p) * F : (first + p + 1) * F] = message[:, p * ATOM : (p + 1) * ATOM]
    out[SAME * F :] = near[...]


def project_own_kernel(half, got, constants, table, out):
    filtered = filtered_sums(half, got, constants)
    for first in range(0, SAME, 8):
        message = dot(filtered, table[:, first * ATOM : (first + 8) * ATOM], ((1,), (0,)))
        for p in range(8):
            out[first + p] = message[:, p * ATOM : (p + 1) * ATOM]


def join_kernel(own, received, out):
    for p in range(SAME):
        out[p] = (own[p] + received[p * F : (p + 1) * F].astype(jnp.float32)).astype(jnp.bfloat16)


def finish_kernel(arrived, scalar, out):
    total = arrived[0].astype(jnp.float32)
    for i in range(1, SAME):
        total = total + arrived[i].astype(jnp.float32)
    out[...] = (scalar[...] + total).astype(jnp.bfloat16)


def short_kernel(
    core, packed, vec, ids, near, far, node_weight, bias, message_weight, radial_weight, messages,
    scalar_out, vector_out, feats, ext, chosen, filters, directions,
):
    pos = summed(packed[F:].astype(jnp.float32))
    feats[:, :ATOM] = packed[:F]
    ext[192:384, :ATOM] = jnp.concatenate([vec[0], vec[1], vec[2]], axis=0)
    ext[384:, :ATOM] = packed[F:]
    near_at = pl.ds(pl.multiple_of((2 - core[0]) * ATOM, ATOM), ATOM)
    far_at = pl.ds(pl.multiple_of((1 + core[0]) * ATOM, ATOM), ATOM)
    for side, start, at in ((near, SAME * F, near_at), (far, 0, far_at)):
        feats[:, at] = side[start : start + F]
        ext[192:384, at] = side[start + PACK : start + HALO_ROWS]
        ext[384:, at] = side[start + F : start + PACK]
    bias_column = jnp.broadcast_to(bias[...], (8, F)).T[:, 0:1]
    hidden = dot(node_weight[...], feats[...], ((0,), (0,))) + bias_column
    hidden = (hidden / (1.0 + jnp.exp(-hidden))).astype(jnp.bfloat16)
    ext[:192] = dot(message_weight[...], hidden, ((0,), (0,))).astype(jnp.bfloat16)

    number = lax.broadcasted_iota(jnp.int32, (3 * ATOM, ATOM), 0)
    for j in range(NBR):
        chosen[:, j * ATOM : (j + 1) * ATOM] = jnp.where(number == ids[j : j + 1, :], 1.0, 0.0).astype(jnp.bfloat16)
    found = dot(ext[384:], chosen[...], ((1,), (0,)))
    offset = summed(found) - jnp.concatenate([pos] * NBR, axis=1)
    offset = offset - jnp.floor(offset + 0.5)
    side = lax.broadcasted_iota(jnp.int32, (3, 1), 0)
    box = jnp.where(side == 2, slab_depth * SLABS, side_length).astype(jnp.float32)
    cartesian = offset * box
    square = cartesian * cartesian
    distance = jnp.sqrt(square[0:1] + square[1:2] + square[2:3])
    directions[0:3] = cartesian / jnp.maximum(distance, distance_floor)
    center = lax.broadcasted_iota(jnp.int32, (NRBF, 1), 0).astype(jnp.float32) * (radial_reach / (NRBF - 1))
    away = (distance - center) / (1.5 * radial_reach / NRBF)
    radial = jnp.exp(-(away * away)).astype(jnp.bfloat16)
    filters[...] = dot(radial_weight[...], radial, ((0,), (0,)))

    def slots(step, sums):
        at = pl.ds(pl.multiple_of(step * 2 * ATOM, 2 * ATOM), 2 * ATOM)
        picked = dot(ext[:384], chosen[:, at], ((1,), (0,)))
        terms = picked[:192] * filters[:, at]
        toward = directions[:, at]
        parts = [terms[:F]]
        for x in range(3):
            parts.append(
                picked[192 + x * F : 192 + (x + 1) * F] * terms[F : 2 * F] + terms[2 * F :] * toward[x : x + 1]
            )
        return tuple(s + p[:, :ATOM] + p[:, ATOM:] for s, p in zip(sums, parts))

    zero = jnp.zeros((F, ATOM), jnp.float32)
    sums = lax.fori_loop(0, NBR // 2, slots, (zero,) * 4)
    scalar_out[...] = packed[:F].astype(jnp.float32) + sums[0]
    for x in range(3):
        vector_out[x] = (vec[x].astype(jnp.float32) + sums[1 + x]).astype(jnp.bfloat16)


def exchanged(x, axes):
    return lax.all_to_all(x, axes, split_axis=0, concat_axis=0, tiled=True)


def swapped(x, first):
    pairs = [((first + i) % SLABS, (first + (i ^ 1)) % SLABS) for i in range(SLABS)]
    return lax.ppermute(x, all_axes, pairs)


def shards(
    features, vectors, positions, neighbours, halo_lists, lattice, kspace_filter,
    node_weight, node_bias, message_weight, radial_weight, ewald_weight,
):
    bf16, f32 = jnp.bfloat16, jnp.float32
    shape = jax.ShapeDtypeStruct
    half_at = lax.axis_index("yh") * KDEV
    k_at = lax.axis_index(kb_axes) * 2 * KDEV + half_at
    packed = packed_rows(features, positions)
    own = exchanged(jnp.broadcast_to(packed, (SAME, PACK, ATOM)), same_axes)
    other = swapped(own, 0)
    own_lattice = lax.dynamic_slice_in_dim(lattice, k_at, KDEV, 1).astype(f32)
    constants = jnp.pad(kspace_filter, ((0, 0), (0, F)))
    constants = constants + jnp.pad(ewald_weight.astype(f32), ((0, 0), (2 * KDEV, 0)))
    half = half_at.astype(jnp.int32).reshape(1)
    core = lax.axis_index("c").astype(jnp.int32).reshape(1)
    halo = shape((HALO_ROWS, ATOM), bf16)
    far, near = call(halo_kernel, [SM, VM, VM, VM], (halo, halo), core, packed, vectors, halo_lists)
    far = swapped(far, 1)
    half_table = shape((2 * KDEV, SAME * ATOM), bf16)
    own_table, own_total, columns = call(
        own_table_kernel,
        [VM, VM, ANY],
        (half_table, shape((2 * KDEV, F), f32), shape((3, KDEV, ATOM), f32)),
        own, own_lattice, constants,
        flops=37 * 10**8,
    )
    other_table, partial = call(
        other_table_kernel,
        [VM, VM, VM, ANY],
        (half_table, shape((KDEV, 2 * F), bf16)),
        other, columns, own_total, far,
        scratch=[VM((2 * KDEV, F), f32)],
    )
    arrived = exchanged(partial.reshape(DEPTH, KDEV // DEPTH, 2 * F), "z")
    owned = call(sum_kernel, [VM], shape((DEPTH, KDEV // DEPTH, 2 * F), bf16), arrived)
    totals = exchanged(owned, "z").reshape(KDEV, 2 * F)
    for_other = call(
        project_other_kernel,
        [SM] + [VM] * 4,
        shape((SAME * F + HALO_ROWS, ATOM), bf16),
        half, totals, constants, other_table, near,
    )
    received = swapped(for_other, 0)
    own_messages = call(
        project_own_kernel, [SM] + [VM] * 3, shape((SAME, F, ATOM), f32), half, totals, constants, own_table,
        flops=10**9,
    )
    messages = call(join_kernel, [VM] * 2, shape((SAME, F, ATOM), bf16), own_messages, received)
    returned = exchanged(messages, same_axes)
    scalar, new_vectors = call(
        short_kernel,
        [SM] + [VM] * 9 + [ANY],
        (shape((F, ATOM), f32), shape((3, F, ATOM), bf16)),
        core, packed, vectors, neighbours, received, far,
        node_weight, node_bias.reshape(1, F), message_weight, radial_weight, messages,
        scratch=[
            VM((F, 3 * ATOM), bf16),
            VM((400, 3 * ATOM), bf16),
            VM((3 * ATOM, NBR * ATOM), bf16),
            VM((192, NBR * ATOM), f32),
            VM((8, NBR * ATOM), f32),
        ],
    )
    new_features = call(finish_kernel, [VM] * 2, shape((F, ATOM), bf16), returned, scalar)
    return new_features, new_vectors


def solution(mesh):
    fine = Mesh(mesh.devices.reshape(2, 16, 2, 4, 2), all_axes)
    atoms = P(None, all_axes)
    placed = (
        atoms, P(None, None, all_axes), atoms, atoms, atoms, P(), P(None, kb_axes),
        P(), P(), P(), P(), P(),
    )
    return jax.shard_map(
        shards,
        mesh=fine,
        in_specs=placed,
        out_specs=(atoms, P(None, None, all_axes)),
        check_vma=False,
    )
```

```python
import math

import jax
import jax.numpy as jnp
from jax import lax
from jax.experimental import pallas as pl
from jax.experimental.pallas import tpu as pltpu
from jax.sharding import Mesh
from jax.sharding import PartitionSpec as P

F = 64
NRBF = 20
NBR = 16
ATOM = 128
KDEV = 256
PLANE = 32
SAME = 16
KB = 16
DEPTH = 16
SLABS = 512
KVEC = 8192
ATOMS = 65536
PACK = 80
HALO_ROWS = 272

same_axes = ("yh", "yl", "x")
kb_axes = ("yl", "x", "c")
all_axes = ("yh", "z", "yl", "x", "c")

side_length = 6.0
slab_depth = 6.0
radial_reach = 6.0
distance_floor = 1.0
norm_scale = 1.0 / math.sqrt(KVEC * ATOMS)

sine_terms = (4.44287959, -7.30781805, 3.59778873, -0.79123821)
cosine_terms = (1.41420408, -6.97764206, 5.71523839, -1.72834865)
whole_turns = 1.5 * 2.0**23

VMEM_LIMIT = 16 * 2**20


def dot(a, b, dims):
    return lax.dot_general(a, b, (dims, ((), ())), preferred_element_type=jnp.float32)


def polynomial(terms, u):
    value = terms[-1] * u + terms[-2]
    for term in terms[-3::-1]:
        value = value * u + term
    return value


def cosine_and_sine(turns):
    r = turns - ((turns + whole_turns) - whole_turns)
    u = r * r
    s = r * polynomial(sine_terms, u)
    c = polynomial(cosine_terms, u)
    return 1.0 - s * s, s * c


VM, SM, ANY = pltpu.VMEM, pltpu.SMEM, pl.ANY


def call(kernel, places, outs, *operands, scratch=(), flops=0):
    return pl.pallas_call(
        kernel,
        out_shape=outs,
        in_specs=[pl.BlockSpec(memory_space=place) for place in places],
        out_specs=jax.tree.map(lambda _: pl.BlockSpec(memory_space=VM), outs),
        scratch_shapes=list(scratch),
        compiler_params=pltpu.CompilerParams(vmem_limit_bytes=VMEM_LIMIT),
        cost_estimate=pl.CostEstimate(flops=flops, bytes_accessed=0, transcendentals=0),
    )(*operands)


def packed_rows(feat, pos):
    placed = [jnp.pad(pos, ((at, PACK - at - 3), (0, 0))) for at in (F, F + 3, F + 6)]
    firsts = [lax.reduce_precision(value, 8, 7) for value in placed]
    seconds = [lax.reduce_precision(value - first, 8, 7) for value, first in zip(placed[1:], firsts[1:])]
    pieces = firsts[0] + seconds[0] + ((placed[2] - firsts[2]) - seconds[1])
    return jnp.pad(feat, ((0, PACK - F), (0, 0))) + pieces.astype(jnp.bfloat16)


def summed(pieces):
    return pieces[0:3] + pieces[3:6] + pieces[6:9]


def halo_kernel(core, packed, vec, halo, far, near):
    rows = jnp.concatenate([packed[...], vec[0], vec[1], vec[2]], axis=0)
    atom = lax.broadcasted_iota(jnp.int32, (ATOM, ATOM), 0)
    for row, out in ((1 - core[0], far), (core[0], near)):
        chosen = jnp.where(atom == halo[pl.ds(row, 1), :], 1.0, 0.0).astype(jnp.bfloat16)
        out[...] = dot(rows, chosen, ((1,), (0,))).astype(jnp.bfloat16)


def add_atoms(got, table, columns, total):
    for first in range(0, SAME, 2):
        both = jnp.concatenate([got[first], got[first + 1]], axis=1)
        pos = summed(both[F:].astype(jnp.float32))
        at = slice(first * ATOM, (first + 2) * ATOM)
        for k in range(0, KDEV, 64):
            rows = slice(k, k + 64)
            halves = []
            for lanes in (slice(0, ATOM), slice(ATOM, 2 * ATOM)):
                halves.append(
                    (columns[0, rows] * pos[0:1, lanes] + columns[1, rows] * pos[1:2, lanes])
                    + columns[2, rows] * pos[2:3, lanes]
                )
            cosines, sines = cosine_and_sine(jnp.concatenate(halves, axis=1))
            cosines, sines = cosines.astype(jnp.bfloat16), sines.astype(jnp.bfloat16)
            table[k : k + 64, at] = cosines
            table[KDEV + k : KDEV + k + 64, at] = sines
            sums = dot(jnp.concatenate([cosines, sines], axis=0), both[:F], ((1,), (1,)))
            total[k : k + 64] += sums[:64]
            total[KDEV + k : KDEV + k + 64] += sums[64:]


def own_table_kernel(got, lattice, constants, table, total, columns):
    turned = jnp.concatenate([lattice[...], jnp.zeros((5, KDEV), jnp.float32)], axis=0).T
    for i in range(3):
        columns[i] = jnp.broadcast_to(turned[:, i : i + 1], (KDEV, ATOM))
    total[...] = jnp.zeros_like(total)
    add_atoms(got, table, columns, total)


def other_table_kernel(got, columns, own_total, far, table, partial, total):
    total[...] = own_total[...]
    add_atoms(got, table, columns, total)
    partial[...] = jnp.concatenate([total[:KDEV], total[KDEV:]], axis=1).astype(jnp.bfloat16)


def sum_kernel(arrived, out):
    total = arrived[0].astype(jnp.float32)
    for i in range(1, DEPTH):
        total = total + arrived[i].astype(jnp.float32)
    total = total.astype(jnp.bfloat16)
    for i in range(DEPTH):
        out[i] = total


def filtered_sums(half, got, constants):
    own = constants[:, pl.ds(pl.multiple_of(half[0], KDEV), KDEV)] * norm_scale
    weight = constants[:, 2 * KDEV :].astype(jnp.bfloat16)
    total = [dot(weight, got[:, part * F : (part + 1) * F], ((0,), (1,))) for part in range(2)]
    return jnp.concatenate([own * total[0], own * total[1]], axis=1).astype(jnp.bfloat16)


def project_other_kernel(half, got, constants, table, near, out):
    filtered = filtered_sums(half, got, constants)
    for first in range(0, SAME, 8):
        message = dot(filtered, table[:, first * ATOM : (first + 8) * ATOM], ((1,), (0,))).astype(jnp.bfloat16)
        for p in range(8):
            out[(first + p) * F : (first + p + 1) * F] = message[:, p * ATOM : (p + 1) * ATOM]
    out[SAME * F :] = near[...]


def project_own_kernel(half, got, constants, table, out):
    filtered = filtered_sums(half, got, constants)
    for first in range(0, SAME, 8):
        message = dot(filtered, table[:, first * ATOM : (first + 8) * ATOM], ((1,), (0,)))
        for p in range(8):
            out[first + p] = message[:, p * ATOM : (p + 1) * ATOM]


def join_kernel(own, received, out):
    for p in range(SAME):
        out[p] = (own[p] + received[p * F : (p + 1) * F].astype(jnp.float32)).astype(jnp.bfloat16)


def finish_kernel(arrived, scalar, out):
    total = arrived[0].astype(jnp.float32)
    for i in range(1, SAME):
        total = total + arrived[i].astype(jnp.float32)
    out[...] = (scalar[...] + total).astype(jnp.bfloat16)


def short_kernel(
    core, packed, vec, ids, near, far_within, far_across, node_weight, bias, message_weight, radial_weight, messages,
    scalar_out, vector_out, feats, ext, chosen, filters, directions,
):
    pos = summed(packed[F:].astype(jnp.float32))
    feats[:, :ATOM] = packed[:F]
    ext[192:384, :ATOM] = jnp.concatenate([vec[0], vec[1], vec[2]], axis=0)
    ext[384:, :ATOM] = packed[F:]
    near_at = pl.ds(pl.multiple_of((2 - core[0]) * ATOM, ATOM), ATOM)
    far_at = pl.ds(pl.multiple_of((1 + core[0]) * ATOM, ATOM), ATOM)
    far = far_within[...] + far_across[...]
    for side, start, at in ((near, SAME * F, near_at), (far, 0, far_at)):
        feats[:, at] = side[start : start + F]
        ext[192:384, at] = side[start + PACK : start + HALO_ROWS]
        ext[384:, at] = side[start + F : start + PACK]
    bias_column = jnp.broadcast_to(bias[...], (8, F)).T[:, 0:1]
    hidden = dot(node_weight[...], feats[...], ((0,), (0,))) + bias_column
    hidden = (hidden / (1.0 + jnp.exp(-hidden))).astype(jnp.bfloat16)
    ext[:192] = dot(message_weight[...], hidden, ((0,), (0,))).astype(jnp.bfloat16)

    number = lax.broadcasted_iota(jnp.int32, (3 * ATOM, ATOM), 0)
    for j in range(NBR):
        chosen[:, j * ATOM : (j + 1) * ATOM] = jnp.where(number == ids[j : j + 1, :], 1.0, 0.0).astype(jnp.bfloat16)
    found = dot(ext[384:], chosen[...], ((1,), (0,)))
    offset = summed(found) - jnp.concatenate([pos] * NBR, axis=1)
    offset = offset - jnp.floor(offset + 0.5)
    side = lax.broadcasted_iota(jnp.int32, (3, 1), 0)
    box = jnp.where(side == 2, slab_depth * SLABS, side_length).astype(jnp.float32)
    cartesian = offset * box
    square = cartesian * cartesian
    distance = jnp.sqrt(square[0:1] + square[1:2] + square[2:3])
    directions[0:3] = cartesian / jnp.maximum(distance, distance_floor)
    center = lax.broadcasted_iota(jnp.int32, (NRBF, 1), 0).astype(jnp.float32) * (radial_reach / (NRBF - 1))
    away = (distance - center) / (1.5 * radial_reach / NRBF)
    radial = jnp.exp(-(away * away)).astype(jnp.bfloat16)
    filters[...] = dot(radial_weight[...], radial, ((0,), (0,)))

    def slots(step, sums):
        at = pl.ds(pl.multiple_of(step * 2 * ATOM, 2 * ATOM), 2 * ATOM)
        picked = dot(ext[:384], chosen[:, at], ((1,), (0,)))
        terms = picked[:192] * filters[:, at]
        toward = directions[:, at]
        parts = [terms[:F]]
        for x in range(3):
            parts.append(
                picked[192 + x * F : 192 + (x + 1) * F] * terms[F : 2 * F] + terms[2 * F :] * toward[x : x + 1]
            )
        return tuple(s + p[:, :ATOM] + p[:, ATOM:] for s, p in zip(sums, parts))

    zero = jnp.zeros((F, ATOM), jnp.float32)
    sums = lax.fori_loop(0, NBR // 2, slots, (zero,) * 4)
    scalar_out[...] = packed[:F].astype(jnp.float32) + sums[0]
    for x in range(3):
        vector_out[x] = (vec[x].astype(jnp.float32) + sums[1 + x]).astype(jnp.bfloat16)


def exchanged(x, axes):
    return lax.all_to_all(x, axes, split_axis=0, concat_axis=0, tiled=True)


def swapped(x, first, within=None):
    pairs = [((first + i) % SLABS, (first + (i ^ 1)) % SLABS) for i in range(SLABS)]
    if within is not None:
        pairs = [(a, b) for a, b in pairs if (a // KB == b // KB) == within]
    return lax.ppermute(x, all_axes, pairs)


def shards(
    features, vectors, positions, neighbours, halo_lists, lattice, kspace_filter,
    node_weight, node_bias, message_weight, radial_weight, ewald_weight,
):
    bf16, f32 = jnp.bfloat16, jnp.float32
    shape = jax.ShapeDtypeStruct
    half_at = lax.axis_index("yh") * KDEV
    k_at = lax.axis_index(kb_axes) * 2 * KDEV + half_at
    packed = packed_rows(features, positions)
    own = exchanged(jnp.broadcast_to(packed, (SAME, PACK, ATOM)), same_axes)
    other = swapped(own, 0)
    own_lattice = lax.dynamic_slice_in_dim(lattice, k_at, KDEV, 1).astype(f32)
    constants = jnp.pad(kspace_filter, ((0, 0), (0, F)))
    constants = constants + jnp.pad(ewald_weight.astype(f32), ((0, 0), (2 * KDEV, 0)))
    half = half_at.astype(jnp.int32).reshape(1)
    core = lax.axis_index("c").astype(jnp.int32).reshape(1)
    halo = shape((HALO_ROWS, ATOM), bf16)
    far, near = call(halo_kernel, [SM, VM, VM, VM], (halo, halo), core, packed, vectors, halo_lists)
    far_within, far_across = swapped(far, 1, True), swapped(far, 1, False)
    half_table = shape((2 * KDEV, SAME * ATOM), bf16)
    own_table, own_total, columns = call(
        own_table_kernel,
        [VM, VM, ANY],
        (half_table, shape((2 * KDEV, F), f32), shape((3, KDEV, ATOM), f32)),
        own, own_lattice, constants,
        flops=37 * 10**8,
    )
    other_table, partial = call(
        other_table_kernel,
        [VM, VM, VM, ANY],
        (half_table, shape((KDEV, 2 * F), bf16)),
        other, columns, own_total, far_within,
        scratch=[VM((2 * KDEV, F), f32)],
    )
    arrived = exchanged(partial.reshape(DEPTH, KDEV // DEPTH, 2 * F), "z")
    owned = call(sum_kernel, [VM], shape((DEPTH, KDEV // DEPTH, 2 * F), bf16), arrived)
    totals = exchanged(owned, "z").reshape(KDEV, 2 * F)
    for_other = call(
        project_other_kernel,
        [SM] + [VM] * 4,
        shape((SAME * F + HALO_ROWS, ATOM), bf16),
        half, totals, constants, other_table, near,
    )
    received = swapped(for_other, 0)
    own_messages = call(
        project_own_kernel, [SM] + [VM] * 3, shape((SAME, F, ATOM), f32), half, totals, constants, own_table,
        flops=10**9,
    )
    messages = call(join_kernel, [VM] * 2, shape((SAME, F, ATOM), bf16), own_messages, received)
    returned = exchanged(messages, same_axes)
    scalar, new_vectors = call(
        short_kernel,
        [SM] + [VM] * 10 + [ANY],
        (shape((F, ATOM), f32), shape((3, F, ATOM), bf16)),
        core, packed, vectors, neighbours, received, far_within, far_across,
        node_weight, node_bias.reshape(1, F), message_weight, radial_weight, messages,
        scratch=[
            VM((F, 3 * ATOM), bf16),
            VM((400, 3 * ATOM), bf16),
            VM((3 * ATOM, NBR * ATOM), bf16),
            VM((192, NBR * ATOM), f32),
            VM((8, NBR * ATOM), f32),
        ],
    )
    new_features = call(finish_kernel, [VM] * 2, shape((F, ATOM), bf16), returned, scalar)
    return new_features, new_vectors


def solution(mesh):
    fine = Mesh(mesh.devices.reshape(2, 16, 2, 4, 2), all_axes)
    atoms = P(None, all_axes)
    placed = (
        atoms, P(None, None, all_axes), atoms, atoms, atoms, P(), P(None, kb_axes),
        P(), P(), P(), P(), P(),
    )
    return jax.shard_map(
        shards,
        mesh=fine,
        in_specs=placed,
        out_specs=(atoms, P(None, None, all_axes)),
        check_vma=False,
    )
```

```python
import math

import jax
import jax.numpy as jnp
from jax import lax
from jax.experimental import pallas as pl
from jax.experimental.pallas import tpu as pltpu
from jax.sharding import Mesh
from jax.sharding import PartitionSpec as P

F = 64
NRBF = 20
NBR = 16
ATOM = 128
KDEV = 256
PLANE = 32
SAME = 16
DEPTH = 16
SLABS = 512
KVEC = 8192
ATOMS = 65536
PACK = 80
HALO_ROWS = 272

same_axes = ("x", "yh", "yl")
kb_axes = ("yl", "x", "c")
all_axes = ("yh", "z", "yl", "x", "c")

side_length = 6.0
slab_depth = 6.0
radial_reach = 6.0
distance_floor = 1.0
norm_scale = 1.0 / math.sqrt(KVEC * ATOMS)

sine_terms = (4.44287959, -7.30781805, 3.59778873, -0.79123821)
cosine_terms = (1.41420408, -6.97764206, 5.71523839, -1.72834865)
whole_turns = 1.5 * 2.0**23

VMEM_LIMIT = 16 * 2**20


def dot(a, b, dims):
    return lax.dot_general(a, b, (dims, ((), ())), preferred_element_type=jnp.float32)


def polynomial(terms, u):
    value = terms[-1] * u + terms[-2]
    for term in terms[-3::-1]:
        value = value * u + term
    return value


def cosine_and_sine(turns):
    r = turns - ((turns + whole_turns) - whole_turns)
    u = r * r
    s = r * polynomial(sine_terms, u)
    c = polynomial(cosine_terms, u)
    return 1.0 - s * s, s * c


VM, SM, ANY = pltpu.VMEM, pltpu.SMEM, pl.ANY


def call(kernel, places, outs, *operands, scratch=(), flops=0):
    return pl.pallas_call(
        kernel,
        out_shape=outs,
        in_specs=[pl.BlockSpec(memory_space=place) for place in places],
        out_specs=jax.tree.map(lambda _: pl.BlockSpec(memory_space=VM), outs),
        scratch_shapes=list(scratch),
        compiler_params=pltpu.CompilerParams(vmem_limit_bytes=VMEM_LIMIT),
        cost_estimate=pl.CostEstimate(flops=flops, bytes_accessed=0, transcendentals=0),
    )(*operands)


def packed_rows(feat, pos):
    placed = [jnp.pad(pos, ((at, PACK - at - 3), (0, 0))) for at in (F, F + 3, F + 6)]
    firsts = [lax.reduce_precision(value, 8, 7) for value in placed]
    seconds = [lax.reduce_precision(value - first, 8, 7) for value, first in zip(placed[1:], firsts[1:])]
    pieces = firsts[0] + seconds[0] + ((placed[2] - firsts[2]) - seconds[1])
    return jnp.pad(feat, ((0, PACK - F), (0, 0))) + pieces.astype(jnp.bfloat16)


def summed(pieces):
    return pieces[0:3] + pieces[3:6] + pieces[6:9]


def halo_kernel(core, packed, vec, halo, far, near):
    rows = jnp.concatenate([packed[...], vec[0], vec[1], vec[2]], axis=0)
    atom = lax.broadcasted_iota(jnp.int32, (ATOM, ATOM), 0)
    for row, out in ((1 - core[0], far), (core[0], near)):
        chosen = jnp.where(atom == halo[pl.ds(row, 1), :], 1.0, 0.0).astype(jnp.bfloat16)
        out[...] = dot(rows, chosen, ((1,), (0,))).astype(jnp.bfloat16)


def add_atoms(got, table, columns, total):
    for first in range(0, SAME, 2):
        both = jnp.concatenate([got[first], got[first + 1]], axis=1)
        pos = summed(both[F:].astype(jnp.float32))
        at = slice(first * ATOM, (first + 2) * ATOM)
        for k in range(0, KDEV, 64):
            rows = slice(k, k + 64)
            halves = []
            for lanes in (slice(0, ATOM), slice(ATOM, 2 * ATOM)):
                halves.append(
                    (columns[0, rows] * pos[0:1, lanes] + columns[1, rows] * pos[1:2, lanes])
                    + columns[2, rows] * pos[2:3, lanes]
                )
            cosines, sines = cosine_and_sine(jnp.concatenate(halves, axis=1))
            cosines, sines = cosines.astype(jnp.bfloat16), sines.astype(jnp.bfloat16)
            table[k : k + 64, at] = cosines
            table[KDEV + k : KDEV + k + 64, at] = sines
            sums = dot(jnp.concatenate([cosines, sines], axis=0), both[:F], ((1,), (1,)))
            total[k : k + 64] += sums[:64]
            total[KDEV + k : KDEV + k + 64] += sums[64:]


def own_table_kernel(got, lattice, constants, table, total, columns):
    turned = jnp.concatenate([lattice[...], jnp.zeros((5, KDEV), jnp.float32)], axis=0).T
    for i in range(3):
        columns[i] = jnp.broadcast_to(turned[:, i : i + 1], (KDEV, ATOM))
    total[...] = jnp.zeros_like(total)
    add_atoms(got, table, columns, total)


def other_table_kernel(got, columns, own_total, far, table, partial, total):
    total[...] = own_total[...]
    add_atoms(got, table, columns, total)
    partial[...] = jnp.concatenate([total[:KDEV], total[KDEV:]], axis=1).astype(jnp.bfloat16)


def sum_kernel(arrived, out):
    total = arrived[0].astype(jnp.float32)
    for i in range(1, DEPTH):
        total = total + arrived[i].astype(jnp.float32)
    total = total.astype(jnp.bfloat16)
    for i in range(DEPTH):
        out[i] = total


def filtered_sums(half, got, constants):
    own = constants[:, pl.ds(pl.multiple_of(half[0], KDEV), KDEV)] * norm_scale
    weight = constants[:, 2 * KDEV :].astype(jnp.bfloat16)
    total = [dot(weight, got[:, part * F : (part + 1) * F], ((0,), (1,))) for part in range(2)]
    return jnp.concatenate([own * total[0], own * total[1]], axis=1).astype(jnp.bfloat16)


def project_other_kernel(half, got, constants, table, near, out):
    filtered = filtered_sums(half, got, constants)
    for first in range(0, SAME, 8):
        message = dot(filtered, table[:, first * ATOM : (first + 8) * ATOM], ((1,), (0,))).astype(jnp.bfloat16)
        for p in range(8):
            out[(first + p) * F : (first + p + 1) * F] = message[:, p * ATOM : (p + 1) * ATOM]
    out[SAME * F :] = near[...]


def project_own_kernel(half, got, constants, table, out):
    filtered = filtered_sums(half, got, constants)
    for first in range(0, SAME, 8):
        message = dot(filtered, table[:, first * ATOM : (first + 8) * ATOM], ((1,), (0,)))
        for p in range(8):
            out[first + p] = message[:, p * ATOM : (p + 1) * ATOM]


def join_kernel(own, received, out):
    for p in range(SAME):
        out[p] = (own[p] + received[p * F : (p + 1) * F].astype(jnp.float32)).astype(jnp.bfloat16)


def finish_kernel(arrived, scalar, out):
    total = arrived[0].astype(jnp.float32)
    for i in range(1, SAME):
        total = total + arrived[i].astype(jnp.float32)
    out[...] = (scalar[...] + total).astype(jnp.bfloat16)


def short_kernel(
    core, packed, vec, ids, near, far, node_weight, bias, message_weight, radial_weight, messages,
    scalar_out, vector_out, feats, ext, chosen, filters, directions,
):
    pos = summed(packed[F:].astype(jnp.float32))
    feats[:, :ATOM] = packed[:F]
    ext[192:384, :ATOM] = jnp.concatenate([vec[0], vec[1], vec[2]], axis=0)
    ext[384:, :ATOM] = packed[F:]
    near_at = pl.ds(pl.multiple_of((2 - core[0]) * ATOM, ATOM), ATOM)
    far_at = pl.ds(pl.multiple_of((1 + core[0]) * ATOM, ATOM), ATOM)
    for side, start, at in ((near, SAME * F, near_at), (far, 0, far_at)):
        feats[:, at] = side[start : start + F]
        ext[192:384, at] = side[start + PACK : start + HALO_ROWS]
        ext[384:, at] = side[start + F : start + PACK]
    bias_column = jnp.broadcast_to(bias[...], (8, F)).T[:, 0:1]
    hidden = dot(node_weight[...], feats[...], ((0,), (0,))) + bias_column
    hidden = (hidden / (1.0 + jnp.exp(-hidden))).astype(jnp.bfloat16)
    ext[:192] = dot(message_weight[...], hidden, ((0,), (0,))).astype(jnp.bfloat16)

    number = lax.broadcasted_iota(jnp.int32, (3 * ATOM, ATOM), 0)
    for j in range(NBR):
        chosen[:, j * ATOM : (j + 1) * ATOM] = jnp.where(number == ids[j : j + 1, :], 1.0, 0.0).astype(jnp.bfloat16)
    found = dot(ext[384:], chosen[...], ((1,), (0,)))
    offset = summed(found) - jnp.concatenate([pos] * NBR, axis=1)
    offset = offset - jnp.floor(offset + 0.5)
    side = lax.broadcasted_iota(jnp.int32, (3, 1), 0)
    box = jnp.where(side == 2, slab_depth * SLABS, side_length).astype(jnp.float32)
    cartesian = offset * box
    square = cartesian * cartesian
    distance = jnp.sqrt(square[0:1] + square[1:2] + square[2:3])
    directions[0:3] = cartesian / jnp.maximum(distance, distance_floor)
    center = lax.broadcasted_iota(jnp.int32, (NRBF, 1), 0).astype(jnp.float32) * (radial_reach / (NRBF - 1))
    away = (distance - center) / (1.5 * radial_reach / NRBF)
    radial = jnp.exp(-(away * away)).astype(jnp.bfloat16)
    filters[...] = dot(radial_weight[...], radial, ((0,), (0,)))

    def slots(step, sums):
        at = pl.ds(pl.multiple_of(step * 2 * ATOM, 2 * ATOM), 2 * ATOM)
        picked = dot(ext[:384], chosen[:, at], ((1,), (0,)))
        terms = picked[:192] * filters[:, at]
        toward = directions[:, at]
        parts = [terms[:F]]
        for x in range(3):
            parts.append(
                picked[192 + x * F : 192 + (x + 1) * F] * terms[F : 2 * F] + terms[2 * F :] * toward[x : x + 1]
            )
        return tuple(s + p[:, :ATOM] + p[:, ATOM:] for s, p in zip(sums, parts))

    zero = jnp.zeros((F, ATOM), jnp.float32)
    sums = lax.fori_loop(0, NBR // 2, slots, (zero,) * 4)
    scalar_out[...] = packed[:F].astype(jnp.float32) + sums[0]
    for x in range(3):
        vector_out[x] = (vec[x].astype(jnp.float32) + sums[1 + x]).astype(jnp.bfloat16)


def exchanged(x, axes):
    return lax.all_to_all(x, axes, split_axis=0, concat_axis=0, tiled=True)


def swapped(x, first):
    pairs = [((first + i) % SLABS, (first + (i ^ 1)) % SLABS) for i in range(SLABS)]
    return lax.ppermute(x, all_axes, pairs)


def shards(
    features, vectors, positions, neighbours, halo_lists, lattice, kspace_filter,
    node_weight, node_bias, message_weight, radial_weight, ewald_weight,
):
    bf16, f32 = jnp.bfloat16, jnp.float32
    shape = jax.ShapeDtypeStruct
    half_at = lax.axis_index("yh") * KDEV
    k_at = lax.axis_index(kb_axes) * 2 * KDEV + half_at
    packed = packed_rows(features, positions)
    own = exchanged(jnp.broadcast_to(packed, (SAME, PACK, ATOM)), same_axes)
    other = swapped(own, 0)
    own_lattice = lax.dynamic_slice_in_dim(lattice, k_at, KDEV, 1).astype(f32)
    constants = jnp.pad(kspace_filter, ((0, 0), (0, F)))
    constants = constants + jnp.pad(ewald_weight.astype(f32), ((0, 0), (2 * KDEV, 0)))
    half = half_at.astype(jnp.int32).reshape(1)
    core = lax.axis_index("c").astype(jnp.int32).reshape(1)
    halo = shape((HALO_ROWS, ATOM), bf16)
    far, near = call(halo_kernel, [SM, VM, VM, VM], (halo, halo), core, packed, vectors, halo_lists)
    far = swapped(far, 1)
    half_table = shape((2 * KDEV, SAME * ATOM), bf16)
    own_table, own_total, columns = call(
        own_table_kernel,
        [VM, VM, ANY],
        (half_table, shape((2 * KDEV, F), f32), shape((3, KDEV, ATOM), f32)),
        own, own_lattice, constants,
        flops=37 * 10**8,
    )
    other_table, partial = call(
        other_table_kernel,
        [VM, VM, VM, ANY],
        (half_table, shape((KDEV, 2 * F), bf16)),
        other, columns, own_total, far,
        scratch=[VM((2 * KDEV, F), f32)],
    )
    arrived = exchanged(partial.reshape(DEPTH, KDEV // DEPTH, 2 * F), "z")
    owned = call(sum_kernel, [VM], shape((DEPTH, KDEV // DEPTH, 2 * F), bf16), arrived)
    totals = exchanged(owned, "z").reshape(KDEV, 2 * F)
    for_other = call(
        project_other_kernel,
        [SM] + [VM] * 4,
        shape((SAME * F + HALO_ROWS, ATOM), bf16),
        half, totals, constants, other_table, near,
    )
    received = swapped(for_other, 0)
    own_messages = call(
        project_own_kernel, [SM] + [VM] * 3, shape((SAME, F, ATOM), f32), half, totals, constants, own_table,
        flops=10**9,
    )
    messages = call(join_kernel, [VM] * 2, shape((SAME, F, ATOM), bf16), own_messages, received)
    returned = exchanged(messages, same_axes)
    scalar, new_vectors = call(
        short_kernel,
        [SM] + [VM] * 9 + [ANY],
        (shape((F, ATOM), f32), shape((3, F, ATOM), bf16)),
        core, packed, vectors, neighbours, received, far,
        node_weight, node_bias.reshape(1, F), message_weight, radial_weight, messages,
        scratch=[
            VM((F, 3 * ATOM), bf16),
            VM((400, 3 * ATOM), bf16),
            VM((3 * ATOM, NBR * ATOM), bf16),
            VM((192, NBR * ATOM), f32),
            VM((8, NBR * ATOM), f32),
        ],
    )
    new_features = call(finish_kernel, [VM] * 2, shape((F, ATOM), bf16), returned, scalar)
    return new_features, new_vectors


def solution(mesh):
    fine = Mesh(mesh.devices.reshape(2, 16, 2, 4, 2), all_axes)
    atoms = P(None, all_axes)
    placed = (
        atoms, P(None, None, all_axes), atoms, atoms, atoms, P(), P(None, kb_axes),
        P(), P(), P(), P(), P(),
    )
    return jax.shard_map(
        shards,
        mesh=fine,
        in_specs=placed,
        out_specs=(atoms, P(None, None, all_axes)),
        check_vma=False,
    )
```

```python
import math

import jax
import jax.numpy as jnp
from jax import lax
from jax.experimental import pallas as pl
from jax.experimental.pallas import tpu as pltpu
from jax.sharding import Mesh
from jax.sharding import PartitionSpec as P

F = 64
NRBF = 20
NBR = 16
ATOM = 128
KDEV = 256
PLANE = 32
SAME = 16
DEPTH = 16
SLABS = 512
KVEC = 8192
ATOMS = 65536
PACK = 80
HALO_ROWS = 272

same_axes = ("x", "yh", "yl")
kb_axes = ("yl", "x", "c")
all_axes = ("yh", "z", "yl", "x", "c")

side_length = 6.0
slab_depth = 6.0
radial_reach = 6.0
distance_floor = 1.0
norm_scale = 1.0 / math.sqrt(KVEC * ATOMS)

sine_terms = (4.44287959, -7.30781805, 3.59778873, -0.79123821)
cosine_terms = (1.41420408, -6.97764206, 5.71523839, -1.72834865)
whole_turns = 1.5 * 2.0**23

VMEM_LIMIT = 16 * 2**20


def dot(a, b, dims):
    return lax.dot_general(a, b, (dims, ((), ())), preferred_element_type=jnp.float32)


def polynomial(terms, u):
    value = terms[-1] * u + terms[-2]
    for term in terms[-3::-1]:
        value = value * u + term
    return value


def cosine_and_sine(turns):
    r = turns - ((turns + whole_turns) - whole_turns)
    u = r * r
    s = r * polynomial(sine_terms, u)
    c = polynomial(cosine_terms, u)
    return 1.0 - s * s, s * c


VM, SM, ANY = pltpu.VMEM, pltpu.SMEM, pl.ANY


def call(kernel, places, outs, *operands, scratch=(), flops=0, far_outs=()):
    return pl.pallas_call(
        kernel,
        out_shape=outs,
        in_specs=[pl.BlockSpec(memory_space=place) for place in places],
        out_specs=jax.tree.map(lambda _: pl.BlockSpec(memory_space=VM), outs)
        if not far_outs
        else tuple(pl.BlockSpec(memory_space=ANY if i in far_outs else VM) for i in range(len(outs))),
        scratch_shapes=list(scratch),
        compiler_params=pltpu.CompilerParams(vmem_limit_bytes=VMEM_LIMIT),
        cost_estimate=pl.CostEstimate(flops=flops, bytes_accessed=0, transcendentals=0),
    )(*operands)


def packed_rows(feat, pos):
    placed = [jnp.pad(pos, ((at, PACK - at - 3), (0, 0))) for at in (F, F + 3, F + 6)]
    firsts = [lax.reduce_precision(value, 8, 7) for value in placed]
    seconds = [lax.reduce_precision(value - first, 8, 7) for value, first in zip(placed[1:], firsts[1:])]
    pieces = firsts[0] + seconds[0] + ((placed[2] - firsts[2]) - seconds[1])
    return jnp.pad(feat, ((0, PACK - F), (0, 0))) + pieces.astype(jnp.bfloat16)


def copies_kernel(packed, out, done):
    copies = [pltpu.make_async_copy(packed, out.at[p], done.at[p]) for p in range(SAME)]
    for copy in copies:
        copy.start()
    for copy in copies:
        copy.wait()


def summed(pieces):
    return pieces[0:3] + pieces[3:6] + pieces[6:9]


def halo_kernel(core, packed, vec, halo, far, near):
    rows = jnp.concatenate([packed[...], vec[0], vec[1], vec[2]], axis=0)
    atom = lax.broadcasted_iota(jnp.int32, (ATOM, ATOM), 0)
    for row, out in ((1 - core[0], far), (core[0], near)):
        chosen = jnp.where(atom == halo[pl.ds(row, 1), :], 1.0, 0.0).astype(jnp.bfloat16)
        out[...] = dot(rows, chosen, ((1,), (0,))).astype(jnp.bfloat16)


def add_atoms(got, table, columns, total):
    for first in range(0, SAME, 2):
        both = jnp.concatenate([got[first], got[first + 1]], axis=1)
        pos = summed(both[F:].astype(jnp.float32))
        at = slice(first * ATOM, (first + 2) * ATOM)
        for k in range(0, KDEV, 64):
            rows = slice(k, k + 64)
            halves = []
            for lanes in (slice(0, ATOM), slice(ATOM, 2 * ATOM)):
                halves.append(
                    (columns[0, rows] * pos[0:1, lanes] + columns[1, rows] * pos[1:2, lanes])
                    + columns[2, rows] * pos[2:3, lanes]
                )
            cosines, sines = cosine_and_sine(jnp.concatenate(halves, axis=1))
            cosines, sines = cosines.astype(jnp.bfloat16), sines.astype(jnp.bfloat16)
            table[k : k + 64, at] = cosines
            table[KDEV + k : KDEV + k + 64, at] = sines
            sums = dot(jnp.concatenate([cosines, sines], axis=0), both[:F], ((1,), (1,)))
            total[k : k + 64] += sums[:64]
            total[KDEV + k : KDEV + k + 64] += sums[64:]


def own_table_kernel(got, lattice, constants, table, total, columns):
    turned = jnp.concatenate([lattice[...], jnp.zeros((5, KDEV), jnp.float32)], axis=0).T
    for i in range(3):
        columns[i] = jnp.broadcast_to(turned[:, i : i + 1], (KDEV, ATOM))
    total[...] = jnp.zeros_like(total)
    add_atoms(got, table, columns, total)


def other_table_kernel(got, columns, own_total, far, table, partial, total):
    total[...] = own_total[...]
    add_atoms(got, table, columns, total)
    partial[...] = jnp.concatenate([total[:KDEV], total[KDEV:]], axis=1).astype(jnp.bfloat16)


def sum_kernel(arrived, out):
    total = arrived[0].astype(jnp.float32)
    for i in range(1, DEPTH):
        total = total + arrived[i].astype(jnp.float32)
    total = total.astype(jnp.bfloat16)
    for i in range(DEPTH):
        out[i] = total


def filtered_sums(half, got, constants):
    own = constants[:, pl.ds(pl.multiple_of(half[0], KDEV), KDEV)] * norm_scale
    weight = constants[:, 2 * KDEV :].astype(jnp.bfloat16)
    total = [dot(weight, got[:, part * F : (part + 1) * F], ((0,), (1,))) for part in range(2)]
    return jnp.concatenate([own * total[0], own * total[1]], axis=1).astype(jnp.bfloat16)


def project_other_kernel(half, got, constants, table, near, out):
    filtered = filtered_sums(half, got, constants)
    for first in range(0, SAME, 8):
        message = dot(filtered, table[:, first * ATOM : (first + 8) * ATOM], ((1,), (0,))).astype(jnp.bfloat16)
        for p in range(8):
            out[(first + p) * F : (first + p + 1) * F] = message[:, p * ATOM : (p + 1) * ATOM]
    out[SAME * F :] = near[...]


def project_own_kernel(half, got, constants, table, out):
    filtered = filtered_sums(half, got, constants)
    for first in range(0, SAME, 8):
        message = dot(filtered, table[:, first * ATOM : (first + 8) * ATOM], ((1,), (0,)))
        for p in range(8):
            out[first + p] = message[:, p * ATOM : (p + 1) * ATOM]


def join_kernel(own, received, out):
    for p in range(SAME):
        out[p] = (own[p] + received[p * F : (p + 1) * F].astype(jnp.float32)).astype(jnp.bfloat16)


def finish_kernel(arrived, scalar, out):
    total = arrived[0].astype(jnp.float32)
    for i in range(1, SAME):
        total = total + arrived[i].astype(jnp.float32)
    out[...] = (scalar[...] + total).astype(jnp.bfloat16)


def short_kernel(
    core, packed, vec, ids, near, far, node_weight, bias, message_weight, radial_weight, messages,
    scalar_out, vector_out, feats, ext, chosen, filters, directions,
):
    pos = summed(packed[F:].astype(jnp.float32))
    feats[:, :ATOM] = packed[:F]
    ext[192:384, :ATOM] = jnp.concatenate([vec[0], vec[1], vec[2]], axis=0)
    ext[384:, :ATOM] = packed[F:]
    near_at = pl.ds(pl.multiple_of((2 - core[0]) * ATOM, ATOM), ATOM)
    far_at = pl.ds(pl.multiple_of((1 + core[0]) * ATOM, ATOM), ATOM)
    for side, start, at in ((near, SAME * F, near_at), (far, 0, far_at)):
        feats[:, at] = side[start : start + F]
        ext[192:384, at] = side[start + PACK : start + HALO_ROWS]
        ext[384:, at] = side[start + F : start + PACK]
    bias_column = jnp.broadcast_to(bias[...], (8, F)).T[:, 0:1]
    hidden = dot(node_weight[...], feats[...], ((0,), (0,))) + bias_column
    hidden = (hidden / (1.0 + jnp.exp(-hidden))).astype(jnp.bfloat16)
    ext[:192] = dot(message_weight[...], hidden, ((0,), (0,))).astype(jnp.bfloat16)

    number = lax.broadcasted_iota(jnp.int32, (3 * ATOM, ATOM), 0)
    for j in range(NBR):
        chosen[:, j * ATOM : (j + 1) * ATOM] = jnp.where(number == ids[j : j + 1, :], 1.0, 0.0).astype(jnp.bfloat16)
    found = dot(ext[384:], chosen[...], ((1,), (0,)))
    offset = summed(found) - jnp.concatenate([pos] * NBR, axis=1)
    offset = offset - jnp.floor(offset + 0.5)
    side = lax.broadcasted_iota(jnp.int32, (3, 1), 0)
    box = jnp.where(side == 2, slab_depth * SLABS, side_length).astype(jnp.float32)
    cartesian = offset * box
    square = cartesian * cartesian
    distance = jnp.sqrt(square[0:1] + square[1:2] + square[2:3])
    directions[0:3] = cartesian / jnp.maximum(distance, distance_floor)
    center = lax.broadcasted_iota(jnp.int32, (NRBF, 1), 0).astype(jnp.float32) * (radial_reach / (NRBF - 1))
    away = (distance - center) / (1.5 * radial_reach / NRBF)
    radial = jnp.exp(-(away * away)).astype(jnp.bfloat16)
    filters[...] = dot(radial_weight[...], radial, ((0,), (0,)))

    def slots(step, sums):
        at = pl.ds(pl.multiple_of(step * 2 * ATOM, 2 * ATOM), 2 * ATOM)
        picked = dot(ext[:384], chosen[:, at], ((1,), (0,)))
        terms = picked[:192] * filters[:, at]
        toward = directions[:, at]
        parts = [terms[:F]]
        for x in range(3):
            parts.append(
                picked[192 + x * F : 192 + (x + 1) * F] * terms[F : 2 * F] + terms[2 * F :] * toward[x : x + 1]
            )
        return tuple(s + p[:, :ATOM] + p[:, ATOM:] for s, p in zip(sums, parts))

    zero = jnp.zeros((F, ATOM), jnp.float32)
    sums = lax.fori_loop(0, NBR // 2, slots, (zero,) * 4)
    scalar_out[...] = packed[:F].astype(jnp.float32) + sums[0]
    for x in range(3):
        vector_out[x] = (vec[x].astype(jnp.float32) + sums[1 + x]).astype(jnp.bfloat16)


def exchanged(x, axes):
    return lax.all_to_all(x, axes, split_axis=0, concat_axis=0, tiled=True)


def swapped(x, first):
    pairs = [((first + i) % SLABS, (first + (i ^ 1)) % SLABS) for i in range(SLABS)]
    return lax.ppermute(x, all_axes, pairs)


def shards(
    features, vectors, positions, neighbours, halo_lists, lattice, kspace_filter,
    node_weight, node_bias, message_weight, radial_weight, ewald_weight,
):
    bf16, f32 = jnp.bfloat16, jnp.float32
    shape = jax.ShapeDtypeStruct
    half_at = lax.axis_index("yh") * KDEV
    k_at = lax.axis_index(kb_axes) * 2 * KDEV + half_at
    packed = packed_rows(features, positions)
    (copies,) = call(
        copies_kernel, [VM], (shape((SAME, PACK, ATOM), bf16),), packed,
        scratch=[pltpu.SemaphoreType.DMA((SAME,))],
        far_outs=(0,),
    )
    own = exchanged(copies, same_axes)
    other = swapped(own, 0)
    own_lattice = lax.dynamic_slice_in_dim(lattice, k_at, KDEV, 1).astype(f32)
    constants = jnp.pad(kspace_filter, ((0, 0), (0, F)))
    constants = constants + jnp.pad(ewald_weight.astype(f32), ((0, 0), (2 * KDEV, 0)))
    half = half_at.astype(jnp.int32).reshape(1)
    core = lax.axis_index("c").astype(jnp.int32).reshape(1)
    halo = shape((HALO_ROWS, ATOM), bf16)
    far, near = call(halo_kernel, [SM, VM, VM, VM], (halo, halo), core, packed, vectors, halo_lists)
    far = swapped(far, 1)
    half_table = shape((2 * KDEV, SAME * ATOM), bf16)
    own_table, own_total, columns = call(
        own_table_kernel,
        [VM, VM, ANY],
        (half_table, shape((2 * KDEV, F), f32), shape((3, KDEV, ATOM), f32)),
        own, own_lattice, constants,
        flops=37 * 10**8,
    )
    other_table, partial = call(
        other_table_kernel,
        [VM, VM, VM, ANY],
        (half_table, shape((KDEV, 2 * F), bf16)),
        other, columns, own_total, far,
        scratch=[VM((2 * KDEV, F), f32)],
    )
    arrived = exchanged(partial.reshape(DEPTH, KDEV // DEPTH, 2 * F), "z")
    owned = call(sum_kernel, [VM], shape((DEPTH, KDEV // DEPTH, 2 * F), bf16), arrived)
    totals = exchanged(owned, "z").reshape(KDEV, 2 * F)
    for_other = call(
        project_other_kernel,
        [SM] + [VM] * 4,
        shape((SAME * F + HALO_ROWS, ATOM), bf16),
        half, totals, constants, other_table, near,
    )
    received = swapped(for_other, 0)
    own_messages = call(
        project_own_kernel, [SM] + [VM] * 3, shape((SAME, F, ATOM), f32), half, totals, constants, own_table,
        flops=10**9,
    )
    messages = call(join_kernel, [VM] * 2, shape((SAME, F, ATOM), bf16), own_messages, received)
    returned = exchanged(messages, same_axes)
    scalar, new_vectors = call(
        short_kernel,
        [SM] + [VM] * 9 + [ANY],
        (shape((F, ATOM), f32), shape((3, F, ATOM), bf16)),
        core, packed, vectors, neighbours, received, far,
        node_weight, node_bias.reshape(1, F), message_weight, radial_weight, messages,
        scratch=[
            VM((F, 3 * ATOM), bf16),
            VM((400, 3 * ATOM), bf16),
            VM((3 * ATOM, NBR * ATOM), bf16),
            VM((192, NBR * ATOM), f32),
            VM((8, NBR * ATOM), f32),
        ],
    )
    new_features = call(finish_kernel, [VM] * 2, shape((F, ATOM), bf16), returned, scalar)
    return new_features, new_vectors


def solution(mesh):
    fine = Mesh(mesh.devices.reshape(2, 16, 2, 4, 2), all_axes)
    atoms = P(None, all_axes)
    placed = (
        atoms, P(None, None, all_axes), atoms, atoms, atoms, P(), P(None, kb_axes),
        P(), P(), P(), P(), P(),
    )
    return jax.shard_map(
        shards,
        mesh=fine,
        in_specs=placed,
        out_specs=(atoms, P(None, None, all_axes)),
        check_vma=False,
    )
```
